32 devices in a mesh: grp: 4 (over y, x), fsdp: 8 (over z, core).
Axes of the slice: x: 2, y: 2, z: 4, core: 2. Of those that a mesh axis runs over, the one named last changes fastest.
Arguments:
- tokens: int32 [2, 4, 2048], P(None, 'grp', 'fsdp'), may hold values from 0 to 32127
- routes: int32 [2, 4, 2048, 1], P(None, 'grp', 'fsdp'), may hold values from 0 to 1; in each aligned block of 256 rows (0 to 255, 256 to 511, ..., all dimensions but the last counted through in order) at most 192 rows name the same one
- segments: int32 [2, 4, 2048], P(None, 'grp', 'fsdp'), may hold values from 0 to 2, as said below
- loss_pos: int32 [2, 4, 128], P(None, 'grp', 'fsdp'), may hold values from 0 to 253, as said below
- embedding: float32 [32128, 768], P('fsdp'), may hold values from -6 to 6
- embedding_first: float32 [4, 32128, 768], P('grp', 'fsdp'), may hold values from -1.1920929e-07 to 1.1920929e-07
- embedding_second: float32 [4, 32128, 768], P('grp', 'fsdp'), may hold values from 1.5808284e-14 to 2.1077713e-13
- embedding_outer: float32 [32128, 768], P('fsdp'), may hold values from -3 to 3
- attention: float32 [5, 768, 768], P(None, 'fsdp'), may hold values from -0.21875 to 0.21875
- attention_first: float32 [4, 5, 768, 768], P('grp', None, 'fsdp'), may hold values from -4.7683716e-07 to 4.7683716e-07
- attention_second: float32 [4, 5, 768, 768], P('grp', None, 'fsdp'), may hold values from 1.5808284e-14 to 2.1077713e-13
- attention_outer: float32 [5, 768, 768], P(None, 'fsdp'), may hold values from -0.0625 to 0.0625
- experts: float32 [2, 2, 768, 3072], P(None, None, None, 'fsdp'), may hold values from -0.21875 to 0.21875
- experts_first: float32 [4, 2, 2, 768, 3072], P('grp', None, None, None, 'fsdp'), may hold values from -4.7683716e-07 to 4.7683716e-07
- experts_second: float32 [4, 2, 2, 768, 3072], P('grp', None, None, None, 'fsdp'), may hold values from 3.952071e-15 to 5.2694282e-14
- experts_outer: float32 [2, 2, 768, 3072], P(None, None, None, 'fsdp'), may hold values from -0.0625 to 0.0625
- vectors: float32 [6, 768], replicated, may hold values from -0.35 to 1.6, as said below
- vectors_first: float32 [4, 6, 768], P('grp'), may hold values from -1.9073486e-06 to 1.9073486e-06
- vectors_second: float32 [4, 6, 768], P('grp'), may hold values from 2.5293255e-13 to 3.372434e-12
- vectors_outer: float32 [6, 768], replicated, may hold values from -0.625 to 0.625
Outputs:
- losses: float32 [4, 2], P('grp')
- gradient_norms: float32 [4, 2], P('grp')
- embedding_moment: float32 [4, 32128, 768], P('grp', 'fsdp')
- embedding_square: float32 [4, 32128, 768], P('grp', 'fsdp')
- embedding_master: float32 [32128, 768], P('fsdp')
- embedding_momentum: float32 [32128, 768], P('fsdp')
- embedding_copy: bfloat16 [32128, 768], P('fsdp')
- attention_moment: float32 [4, 5, 768, 768], P('grp', None, 'fsdp')
- attention_square: float32 [4, 5, 768, 768], P('grp', None, 'fsdp')
- attention_master: float32 [5, 768, 768], P(None, 'fsdp')
- attention_momentum: float32 [5, 768, 768], P(None, 'fsdp')
- attention_copy: bfloat16 [5, 768, 768], P(None, 'fsdp')
- experts_moment: float32 [4, 2, 2, 768, 3072], P('grp', None, None, None, 'fsdp')
- experts_square: float32 [4, 2, 2, 768, 3072], P('grp', None, None, None, 'fsdp')
- experts_master: float32 [2, 2, 768, 3072], P(None, None, None, 'fsdp')
- experts_momentum: float32 [2, 2, 768, 3072], P(None, None, None, 'fsdp')
- experts_copy: bfloat16 [2, 2, 768, 3072], P(None, None, None, 'fsdp')
- vectors_gradient: float32 [4, 6, 768], P('grp')
- vectors_moment: float32 [4, 6, 768], P('grp')
- vectors_square: float32 [4, 6, 768], P('grp')
- vectors_master: float32 [6, 768], replicated
- vectors_momentum: float32 [6, 768], replicated
The draws below stay inside these ranges and needn't reach their ends.
Inputs may be any that keep to these rules, and one draw needn't show every extreme that they name: `segments`: on each device's 256 slots: 0 for a first document, 1 for a second one, 2 for padding at the end; each document present has 64 slots or more; in every step and group one device holds a single document of 256 slots. `loss_pos`: A position on the device, inside a document that has two more slots after it. `routes`: at most 192 of one device's 256 tokens name the same expert. `vectors`: rows 0 to 3 near one, the router's rows small.
All inputs are finite; a program needn't handle non-finite values.
Results may differ from the reference program's by a relative error of at most 0.033.
Values may be sent and summed in bfloat16 or wider, within the bound.
A program may use at most 448 MiB of HBM per device.

```python
import math
import jax
import jax.numpy as jnp
import numpy as np
from jax import lax

D = 768
HEADS = 12
HEAD_DIM = 64
FF = 3072
VOCAB = 32128
EXPERTS = 2
INNER = 2
STEP0 = 5
TOK_DEV = 256
LOSS_DEV = 16
MINLEN = 64
CAP = 192
GROUPS = 4
GTOK = 2048
PARAMS = 37065216
N_FSDP = 8


def layout_draw(key):
    keys_four = jax.random.split(jax.random.fold_in(key, 11), 4)
    blocks = INNER * GROUPS * N_FSDP
    first_len = jax.random.randint(keys_four[0], (blocks,), MINLEN, TOK_DEV - MINLEN + 1)
    room = TOK_DEV - first_len - MINLEN + 1
    second_len = MINLEN + jax.random.randint(keys_four[1], (blocks,), 0, room)
    chosen = jax.random.randint(keys_four[2], (INNER * GROUPS, 1), 0, N_FSDP)
    places = jnp.arange(N_FSDP)[None, :]
    whole = (places == chosen).reshape(blocks)
    short = (places == (chosen + 1) % N_FSDP).reshape(blocks)
    first_len = jnp.where(whole, TOK_DEV, jnp.where(short, MINLEN, first_len))
    second_len = jnp.where(whole, 0, jnp.where(short, MINLEN, second_len))
    positions = jnp.arange(TOK_DEV)[None, :]
    segment_ids = (positions >= first_len[:, None]).astype(jnp.int32) + (positions >= (first_len + second_len)[:, None]).astype(jnp.int32)
    valid = first_len - 2 + jnp.maximum(second_len - 2, 0)
    drawn = jax.random.randint(keys_four[3], (blocks, LOSS_DEV), 0, valid[:, None])
    picked = jnp.where(drawn < (first_len - 2)[:, None], drawn, drawn + 2)
    picked = picked.at[:, 0].set(jnp.where(whole, TOK_DEV - 3, picked[:, 0]))
    picked = picked.at[:, 1].set(jnp.where(whole, 0, picked[:, 1]))
    return (segment_ids.reshape(INNER, GROUPS, N_FSDP * TOK_DEV).astype(jnp.int32), picked.reshape(INNER, GROUPS, N_FSDP * LOSS_DEV).astype(jnp.int32))


def draw_segments(key, part):
    return layout_draw(key)[0]


def draw_loss_pos(key, part):
    return layout_draw(key)[1]


def draw_vectors(key, part):
    keys_two = jax.random.split(jax.random.fold_in(key, 5), 2)
    row_ids = jnp.arange(4 + EXPERTS)[:, None]
    gains = 1.0 + 0.18 * jnp.clip(jax.random.normal(keys_two[0], (4 + EXPERTS, D), jnp.float32), -3.0, 3.0)
    router = 0.8 * D ** (-0.5) * jnp.clip(jax.random.normal(keys_two[1], (4 + EXPERTS, D), jnp.float32), -3.0, 3.0)
    return jnp.where(row_ids < 4, gains, router).astype(jnp.float32)


def with_ends(entries, own_key, least, top_value):
    place = [jax.random.randint(jax.random.fold_in(own_key, axis), (), 0, length) for axis, length in enumerate(entries.shape)]
    widest = entries.shape.index(max(entries.shape))
    neighbour = place[:widest] + [(place[widest] + 1) % entries.shape[widest]] + place[widest + 1:]
    return entries.at[tuple(place)].set(least).at[tuple(neighbour)].set(top_value)


def block_levels(own_key, shape, shards, least, largest):
    def one(position, shards_of):
        draws = jax.random.uniform(jax.random.fold_in(jax.random.fold_in(own_key, 6), position), (shards_of,), jnp.float32, least / len(shards), largest / len(shards))
        return jnp.repeat(jnp.exp(draws), shape[position] // shards_of).reshape((-1,) + (1,) * (len(shape) - position - 1))

    level = one(*shards[0])
    for cut in shards[1:]:
        level = level * one(*cut)
    return level


def rank_table(count, skew):
    loads = [(1 << 20) // math.isqrt(rank ** skew) + 1 for rank in range(1, count + 1)]
    spread = 1 + sum(loads) // (1 << 30)
    return np.cumsum(np.array([max(1, weight // spread) for weight in loads]))


def ranked(key, extent, count, lean):
    table = rank_table(count, lean)
    lot = jax.random.randint(jax.random.fold_in(key, 1), extent, 0, int(table[count - 1]))
    grade = jnp.searchsorted(jnp.asarray(table, jnp.int32), lot, side="right")
    return jax.random.permutation(jax.random.fold_in(key, 2), count)[grade].astype(jnp.int32)


def assign_block(rng, own, number, rows, count, top, bound, slope):
    order = jax.random.permutation(rng, count)
    packed, common = portions_of(count, rows * top, bound, slope, True), portions_of(count, rows * top, bound, slope, False)
    places = jnp.arange(count)

    def named(sizes, turn):
        used = int((sizes > 0).sum())
        fixed = max(1, used // 4)
        shifted = fixed + (places - fixed + turn * (used - fixed)) % max(1, count - fixed)
        return jnp.zeros((count,), jnp.int32).at[order[jnp.where(places < fixed, places, shifted)]].set(jnp.asarray(sizes, jnp.int32))

    sizes = jnp.where(number % 4 == 0, named(packed, number // 4), named(common, number - number // 4 - 1))
    mixed = jax.random.permutation(jax.random.fold_in(own, 3), count)
    source_of, taker = mixed[0:count // 2 * 2:2], mixed[1:count // 2 * 2:2]
    margin = jnp.minimum(sizes[source_of] - 1, bound - sizes[taker]) // 2
    margin = jnp.where((source_of == order[0]) | (taker == order[0]) | (sizes[taker] == 0), 0, jnp.maximum(margin, 0))
    shifted = jax.random.randint(jax.random.fold_in(own, 4), (count // 2,), 0, 1 << 20) % (margin + 1)
    sizes = sizes.at[source_of].add(-shifted).at[taker].add(shifted)
    items = jnp.searchsorted(jnp.cumsum(sizes), jnp.arange(rows * top), side="right").astype(jnp.int32)
    grid = items.reshape(top, rows).T
    grid = grid[jax.random.permutation(jax.random.fold_in(own, 1), rows)]
    turn = jax.random.randint(jax.random.fold_in(own, 2), (rows, 1), 0, top)
    return jnp.take_along_axis(grid, (jnp.arange(top)[None, :] + turn) % top, axis=1)


def portions_of(count, total, bound, skew, full):
    weights = [(1 << 20) // math.isqrt(grade ** skew) + 1 for grade in range(1, count + 1)]
    largest = bound if full else min(bound, max(-(-total // count), total * weights[0] // sum(weights)))
    least = 1 if total - largest >= count - 1 else 0
    given, rest = [largest] + [least] * (count - 1), total - largest - least * (count - 1)
    while rest > 0:
        movable = [i for i in range(1, count) if given[i] < largest] or [i for i in range(1, count) if given[i] < bound]
        pool, left = sum([weights[i] for i in movable]), rest
        for i in movable:
            extra = min(bound - given[i], max(1, left * weights[i] // pool), rest)
            given[i] = given[i] + extra
            rest = rest - extra
    return np.array(given)


def normal_values(key, dims, deviation, bound, shards=(), kind=jnp.bfloat16):
    loudness = block_levels(key, dims, shards, -0.22, 0.18) if shards else 1.0
    values = jax.random.normal(key, dims, jnp.float32) * deviation * loudness
    return jnp.minimum(jnp.maximum(values, -bound), bound).astype(kind)


def setup_inputs(seed: int = 0) -> dict:
    key_list = jax.random.split(jax.random.key(seed), 21)
    tokens = with_ends(ranked(key_list[0], (INNER, GROUPS, GTOK), VOCAB, 2), jax.random.fold_in(key_list[0], 3), 0, VOCAB - 1).astype(jnp.int32)
    routes_keys = jax.random.split(jax.random.fold_in(key_list[1], 1), INNER * GROUPS * GTOK // TOK_DEV)
    routes_turns = jax.random.permutation(jax.random.fold_in(key_list[1], 3), INNER * GROUPS * GTOK // TOK_DEV)
    routes = jax.vmap(lambda own, number: assign_block(jax.random.fold_in(key_list[1], 2), own, number, TOK_DEV, EXPERTS, 1, CAP, 1))(routes_keys, routes_turns).reshape((INNER, GROUPS, GTOK, 1))
    segments = draw_segments(jax.random.fold_in(key_list[20], 71), 0)
    loss_pos = draw_loss_pos(jax.random.fold_in(key_list[20], 71), 0)
    embedding = normal_values(key_list[4], (VOCAB, D), 1.5, 6.0, ((0, 8),), jnp.float32)
    embedding_first = normal_values(key_list[5], (GROUPS, VOCAB, D), (0.03 * (0.0025 / (N_FSDP * LOSS_DEV * PARAMS)) ** 0.5), 1.1920928955078125e-07, ((0, 4), (1, 8)), jnp.float32)
    embedding_second = jnp.clip(jnp.exp(math.log(2.107771287151658e-13) - 2.5902672 * jax.random.uniform(key_list[6], (GROUPS, VOCAB, D), jnp.float32) ** block_levels(key_list[6], (GROUPS, VOCAB, D), ((0, 4), (1, 8)), -0.2, 0.2)), 1.5808284314824256e-14, 2.107771287151658e-13)
    embedding_outer = normal_values(key_list[7], (VOCAB, D), 0.5, 3.0, ((0, 8),), jnp.float32)
    attention = normal_values(key_list[8], (5, D, D), D ** -0.5, 0.21875, ((1, 8),), jnp.float32)
    attention_first = normal_values(key_list[9], (GROUPS, 5, D, D), (0.11 * (0.0025 / (N_FSDP * LOSS_DEV * PARAMS)) ** 0.5), 4.76837158203125e-07, ((0, 4), (2, 8)), jnp.float32)
    attention_second = jnp.clip(jnp.exp(math.log(2.107771287151658e-13) - 2.5902672 * jax.random.uniform(key_list[10], (GROUPS, 5, D, D), jnp.float32) ** block_levels(key_list[10], (GROUPS, 5, D, D), ((0, 4), (2, 8)), -0.2, 0.2)), 1.5808284314824256e-14, 2.107771287151658e-13)
    attention_outer = normal_values(key_list[11], (5, D, D), 0.012, 0.0625, ((1, 8),), jnp.float32)
    experts = normal_values(key_list[12], (EXPERTS, 2, D, FF), D ** -0.5, 0.21875, ((3, 8),), jnp.float32)
    experts_first = normal_values(key_list[13], (GROUPS, EXPERTS, 2, D, FF), (0.11 * (0.0025 / (N_FSDP * LOSS_DEV * PARAMS)) ** 0.5), 4.76837158203125e-07, ((0, 4), (4, 8)), jnp.float32)
    experts_second = jnp.clip(jnp.exp(math.log(5.269428217879145e-14) - 2.5902672 * jax.random.uniform(key_list[14], (GROUPS, EXPERTS, 2, D, FF), jnp.float32) ** block_levels(key_list[14], (GROUPS, EXPERTS, 2, D, FF), ((0, 4), (4, 8)), -0.2, 0.2)), 3.952071078706064e-15, 5.269428217879145e-14)
    experts_outer = normal_values(key_list[15], (EXPERTS, 2, D, FF), 0.012, 0.0625, ((3, 8),), jnp.float32)
    vectors = draw_vectors(jax.random.fold_in(key_list[20], 71), 0)
    vectors_first = normal_values(key_list[17], (GROUPS, 4 + EXPERTS, D), (0.44 * (0.0025 / (N_FSDP * LOSS_DEV * PARAMS)) ** 0.5), 1.9073486328125e-06, ((0, 4),), jnp.float32)
    vectors_second = jnp.clip(jnp.exp(math.log(3.3724340594426527e-12) - 2.5902672 * jax.random.uniform(key_list[18], (GROUPS, 4 + EXPERTS, D), jnp.float32) ** block_levels(key_list[18], (GROUPS, 4 + EXPERTS, D), ((0, 4),), -0.2, 0.2)), 2.529325490371881e-13, 3.3724340594426527e-12)
    vectors_outer = normal_values(key_list[19], (4 + EXPERTS, D), 0.1, 0.625, (), jnp.float32)
    return dict(tokens=tokens, routes=routes, segments=segments, loss_pos=loss_pos, embedding=embedding, embedding_first=embedding_first, embedding_second=embedding_second, embedding_outer=embedding_outer, attention=attention, attention_first=attention_first, attention_second=attention_second, attention_outer=attention_outer, experts=experts, experts_first=experts_first, experts_second=experts_second, experts_outer=experts_outer, vectors=vectors, vectors_first=vectors_first, vectors_second=vectors_second, vectors_outer=vectors_outer)


@jax.custom_vjp
def low(v):
    return lax.optimization_barrier(v.astype(jnp.bfloat16)).astype(jnp.float32)

@jax.custom_vjp
def low_back(v):
    return v

def low_keep(v):
    return (low(v), None)

def low_pass(kept, grad):
    return (grad,)

def back_keep(v):
    return (v, None)

def back_low(kept, grad):
    return (low(grad),)
low.defvjp(low_keep, low_pass)
low_back.defvjp(back_keep, back_low)
HIGH = lax.Precision.HIGHEST
EPSILON = 1e-06
ATTN_GAIN = 8.0
SECOND_WEIGHT = 0.3
BETA_ONE = 0.9
BETA_TWO = 0.95
ADAM_EPS = 1e-08
DECAY = 0.1
LR_EMBED = 0.5
LR_MATRIX = 0.012
LR_GAIN = 0.3
LR_ROUTER = 0.012
OUTER_RATE = 0.7
OUTER_MOMENTUM = 0.9

def norm_apply(x, gain_row):
    return x * lax.rsqrt(lax.optimization_barrier(jnp.mean(x * x, axis=-1, keepdims=True)) + EPSILON) * gain_row

def block_loss(weights, token_ids, seg_ids, route_ids, pick_ids):
    embedding, attention, experts, vectors = weights
    embed_low = low(embedding)
    attn_low = low(attention)
    expert_low = low(experts)
    count_rows = token_ids.shape[0]
    x_embed = low_back(embed_low[token_ids])
    a = low(norm_apply(x_embed, vectors[0]))
    triple = jnp.einsum('td,jde->jte', a, attn_low[0:3], precision=HIGH)
    triple = low(low_back(triple)).reshape(3, count_rows, HEADS, HEAD_DIM)
    scores = jnp.einsum('qhd,khd->hqk', triple[0], triple[1], precision=HIGH) * HEAD_DIM ** (-0.5)
    scores = low_back(scores)
    places = jnp.arange(count_rows)
    allowed = (places[None, :] <= places[:, None]) & (seg_ids[:, None] == seg_ids[None, :])
    scores = jnp.where(allowed[None], scores, -1e+30)
    probs_low = low(jax.nn.softmax(scores, axis=-1))
    attended = jnp.einsum('hqk,khd->qhd', probs_low, triple[2], precision=HIGH).reshape(count_rows, D)
    attended = low(low_back(attended))
    x_attn = x_embed + low_back(ATTN_GAIN * jnp.dot(attended, attn_low[3], precision=HIGH))
    b = norm_apply(x_attn, vectors[1])
    router_probs = jax.nn.softmax(jnp.dot(b, vectors[4:].T, precision=HIGH), axis=-1)
    gating = jnp.take_along_axis(router_probs, route_ids[:, None], axis=1)[:, 0]
    onehot = (route_ids[:, None] == jnp.arange(EXPERTS, dtype=jnp.int32)[None, :]).astype(jnp.int32)
    slot_ids = (lax.optimization_barrier(jnp.sum(jnp.cumsum(onehot, axis=0) * onehot, axis=1)) - 1).astype(jnp.int32)
    buffer_in = jnp.zeros((EXPERTS, CAP, D), jnp.float32).at[route_ids, slot_ids].set(low(b))
    hidden_pre = low_back(jnp.einsum('ecd,edf->ecf', buffer_in, expert_low[:, 0], precision=HIGH))
    hidden_act = low(jax.nn.gelu(hidden_pre, approximate=True))
    buffer_out = jnp.einsum('ecf,edf->ecd', hidden_act, expert_low[:, 1], precision=HIGH)
    returned = low_back(buffer_out[route_ids, slot_ids])
    x_final = x_attn + gating[:, None] * returned
    z_rows = x_final[pick_ids]
    first_rows = low(norm_apply(z_rows, vectors[2]))
    middle = low_back(jnp.dot(first_rows, attn_low[4], precision=HIGH))
    second_rows = low(norm_apply(middle, vectors[3]))
    total_loss = jnp.zeros((), jnp.float32)
    for rows_in, offset, weight_here in ((first_rows, 1, 1.0), (second_rows, 2, SECOND_WEIGHT)):
        logits = low_back(jnp.dot(rows_in, embed_low.T, precision=HIGH) * (2.0 * D ** (-0.5)))
        targets = token_ids[pick_ids + offset]
        logsum = jax.scipy.special.logsumexp(logits, axis=-1)
        chosen = jnp.take_along_axis(logits, targets[:, None], axis=1)[:, 0]
        total_loss = total_loss + weight_here * jnp.sum(logsum - chosen)
    return total_loss

def group_loss(weights, token_ids, seg_ids, route_ids, pick_ids):
    shaped = (token_ids.reshape(N_FSDP, TOK_DEV), seg_ids.reshape(N_FSDP, TOK_DEV), route_ids.reshape(N_FSDP, TOK_DEV), pick_ids.reshape(N_FSDP, LOSS_DEV))
    checked = jax.checkpoint(block_loss)
    totals = lax.map(lambda items: checked(weights, *items), shaped)
    return jnp.sum(totals) / (N_FSDP * LOSS_DEV)

def adam_update(weight, first_moment, second, gradient, step_float, rate_here, decay_here):
    first_new = BETA_ONE * first_moment + (1.0 - BETA_ONE) * gradient
    second_new = BETA_TWO * second + (1.0 - BETA_TWO) * gradient * gradient
    first_hat = first_new / (1.0 - BETA_ONE ** step_float)
    second_hat = second_new / (1.0 - BETA_TWO ** step_float)
    weight_new = weight - rate_here * (first_hat / (jnp.sqrt(second_hat) + ADAM_EPS) + decay_here * weight)
    return (weight_new, first_new, second_new)

def reference(tokens, routes, segments, loss_pos, embedding, embedding_first, embedding_second, embedding_outer, attention, attention_first, attention_second, attention_outer, experts, experts_first, experts_second, experts_outer, vectors, vectors_first, vectors_second, vectors_outer):
    masters = (embedding, attention, experts, vectors)
    firsts = (embedding_first, attention_first, experts_first, vectors_first)
    seconds = (embedding_second, attention_second, experts_second, vectors_second)
    outers = (embedding_outer, attention_outer, experts_outer, vectors_outer)
    vector_rates = jnp.where(jnp.arange(4 + EXPERTS)[:, None] < 4, LR_GAIN, LR_ROUTER)
    rate_list = (LR_EMBED, LR_MATRIX, LR_MATRIX, vector_rates)
    decay_list = (DECAY, DECAY, DECAY, 0.0)
    threshold = 0.05 / math.sqrt(N_FSDP * LOSS_DEV)
    loss_rows, norm_rows, final_weights, final_first, final_second, last_vectors = ([], [], [], [], [], [])
    for group_idx in range(GROUPS):
        weights = masters
        first_now = tuple((element[group_idx] for element in firsts))
        second_now = tuple((element[group_idx] for element in seconds))
        loss_list, norm_list = ([], [])
        for inner_step in range(INNER):

            def objective(*current):
                return group_loss(current, tokens[inner_step, group_idx], segments[inner_step, group_idx], routes[inner_step, group_idx, :, 0], loss_pos[inner_step, group_idx])
            loss_value, pullback = jax.vjp(objective, *weights)
            gradients = pullback(jnp.ones((), jnp.float32))
            total_sq = jnp.sum(gradients[0] * gradients[0]) + jnp.sum(gradients[1] * gradients[1]) + jnp.sum(gradients[2] * gradients[2]) + jnp.sum(gradients[3] * gradients[3])
            norm_value = jnp.sqrt(total_sq)
            factor = jnp.minimum(1.0, threshold / norm_value)
            gradients = tuple((element * factor for element in gradients))
            step_float = float(STEP0 + inner_step + 1)
            results = [adam_update(weights[k], first_now[k], second_now[k], gradients[k], step_float, rate_list[k], decay_list[k]) for k in range(4)]
            weights = tuple((element[0] for element in results))
            first_now = tuple((element[1] for element in results))
            second_now = tuple((element[2] for element in results))
            loss_list.append(loss_value)
            norm_list.append(norm_value)
        loss_rows.append(jnp.stack(loss_list))
        norm_rows.append(jnp.stack(norm_list))
        final_weights.append(weights)
        final_first.append(first_now)
        final_second.append(second_now)
        last_vectors.append(gradients[3])
    new_master, new_outer, moment_out, square_out = ([], [], [], [])
    for k in range(4):
        delta_sum = masters[k] - final_weights[0][k]
        for group_idx in range(1, GROUPS):
            delta_sum = delta_sum + (masters[k] - final_weights[group_idx][k])
        delta_mean = delta_sum / GROUPS
        outer_new = OUTER_MOMENTUM * outers[k] + delta_mean
        new_outer.append(outer_new)
        new_master.append(masters[k] - OUTER_RATE * (delta_mean + OUTER_MOMENTUM * outer_new))
        moment_out.append(jnp.stack([element[k] for element in final_first]))
        square_out.append(jnp.stack([element[k] for element in final_second]))
    return (jnp.stack(loss_rows), jnp.stack(norm_rows), moment_out[0], square_out[0], new_master[0], new_outer[0], new_master[0].astype(jnp.bfloat16), moment_out[1], square_out[1], new_master[1], new_outer[1], new_master[1].astype(jnp.bfloat16), moment_out[2], square_out[2], new_master[2], new_outer[2], new_master[2].astype(jnp.bfloat16), jnp.stack(last_vectors), moment_out[3], square_out[3], new_master[3], new_outer[3])
```

```python
import math

import jax
import jax.numpy as jnp
from jax import lax
from jax.sharding import PartitionSpec as P

D = 768
HEADS = 12
HEAD_DIM = 64
EXPERTS = 2
STEP0 = 5
CAP = 192


HIGH = lax.Precision.HIGHEST
EPSILON = 1e-06
ATTN_GAIN = 8.0
SECOND_WEIGHT = 0.3
BETA_ONE = 0.9
BETA_TWO = 0.95
ADAM_EPS = 1e-08
DECAY = 0.1
LR_EMBED = 0.5
LR_MATRIX = 0.012
LR_GAIN = 0.3
LR_ROUTER = 0.012
OUTER_RATE = 0.7
OUTER_MOMENTUM = 0.9


def for_sending(value):

    def short(part):
        return part.astype(jnp.bfloat16) if part.dtype == jnp.float32 else part

    return jax.tree.map(short, value)


def smooth_act(values):
    return jax.nn.gelu(values, approximate=True)


def norm_apply(x, gain_row):
    factor = lax.rsqrt(jnp.mean(x * x, axis=-1, keepdims=True) + EPSILON)
    return (x * factor * gain_row, factor)


def norm_back(x, factor, gain_row, upstream):
    normed = x * factor
    gain_grad = jnp.sum(upstream * normed, axis=0)
    scaled = upstream * gain_row
    return (
        factor * (scaled - normed * jnp.mean(scaled * normed, axis=-1, keepdims=True)),
        gain_grad,
    )


def rows_forward(attn_low, vector_w, x_embed, seg_ids, pick_ids):
    a_float, a_factor = norm_apply(x_embed, vector_w[0])
    a = a_float.astype(jnp.bfloat16)
    a_rows = a[pick_ids]
    q = jnp.dot(a_rows, attn_low[0], preferred_element_type=jnp.float32).astype(jnp.bfloat16)
    k = jnp.dot(a, attn_low[1], preferred_element_type=jnp.float32).astype(jnp.bfloat16)
    v = jnp.dot(a, attn_low[2], preferred_element_type=jnp.float32).astype(jnp.bfloat16)
    places = jnp.arange(x_embed.shape[0])
    allowed = (places[None, :] <= pick_ids[:, None]) & (
        seg_ids[pick_ids][:, None] == seg_ids[None, :]
    )
    count = pick_ids.shape[0]
    head_of = jnp.arange(D) // HEAD_DIM
    head_mask = (head_of[None, None, :] == jnp.arange(HEADS)[:, None, None])
    q_wide = jnp.where(head_mask, q[None], 0).reshape(HEADS * count, D)
    scores = jnp.einsum("rd,td->rt", q_wide, k, preferred_element_type=jnp.float32) * HEAD_DIM ** (-0.5)
    allowed = jnp.tile(allowed, (HEADS, 1))
    scores = jnp.where(allowed, scores, -1e30)
    exponent = jnp.exp(scores - jnp.max(scores, axis=-1, keepdims=True))
    probs = exponent / jnp.sum(exponent, axis=-1, keepdims=True)
    spread = jnp.dot(probs.astype(jnp.bfloat16), v, preferred_element_type=jnp.float32)
    o = jnp.sum(jnp.where(head_mask, spread.reshape(HEADS, count, D), 0.0), axis=0).astype(jnp.bfloat16)
    x_attn = x_embed[pick_ids] + ATTN_GAIN * jnp.dot(o, attn_low[3], preferred_element_type=jnp.float32)
    return x_attn, (a_factor, a, a_rows, q_wide, k, v, probs, o, head_mask)


def rows_backward(attn_low, vector_w, x_embed, kept, dx_attn, pick_ids):
    a_factor, a, a_rows, q_wide, k, v, probs, o, head_mask = kept
    count = pick_ids.shape[0]
    dbranch = dx_attn.astype(jnp.bfloat16)
    dwout = ATTN_GAIN * jnp.dot(o.T, dbranch, preferred_element_type=jnp.float32)
    do = (ATTN_GAIN * jnp.dot(dbranch, attn_low[3].T, preferred_element_type=jnp.float32)).astype(jnp.bfloat16)
    do_wide = jnp.where(head_mask, do[None], 0).reshape(HEADS * count, D)
    dprobs = jnp.einsum("rd,td->rt", do_wide, v, preferred_element_type=jnp.float32)
    dscores = (probs * (dprobs - jnp.sum(probs * dprobs, axis=-1, keepdims=True))).astype(jnp.bfloat16)
    factor_qk = HEAD_DIM ** (-0.5)
    dq = jnp.dot(dscores, k, preferred_element_type=jnp.float32).reshape(HEADS, count, D)
    dq = (jnp.sum(jnp.where(head_mask, dq, 0.0), axis=0) * factor_qk).astype(jnp.bfloat16)
    dk = (jnp.dot(dscores.T, q_wide, preferred_element_type=jnp.float32) * factor_qk).astype(jnp.bfloat16)
    dv = jnp.dot(probs.astype(jnp.bfloat16).T, do_wide, preferred_element_type=jnp.float32).astype(jnp.bfloat16)
    dlayer = jnp.stack(
        [
            jnp.dot(a_rows.T, dq, preferred_element_type=jnp.float32),
            jnp.dot(a.T, dk, preferred_element_type=jnp.float32),
            jnp.dot(a.T, dv, preferred_element_type=jnp.float32),
            dwout,
        ]
    )
    places = jnp.arange(x_embed.shape[0])
    pick_mask = (places[:, None] == pick_ids[None, :]).astype(jnp.float32)
    dinput = jnp.dot(dk, attn_low[1].T, preferred_element_type=jnp.float32)
    dinput = dinput + jnp.dot(dv, attn_low[2].T, preferred_element_type=jnp.float32)
    dq_in = jnp.dot(dq, attn_low[0].T, preferred_element_type=jnp.float32)
    dinput = dinput + jnp.dot(pick_mask, dq_in, precision=HIGH)
    dx, gain_attn = norm_back(x_embed, a_factor, vector_w[0], dinput)
    return dx + jnp.dot(pick_mask, dx_attn, precision=HIGH), dlayer, gain_attn


def gather_rows(value, axis=0):
    return lax.all_gather(value, "fsdp", axis=axis, tiled=True)


def scatter_rows(value, axis=0):
    return lax.psum_scatter(
        value.astype(jnp.bfloat16), "fsdp", scatter_dimension=axis, tiled=True
    ).astype(jnp.float32)


def adam_update(weight, first_moment, second, gradient, step_float, rate_here, decay_here):
    first_new = BETA_ONE * first_moment + (1.0 - BETA_ONE) * gradient
    second_new = BETA_TWO * second + (1.0 - BETA_TWO) * gradient * gradient
    first_hat = first_new / (1.0 - BETA_ONE**step_float)
    second_hat = second_new / (1.0 - BETA_TWO**step_float)
    weight_new = weight - rate_here * (
        first_hat / (jnp.sqrt(second_hat) + ADAM_EPS) + decay_here * weight
    )
    return (weight_new, first_new, second_new)


def shards(
    tokens,
    routes,
    segments,
    loss_pos,
    embedding,
    embedding_first,
    embedding_second,
    embedding_outer,
    attention,
    attention_first,
    attention_second,
    attention_outer,
    experts,
    experts_first,
    experts_second,
    experts_outer,
    vectors,
    vectors_first,
    vectors_second,
    vectors_outer,
):
    inner_count = tokens.shape[0]
    vocab_shard = embedding.shape[0]
    vocab_start = lax.axis_index("fsdp") * vocab_shard
    group_count = lax.axis_size("grp")
    row_total = lax.axis_size("fsdp") * loss_pos.shape[2]
    threshold = 0.05 / math.sqrt(row_total)
    logit_scale = 2.0 * D ** (-0.5)
    all_ids = lax.all_gather(tokens[:, 0, :], "fsdp", axis=1, tiled=True)
    vocab_places = jnp.arange(vocab_shard)
    head_weights = jnp.array([1.0, SECOND_WEIGHT], jnp.float32)
    vector_rates = jnp.where(jnp.arange(vectors.shape[0])[:, None] < 4, LR_GAIN, LR_ROUTER)
    rate_list = (LR_EMBED, LR_MATRIX, LR_MATRIX, vector_rates)
    decay_list = (DECAY, DECAY, DECAY, 0.0)
    weights_now = (embedding, attention, experts, vectors)
    first_now = (embedding_first[0], attention_first[0], experts_first[0], vectors_first[0])
    second_now = (embedding_second[0], attention_second[0], experts_second[0], vectors_second[0])
    loss_list = []
    norm_list = []
    for inner_step in range(inner_count):
        embed_w, attn_w, expert_w, vector_w = weights_now
        embed_low = embed_w.astype(jnp.bfloat16)
        attn_low = lax.all_gather(attn_w.astype(jnp.bfloat16), "fsdp", axis=1, tiled=True)
        expert_low = expert_w.astype(jnp.bfloat16)
        ids_group = all_ids[inner_step]
        ids_local = tokens[inner_step, 0]
        seg_ids = segments[inner_step, 0]
        route_ids = routes[inner_step, 0, :, 0]
        pick_ids = loss_pos[inner_step, 0]
        chosen = ids_group - vocab_start
        inside = (chosen >= 0) & (chosen < vocab_shard)
        looked = jnp.take(embed_low, jnp.clip(chosen, 0, vocab_shard - 1), axis=0).astype(
            jnp.float32
        )
        x_embed = lax.psum_scatter(
            jnp.where(inside[:, None], looked, 0.0).astype(jnp.bfloat16),
            "fsdp",
            scatter_dimension=0,
            tiled=True,
        ).astype(jnp.float32)
        x_attn, kept = rows_forward(attn_low, vector_w, x_embed, seg_ids, pick_ids)
        b, b_factor = norm_apply(x_attn, vector_w[1])
        router_probs = jax.nn.softmax(jnp.dot(b, vector_w[4:].T, precision=HIGH), axis=-1)
        row_routes = route_ids[pick_ids]
        onehot = (row_routes[:, None] == jnp.arange(EXPERTS)[None, :]).astype(jnp.float32)
        gating = jnp.sum(router_probs * onehot, axis=1)
        b_all = gather_rows(b.astype(jnp.bfloat16))
        routes_all = gather_rows(row_routes)
        route_mask = routes_all[None, :, None] == jnp.arange(EXPERTS)[:, None, None]
        hidden_pre = jnp.einsum("cd,edf->ecf", b_all, expert_low[:, 0], preferred_element_type=jnp.float32)
        hidden_act = jnp.where(route_mask, smooth_act(hidden_pre), 0.0).astype(jnp.bfloat16)
        y_part = jnp.einsum("ecf,edf->cd", hidden_act, expert_low[:, 1], preferred_element_type=jnp.float32)
        returned = scatter_rows(y_part)
        z_rows = x_attn + gating[:, None] * returned
        first_float, first_factor = norm_apply(z_rows, vector_w[2])
        first_rows = first_float.astype(jnp.bfloat16)
        middle = jnp.dot(first_rows, attn_low[4], preferred_element_type=jnp.float32)
        second_float, second_factor = norm_apply(middle, vector_w[3])
        targets = jnp.stack([ids_local[pick_ids + 1], ids_local[pick_ids + 2]])
        rows_all, targets_all = (
            lax.all_gather(
                jnp.stack([first_rows, second_float.astype(jnp.bfloat16)]),
                "fsdp",
                axis=1,
                tiled=True,
            ),
            lax.all_gather(targets, "fsdp", axis=1, tiled=True),
        )
        logits = (
            jnp.einsum("jrd,vd->jrv", rows_all, embed_low, preferred_element_type=jnp.float32)
            * logit_scale
        )
        relative = targets_all - vocab_start
        onehot_target = (vocab_places[None, None, :] == relative[:, :, None]).astype(jnp.float32)
        target_part = jnp.sum(onehot_target * logits, axis=-1)
        local_top = jnp.max(logits, axis=-1)
        local_sum = jnp.sum(jnp.exp(logits - local_top[:, :, None]), axis=-1)
        parts = lax.all_gather(jnp.stack([local_top, local_sum, target_part]), "fsdp")
        row_top = jnp.max(parts[:, 0], axis=0)
        sum_exp = jnp.sum(parts[:, 1] * jnp.exp(parts[:, 0] - row_top), axis=0)
        target_logit = jnp.sum(parts[:, 2], axis=0)
        logsum = row_top + jnp.log(sum_exp)
        loss_list.append(jnp.sum(head_weights[:, None] * (logsum - target_logit)) / row_total)
        dlogits = (
            (jnp.exp(logits - logsum[:, :, None]) - onehot_target)
            * (head_weights / row_total)[:, None, None]
        ).astype(jnp.bfloat16)
        dembed = (
            jnp.einsum("jrv,jrd->vd", dlogits, rows_all, preferred_element_type=jnp.float32)
            * logit_scale
        )
        drows = (
            jnp.einsum("jrv,vd->jrd", dlogits, embed_low, preferred_element_type=jnp.float32)
            * logit_scale
        )
        drows_own = lax.psum_scatter(
            drows.astype(jnp.bfloat16), "fsdp", scatter_dimension=1, tiled=True
        ).astype(jnp.float32)
        dmiddle, gain_mtp = norm_back(middle, second_factor, vector_w[3], drows_own[1])
        dmiddle_low = dmiddle.astype(jnp.bfloat16)
        dsecond_proj = jnp.dot(first_rows.T, dmiddle_low, preferred_element_type=jnp.float32)
        dfirst = drows_own[0] + jnp.dot(
            dmiddle_low, attn_low[4].T, preferred_element_type=jnp.float32
        )
        dz_rows, gain_final = norm_back(z_rows, first_factor, vector_w[2], dfirst)
        dgating = jnp.sum(dz_rows * returned, axis=1)
        dy_all = gather_rows((gating[:, None] * dz_rows).astype(jnp.bfloat16))
        dy_masked = jnp.where(route_mask, dy_all[None], 0)
        down_grad = jnp.einsum("ecf,ecd->edf", hidden_act, dy_masked, preferred_element_type=jnp.float32)
        dhidden = jnp.einsum("ecd,edf->ecf", dy_masked, expert_low[:, 1], preferred_element_type=jnp.float32)
        unused, act_back = jax.vjp(smooth_act, hidden_pre)
        dhidden_pre = act_back(dhidden)[0].astype(jnp.bfloat16)
        up_grad = jnp.einsum("cd,ecf->edf", b_all, dhidden_pre, preferred_element_type=jnp.float32)
        dexpert = jnp.stack([up_grad, down_grad], axis=1)
        db_part = jnp.einsum("ecf,edf->cd", dhidden_pre, expert_low[:, 0], preferred_element_type=jnp.float32)
        dnormed = scatter_rows(db_part)
        prob_grad = onehot * dgating[:, None]
        dlogit = router_probs * (prob_grad - jnp.sum(router_probs * prob_grad, axis=1, keepdims=True))
        drouter = jnp.dot(dlogit.T, b, precision=HIGH)
        dnormed = dnormed + jnp.dot(dlogit, vector_w[4:], precision=HIGH)
        dx_part, gain_ffn = norm_back(x_attn, b_factor, vector_w[1], dnormed)
        dx_embed, dlayer, gain_attn = rows_backward(
            attn_low, vector_w, x_embed, kept, dz_rows + dx_part, pick_ids
        )
        dattn = scatter_rows(jnp.concatenate([dlayer, dsecond_proj[None]], axis=0), axis=1)
        gather_chosen = ids_group - vocab_start
        gather_inside = (gather_chosen >= 0) & (gather_chosen < vocab_shard)
        seg_index = jnp.where(gather_inside, gather_chosen, vocab_shard)
        added = jax.ops.segment_sum(
            lax.all_gather(dx_embed.astype(jnp.bfloat16), "fsdp", axis=0, tiled=True).astype(
                jnp.float32
            ),
            seg_index,
            num_segments=vocab_shard + 1,
        )
        dembed = dembed + added[:vocab_shard]
        dvector_part = jnp.concatenate(
            [jnp.stack([gain_attn, gain_ffn, gain_final, gain_mtp]), drouter], axis=0
        )
        squares = jnp.sum(dembed * dembed) + jnp.sum(dattn * dattn) + jnp.sum(dexpert * dexpert)
        dvector, squares_all = lax.psum((dvector_part, squares), "fsdp")
        norm_value = jnp.sqrt(squares_all + jnp.sum(dvector * dvector))
        norm_list.append(norm_value)
        factor = jnp.minimum(1.0, threshold / norm_value)
        gradients = (dembed * factor, dattn * factor, dexpert * factor, dvector * factor)
        step_float = float(STEP0 + inner_step + 1)
        results = [
            adam_update(
                weights_now[k],
                first_now[k],
                second_now[k],
                gradients[k],
                step_float,
                rate_list[k],
                decay_list[k],
            )
            for k in range(4)
        ]
        weights_now = tuple((element[0] for element in results))
        first_now = tuple((element[1] for element in results))
        second_now = tuple((element[2] for element in results))
    masters = (embedding, attention, experts, vectors)
    outers = (embedding_outer, attention_outer, experts_outer, vectors_outer)
    deltas = tuple((master - current for master, current in zip(masters, weights_now)))
    summed = jax.tree.map(
        lambda part: part.astype(jnp.float32), lax.psum(for_sending(deltas), "grp")
    )
    new_outer = []
    new_master = []
    for k in range(4):
        delta_mean = summed[k] / group_count
        outer_new = OUTER_MOMENTUM * outers[k] + delta_mean
        new_outer.append(outer_new)
        new_master.append(masters[k] - OUTER_RATE * (delta_mean + OUTER_MOMENTUM * outer_new))
    return (
        jnp.stack(loss_list)[None],
        jnp.stack(norm_list)[None],
        first_now[0][None],
        second_now[0][None],
        new_master[0],
        new_outer[0],
        new_master[0].astype(jnp.bfloat16),
        first_now[1][None],
        second_now[1][None],
        new_master[1],
        new_outer[1],
        new_master[1].astype(jnp.bfloat16),
        first_now[2][None],
        second_now[2][None],
        new_master[2],
        new_outer[2],
        new_master[2].astype(jnp.bfloat16),
        gradients[3][None],
        first_now[3][None],
        second_now[3][None],
        new_master[3],
        new_outer[3],
    )


def solution(mesh):
    return jax.shard_map(
        shards,
        mesh=mesh,
        in_specs=(
            P(None, "grp", "fsdp"),
            P(None, "grp", "fsdp", None),
            P(None, "grp", "fsdp"),
            P(None, "grp", "fsdp"),
            P("fsdp", None),
            P("grp", "fsdp", None),
            P("grp", "fsdp", None),
            P("fsdp", None),
            P(None, "fsdp", None),
            P("grp", None, "fsdp", None),
            P("grp", None, "fsdp", None),
            P(None, "fsdp", None),
            P(None, None, None, "fsdp"),
            P("grp", None, None, None, "fsdp"),
            P("grp", None, None, None, "fsdp"),
            P(None, None, None, "fsdp"),
            P(),
            P("grp", None, None),
            P("grp", None, None),
            P(),
        ),
        out_specs=(
            P("grp", None),
            P("grp", None),
            P("grp", "fsdp", None),
            P("grp", "fsdp", None),
            P("fsdp", None),
            P("fsdp", None),
            P("fsdp", None),
            P("grp", None, "fsdp", None),
            P("grp", None, "fsdp", None),
            P(None, "fsdp", None),
            P(None, "fsdp", None),
            P(None, "fsdp", None),
            P("grp", None, None, None, "fsdp"),
            P("grp", None, None, None, "fsdp"),
            P(None, None, None, "fsdp"),
            P(None, None, None, "fsdp"),
            P(None, None, None, "fsdp"),
            P("grp", None, None),
            P("grp", None, None),
            P("grp", None, None),
            P(),
            P(),
        ),
        check_vma=False,
    )
```

```python
import functools
import math

import jax
import jax.numpy as jnp
from jax import lax
from jax.experimental import pallas as pl
from jax.experimental.pallas import tpu as pltpu
from jax.sharding import PartitionSpec as P

D = 768
HEADS = 12
HEAD_DIM = 64
EXPERTS = 2
STEP0 = 5
CAP = 192


HIGH = lax.Precision.HIGHEST
EPSILON = 1e-06
ATTN_GAIN = 8.0
SECOND_WEIGHT = 0.3
BETA_ONE = 0.9
BETA_TWO = 0.95
ADAM_EPS = 1e-08
DECAY = 0.1
LR_EMBED = 0.5
LR_MATRIX = 0.012
LR_GAIN = 0.3
LR_ROUTER = 0.012
OUTER_RATE = 0.7
OUTER_MOMENTUM = 0.9


def for_sending(value):

    def short(part):
        return part.astype(jnp.bfloat16) if part.dtype == jnp.float32 else part

    return jax.tree.map(short, value)


def smooth_act(values):
    return jax.nn.gelu(values, approximate=True)


def norm_apply(x, gain_row):
    factor = lax.rsqrt(jnp.mean(x * x, axis=-1, keepdims=True) + EPSILON)
    return (x * factor * gain_row, factor)


def norm_back(x, factor, gain_row, upstream):
    normed = x * factor
    gain_grad = jnp.sum(upstream * normed, axis=0)
    scaled = upstream * gain_row
    return (
        factor * (scaled - normed * jnp.mean(scaled * normed, axis=-1, keepdims=True)),
        gain_grad,
    )


def rows_forward(attn_low, vector_w, x_embed, seg_ids, pick_ids):
    a_float, a_factor = norm_apply(x_embed, vector_w[0])
    a = a_float.astype(jnp.bfloat16)
    a_rows = a[pick_ids]
    q = jnp.dot(a_rows, attn_low[0], preferred_element_type=jnp.float32).astype(jnp.bfloat16)
    k = jnp.dot(a, attn_low[1], preferred_element_type=jnp.float32).astype(jnp.bfloat16)
    v = jnp.dot(a, attn_low[2], preferred_element_type=jnp.float32).astype(jnp.bfloat16)
    places = jnp.arange(x_embed.shape[0])
    allowed = (places[None, :] <= pick_ids[:, None]) & (
        seg_ids[pick_ids][:, None] == seg_ids[None, :]
    )
    count = pick_ids.shape[0]
    head_of = jnp.arange(D) // HEAD_DIM
    head_mask = (head_of[None, None, :] == jnp.arange(HEADS)[:, None, None])
    q_wide = jnp.where(head_mask, q[None], 0).reshape(HEADS * count, D)
    scores = jnp.einsum("rd,td->rt", q_wide, k, preferred_element_type=jnp.float32) * HEAD_DIM ** (-0.5)
    allowed = jnp.tile(allowed, (HEADS, 1))
    scores = jnp.where(allowed, scores, -1e30)
    exponent = jnp.exp(scores - jnp.max(scores, axis=-1, keepdims=True))
    probs = exponent / jnp.sum(exponent, axis=-1, keepdims=True)
    spread = jnp.dot(probs.astype(jnp.bfloat16), v, preferred_element_type=jnp.float32)
    o = jnp.sum(jnp.where(head_mask, spread.reshape(HEADS, count, D), 0.0), axis=0).astype(jnp.bfloat16)
    x_attn = x_embed[pick_ids] + ATTN_GAIN * jnp.dot(o, attn_low[3], preferred_element_type=jnp.float32)
    return x_attn, (a_factor, a, a_rows, q_wide, k, v, probs, o, head_mask)


def rows_backward(attn_low, vector_w, x_embed, kept, dx_attn, pick_ids):
    a_factor, a, a_rows, q_wide, k, v, probs, o, head_mask = kept
    count = pick_ids.shape[0]
    dbranch = dx_attn.astype(jnp.bfloat16)
    dwout = ATTN_GAIN * jnp.dot(o.T, dbranch, preferred_element_type=jnp.float32)
    do = (ATTN_GAIN * jnp.dot(dbranch, attn_low[3].T, preferred_element_type=jnp.float32)).astype(jnp.bfloat16)
    do_wide = jnp.where(head_mask, do[None], 0).reshape(HEADS * count, D)
    dprobs = jnp.einsum("rd,td->rt", do_wide, v, preferred_element_type=jnp.float32)
    dscores = (probs * (dprobs - jnp.sum(probs * dprobs, axis=-1, keepdims=True))).astype(jnp.bfloat16)
    factor_qk = HEAD_DIM ** (-0.5)
    dq = jnp.dot(dscores, k, preferred_element_type=jnp.float32).reshape(HEADS, count, D)
    dq = (jnp.sum(jnp.where(head_mask, dq, 0.0), axis=0) * factor_qk).astype(jnp.bfloat16)
    dk = (jnp.dot(dscores.T, q_wide, preferred_element_type=jnp.float32) * factor_qk).astype(jnp.bfloat16)
    dv = jnp.dot(probs.astype(jnp.bfloat16).T, do_wide, preferred_element_type=jnp.float32).astype(jnp.bfloat16)
    dlayer = jnp.stack(
        [
            jnp.dot(a_rows.T, dq, preferred_element_type=jnp.float32),
            jnp.dot(a.T, dk, preferred_element_type=jnp.float32),
            jnp.dot(a.T, dv, preferred_element_type=jnp.float32),
            dwout,
        ]
    )
    places = jnp.arange(x_embed.shape[0])
    pick_mask = (places[:, None] == pick_ids[None, :]).astype(jnp.float32)
    dinput = jnp.dot(dk, attn_low[1].T, preferred_element_type=jnp.float32)
    dinput = dinput + jnp.dot(dv, attn_low[2].T, preferred_element_type=jnp.float32)
    dq_in = jnp.dot(dq, attn_low[0].T, preferred_element_type=jnp.float32)
    dinput = dinput + jnp.dot(pick_mask, dq_in, precision=HIGH)
    dx, gain_attn = norm_back(x_embed, a_factor, vector_w[0], dinput)
    return dx + jnp.dot(pick_mask, dx_attn, precision=HIGH), dlayer, gain_attn


def gather_rows(value, axis=0):
    return lax.all_gather(value, "fsdp", axis=axis, tiled=True)


def scatter_rows(value, axis=0):
    return lax.psum_scatter(
        value.astype(jnp.bfloat16), "fsdp", scatter_dimension=axis, tiled=True
    ).astype(jnp.float32)


TILE = 512
MESH = pl.DeviceIdType.MESH
F32 = jnp.float32
LOW = jnp.bfloat16
X_IN, B_ROWS, Y_PART, HEAD_ROWS, TOPS, D_ROWS, DY_ROWS, DB_PART = range(8)
ROWS_ONE, P_A, ROWS_TWO, DS_A, G_OUT, D_VEC, EXCHANGES = range(8, 15)


def dot_nn(left, right):
    return lax.dot_general(left, right, (((1,), (0,)), ((), ())), preferred_element_type=F32)


def dot_nt(left, right):
    return lax.dot_general(left, right, (((1,), (1,)), ((), ())), preferred_element_type=F32)


def dot_tn(left, right):
    return lax.dot_general(left, right, (((0,), (0,)), ((), ())), preferred_element_type=F32)


def lanes(shape):
    return lax.broadcasted_iota(jnp.int32, shape, len(shape) - 1)


def sublanes(shape):
    return lax.broadcasted_iota(jnp.int32, shape, len(shape) - 2)


def norm_factor(x):
    return lax.rsqrt(jnp.mean(x * x, axis=-1, keepdims=True) + EPSILON)


def norm_grad(x, factor, gain_row, upstream):
    normed = x * factor
    scaled = upstream * gain_row
    back = factor * (scaled - normed * jnp.mean(scaled * normed, axis=-1, keepdims=True))
    return back, jnp.sum(upstream * normed, axis=0, keepdims=True)


GELU_C = math.sqrt(2.0 / math.pi)


def gelu_of(u):
    return 0.5 * u * (1.0 + jnp.tanh(GELU_C * (u + 0.044715 * (u * u * u))))


def gelu_slope(u):
    t = jnp.tanh(GELU_C * (u + 0.044715 * (u * u * u)))
    return 0.5 * (1.0 + t) + 0.5 * u * (1.0 - t * t) * GELU_C * (1.0 + 3.0 * 0.044715 * u * u)


def rows_at_once(n, slots):
    return max(g for g in range(1, n + 1) if n % g == 0 and g * slots <= 512)


def step_kernel(
    dims,
    id_col, id_lane, slot_col, slot_lane, pick_col, pick_lane, seg_rows, seg_lane,
    route_col, route_all, target_lane, vec, eb, attn, expw,
    dembed_out, dattn_out, dexp_out, dvec_out, loss_out,
    xs, xr, gr, ball, ys, yr, rows, tops, drs, drr, dyall, dbs, dbr,
    one, pas, par, two, dss, dsr, dvec, logit_s, dlog_s, pre_s, hid_s, dpre_s, flip_s, tile_s,
    send, recv, out_sem,
):
    n, slots, vocab, vocab_rows, hidden = dims
    row_count = pick_col.shape[0]
    tokens = slot_col.shape[0]
    all_rows = n * row_count
    wide = HEADS * row_count
    shard = D // n
    row_total = float(all_rows)
    scale = 2.0 * D ** (-0.5)
    factor_qk = HEAD_DIM ** (-0.5)
    me = lax.axis_index("fsdp")

    def others(body):
        def one_step(k, carry):
            body(k, lax.rem(me + k, n))
            return carry

        lax.fori_loop(1, n, one_step, 0)

    def link(which, k, source, target, peer, origin):
        return pltpu.make_async_remote_copy(
            src_ref=source,
            dst_ref=target,
            send_sem=send.at[which, k],
            recv_sem=recv.at[which, origin],
            device_id={"fsdp": peer},
            device_id_type=MESH,
        )

    def spread(which, buffer):
        others(lambda k, peer: link(which, k, buffer.at[me], buffer.at[me], peer, me).start())

    def deal(which, source, target):
        others(lambda k, peer: link(which, k, source.at[peer], target.at[me], peer, me).start())

    def arrive(which, target):
        others(
            lambda k, peer: link(which, k, target.at[peer], target.at[peer], peer, peer).wait_recv()
        )

    def sent(which, source):
        others(lambda k, peer: link(which, k, source.at[peer], source.at[peer], peer, me).wait_send())

    def tiled(body, carry):
        whole = vocab_rows // TILE
        carry = lax.fori_loop(
            0, whole, lambda i, c: body(i, pl.multiple_of(i * TILE, TILE), TILE, c), carry
        )
        if vocab_rows % TILE:
            carry = body(whole, whole * TILE, vocab_rows % TILE, carry)
        return carry

    def added(buffer):
        total = buffer[0].astype(F32)
        for j in range(1, n):
            total = total + buffer[j].astype(F32)
        return total

    barrier = pltpu.get_barrier_semaphore()
    others(
        lambda k, peer: pl.semaphore_signal(
            barrier, inc=1, device_id={"fsdp": peer}, device_id_type=MESH
        )
    )
    pl.semaphore_wait(barrier, n - 1)

    group = rows_at_once(n, slots)
    chunk = group * slots

    def look(c, carry):
        ids = id_col[pl.ds(pl.multiple_of(c * chunk, chunk), chunk), :]

        def add(i, start, size, acc):
            hit = (lanes((chunk, size)) + start == ids).astype(F32).astype(LOW)
            return acc + dot_nn(hit, eb[pl.ds(start, size), :])

        found = tiled(add, jnp.zeros((chunk, D), F32))
        xs[pl.ds(c * group, group)] = found.astype(LOW).reshape(group, slots, D)
        return carry

    lax.fori_loop(0, n // group, look, 0)
    deal(X_IN, xs, xr)
    xr[me] = xs[me]
    arrive(X_IN, xr)
    x = jnp.zeros((tokens, D), F32)
    for c in range(n // group):
        hit = (lanes((tokens, chunk)) + c * chunk == slot_col[...]).astype(F32).astype(LOW)
        x = x + dot_nn(hit, xr[c * group : (c + 1) * group].reshape(chunk, D))

    gain_a, gain_b, gain_c, gain_d = (vec[i : i + 1, :] for i in range(4))
    x_factor = norm_factor(x)
    a = (x * x_factor * gain_a).astype(LOW)
    pick = (lanes((row_count, tokens)) == pick_col[...]).astype(F32).astype(LOW)
    x_rows = dot_nn(pick, x.astype(LOW))
    a_rows = dot_nn(pick, a).astype(LOW)
    q = dot_nn(a_rows, attn[0]).astype(LOW)
    k = dot_nn(a, attn[1]).astype(LOW)
    v = dot_nn(a, attn[2]).astype(LOW)
    head_mask = (
        lax.shift_right_logical(lanes((HEADS, row_count, D)), HEAD_DIM.bit_length() - 1)
        == lax.broadcasted_iota(jnp.int32, (HEADS, row_count, D), 0)
    )

    def widen(low_rows):
        return (
            jnp.where(head_mask, low_rows.astype(F32)[None], 0.0).reshape(wide, D).astype(LOW)
        )

    def narrow(values):
        return jnp.sum(jnp.where(head_mask, values.reshape(HEADS, row_count, D), 0.0), axis=0)

    q_wide = widen(q)
    scores = dot_nt(q_wide, k) * factor_qk
    allowed = (lanes((row_count, tokens)) <= pick_col[...]) & (seg_lane[...] == seg_rows[...])
    scores = jnp.where(
        allowed[None], scores.reshape(HEADS, row_count, tokens), -1e30
    ).reshape(wide, tokens)
    exponent = jnp.exp(scores - jnp.max(scores, axis=-1, keepdims=True))
    probs = exponent / jnp.sum(exponent, axis=-1, keepdims=True)
    probs_low = probs.astype(LOW)
    o = narrow(dot_nn(probs_low, v)).astype(LOW)
    x_attn = x_rows + ATTN_GAIN * dot_nn(o, attn[3])

    b_factor = norm_factor(x_attn)
    b = x_attn * b_factor * gain_b
    ball[me] = b.astype(LOW)
    spread(B_ROWS, ball)
    router_rows = [vec[4 + e : 5 + e, :] for e in range(EXPERTS)]
    router_logits = [jnp.sum(b * row, axis=-1, keepdims=True) for row in router_rows]
    highest = router_logits[0]
    for value in router_logits[1:]:
        highest = jnp.maximum(highest, value)
    router_exp = [jnp.exp(value - highest) for value in router_logits]
    router_sum = sum(router_exp[1:], router_exp[0])
    router_probs = [value / router_sum for value in router_exp]
    chosen = [(route_col[...] == e).astype(F32) for e in range(EXPERTS)]
    gate = sum([p * c for p, c in zip(router_probs[1:], chosen[1:])], router_probs[0] * chosen[0])
    one[me, 0] = a_rows
    one[me, 1] = o
    one[me, 2] = q
    a_turned = a.astype(F32).T.astype(LOW)
    pas[...] = dot_nt(a_turned, probs_low).reshape(n, shard, wide).astype(LOW)
    arrive(B_ROWS, ball)
    b_all = ball[...].reshape(all_rows, D)
    y_part = jnp.zeros((all_rows, D), F32)
    for e in range(EXPERTS):
        pre = dot_nn(b_all, expw[e, 0])
        pre_s[e] = pre
        hid = jnp.where(route_all[...] == e, gelu_of(pre), 0.0).astype(LOW)
        hid_s[e] = hid
        y_part = y_part + dot_nt(hid, expw[e, 1])
    ys[...] = y_part.astype(LOW).reshape(n, row_count, D)
    deal(Y_PART, ys, yr)
    yr[me] = ys[me]
    arrive(Y_PART, yr)
    y = added(yr)
    z = x_attn + gate * y

    z_factor = norm_factor(z)
    first = (z * z_factor * gain_c).astype(LOW)
    middle = dot_nn(first, attn[4])
    middle_factor = norm_factor(middle)
    rows[me, 0] = first
    rows[me, 1] = (middle * middle_factor * gain_d).astype(LOW)
    spread(HEAD_ROWS, rows)
    spread(ROWS_ONE, one)
    deal(P_A, pas, par)
    par[me] = pas[me]
    arrive(HEAD_ROWS, rows)
    loss_rows = 2 * all_rows
    head_rows = rows[...].reshape(loss_rows, D)

    def target_hit(start, size):
        return sublanes((size, loss_rows)) + start == target_lane[...]

    def logits_tile(i, start, size, carry):
        top, total, at_target = carry
        value = dot_nt(eb[pl.ds(start, size), :], head_rows) * scale
        if vocab_rows != vocab:
            value = jnp.where(sublanes((size, loss_rows)) + start < vocab, value, -1e30)
        logit_s[pl.ds(start, size), :] = value
        hit = target_hit(start, size)
        at_target = at_target + jnp.sum(jnp.where(hit, value, 0.0), axis=0, keepdims=True)
        new_top = jnp.maximum(top, jnp.max(value, axis=0, keepdims=True))
        total = total * jnp.exp(top - new_top) + jnp.sum(
            jnp.exp(value - new_top), axis=0, keepdims=True
        )
        return new_top, total, at_target

    nothing = jnp.zeros((1, loss_rows), F32)
    top, total, at_target = tiled(logits_tile, (nothing - 1e30, nothing, nothing))
    place = sublanes((8, loss_rows))
    tops[me] = jnp.where(
        place == 0, top, jnp.where(place == 1, total, jnp.where(place == 2, at_target, 0.0))
    )
    spread(TOPS, tops)
    arrive(TOPS, tops)
    top = tops[0, 0:1]
    for j in range(1, n):
        top = jnp.maximum(top, tops[j, 0:1])
    total, at_target = nothing, nothing
    for j in range(n):
        total = total + tops[j, 1:2] * jnp.exp(tops[j, 0:1] - top)
        at_target = at_target + tops[j, 2:3]
    logsum = top + jnp.log(total)
    is_first = lax.rem(lanes((1, loss_rows)), 2 * row_count) < row_count
    weight = jnp.where(is_first, 1.0, SECOND_WEIGHT) / row_total
    loss = jnp.sum(weight * (logsum - at_target), axis=-1, keepdims=True)
    loss_out[...] = jnp.broadcast_to(loss, loss_out.shape)

    def dlogits_tile(i, start, size, acc):
        soft = jnp.exp(logit_s[pl.ds(start, size), :] - logsum)
        low = ((soft - target_hit(start, size).astype(F32)) * weight).astype(LOW)
        dlog_s[pl.ds(start, size), :] = low
        return acc + dot_tn(low, eb[pl.ds(start, size), :])

    drows = tiled(dlogits_tile, jnp.zeros((loss_rows, D), F32)) * scale
    drs[...] = drows.astype(LOW).reshape(n, 2 * row_count, D)
    deal(D_ROWS, drs, drr)
    drr[me] = drs[me]
    arrive(D_ROWS, drr)
    drow = added(drr)
    dmiddle, gain_mtp = norm_grad(middle, middle_factor, gain_d, drow[row_count:])
    dmiddle_low = dmiddle.astype(LOW)
    dfirst = drow[:row_count] + dot_nt(dmiddle_low, attn[4])
    dz, gain_final = norm_grad(z, z_factor, gain_c, dfirst)

    dgate = jnp.sum(dz * y, axis=-1, keepdims=True)
    dyall[me] = (gate * dz).astype(LOW)
    spread(DY_ROWS, dyall)
    arrive(DY_ROWS, dyall)
    dy_all = dyall[...].reshape(all_rows, D)
    db_part = jnp.zeros((all_rows, D), F32)
    for e in range(EXPERTS):
        dhid = dot_nn(dy_all, expw[e, 1])
        slope = jnp.where(route_all[...] == e, gelu_slope(pre_s[e]), 0.0)
        dpre = (slope * dhid).astype(LOW)
        dpre_s[e] = dpre
        db_part = db_part + dot_nt(dpre, expw[e, 0])
    dbs[...] = db_part.astype(LOW).reshape(n, row_count, D)
    deal(DB_PART, dbs, dbr)
    dbr[me] = dbs[me]
    squares = jnp.zeros((1, D), F32)

    def squared(values):
        return jnp.sum(values * values, axis=0, keepdims=True)

    hidden_squares = jnp.zeros((1, hidden), F32)
    for e in range(EXPERTS):
        up = dot_tn(b_all, dpre_s[e])
        down = dot_tn(dy_all, hid_s[e])
        dexp_out[e, 0] = up
        dexp_out[e, 1] = down
        hidden_squares = hidden_squares + squared(up) + squared(down)
    arrive(DB_PART, dbr)
    prob_grads = [c * dgate for c in chosen]
    mixed = sum([p * g for p, g in zip(router_probs[1:], prob_grads[1:])], router_probs[0] * prob_grads[0])
    dlogits = [p * (g - mixed) for p, g in zip(router_probs, prob_grads)]
    drouter = [jnp.sum(g * b, axis=0, keepdims=True) for g in dlogits]
    dnormed = added(dbr)
    for g, row in zip(dlogits, router_rows):
        dnormed = dnormed + g * row
    dx_part, gain_ffn = norm_grad(x_attn, b_factor, gain_b, dnormed)
    dx_attn = dz + dx_part

    dbranch = dx_attn.astype(LOW)
    do = (ATTN_GAIN * dot_nt(dbranch, attn[3])).astype(LOW)
    do_wide = widen(do)
    dprobs = dot_nt(do_wide, v)
    dscores = (probs * (dprobs - jnp.sum(probs * dprobs, axis=-1, keepdims=True))).astype(LOW)
    dq = (narrow(dot_nn(dscores, k)) * factor_qk).astype(LOW)
    two[me, 0] = do
    two[me, 1] = dq
    two[me, 2] = dbranch
    two[me, 3] = dmiddle_low
    dk = (dot_tn(dscores, q_wide) * factor_qk).astype(LOW)
    dv = dot_tn(probs_low, do_wide).astype(LOW)
    dinput = dot_nt(dk, attn[1]) + dot_nt(dv, attn[2])
    dx, gain_attn = norm_grad(x, x_factor, gain_a, dinput)
    row_back, gain_more = norm_grad(x_rows, norm_factor(x_rows), gain_a, dot_nt(dq, attn[0]))
    spots = (sublanes((tokens, row_count)) == pick_lane[...]).astype(F32)
    dx = dx + lax.dot_general(
        spots, row_back + dx_attn, (((1,), (0,)), ((), ())), precision=HIGH,
        preferred_element_type=F32,
    )
    dx_low = dx.astype(LOW)
    sent(X_IN, xs)
    for c in range(n // group):
        hit = (sublanes((chunk, tokens)) + c * chunk == slot_lane[...]).astype(F32).astype(LOW)
        xs[c * group : (c + 1) * group] = dot_nn(hit, dx_low).astype(LOW).reshape(group, slots, D)
    deal(G_OUT, xs, gr)
    gr[me] = xs[me]
    spread(ROWS_TWO, two)
    dss[...] = dot_nt(a_turned, dscores).reshape(n, shard, wide).astype(LOW)
    deal(DS_A, dss, dsr)
    dsr[me] = dss[me]

    arrive(ROWS_ONE, one)
    arrive(P_A, par)
    arrive(ROWS_TWO, two)
    arrive(DS_A, dsr)
    mine = pl.ds(pl.multiple_of(me * shard, 8), shard)

    def own_rows(left, right):
        flip_s[...] = left.astype(F32).reshape(all_rows, D).T
        return dot_nn(flip_s[mine, :].astype(LOW), right.reshape(all_rows, D))

    dkey = jnp.zeros((shard, D), F32)
    dvalue = jnp.zeros((shard, D), F32)
    for j in range(n):
        dkey = dkey + dot_nn(dsr[j], widen(one[j, 2]))
        dvalue = dvalue + dot_nn(par[j], widen(two[j, 0]))
    parts = (
        own_rows(one[:, 0], two[:, 1]),
        dkey * factor_qk,
        dvalue,
        ATTN_GAIN * own_rows(one[:, 1], two[:, 2]),
        own_rows(rows[:, 0], two[:, 3]),
    )
    for i, part in enumerate(parts):
        dattn_out[i] = part
        squares = squares + squared(part)

    arrive(G_OUT, gr)
    whole = vocab_rows // TILE

    def leave(i, start, size):
        slot = lax.rem(i, 2)
        return pltpu.make_async_copy(
            tile_s.at[slot, pl.ds(0, size)], dembed_out.at[pl.ds(start, size)], out_sem.at[slot]
        )

    def dembed_tile(i, start, size, acc):
        value = scale * dot_nn(dlog_s[pl.ds(start, size), :], head_rows)
        for c in range(n // group):
            ids = id_lane[:, c * chunk : (c + 1) * chunk]
            hit = (sublanes((size, chunk)) + start == ids).astype(F32).astype(LOW)
            value = value + dot_nn(hit, gr[c * group : (c + 1) * group].reshape(chunk, D))

        def free():
            leave(i - 2, start - 2 * TILE, TILE).wait()

        if isinstance(i, int):
            if i >= 2:
                free()
        else:
            pl.when(i >= 2)(free)
        tile_s[lax.rem(i, 2), pl.ds(0, size)] = value
        leave(i, start, size).start()
        return acc + squared(value)

    squares = tiled(dembed_tile, squares)
    tiles = [(i, i * TILE, TILE) for i in range(whole)]
    if vocab_rows % TILE:
        tiles.append((whole, whole * TILE, vocab_rows % TILE))
    total_squares = jnp.sum(squares, axis=-1, keepdims=True) + jnp.sum(
        hidden_squares, axis=-1, keepdims=True
    )
    line = sublanes((8, D))
    share = jnp.broadcast_to(total_squares, (8, D))
    for i, value in enumerate([gain_attn + gain_more, gain_ffn, gain_final, gain_mtp] + drouter):
        share = jnp.where(line == i, value, share)
    dvec[me] = share
    spread(D_VEC, dvec)
    arrive(D_VEC, dvec)
    dvec_out[...] = added(dvec)
    for i, start, size in tiles[-2:]:
        leave(i, start, size).wait()
    for which, source in (
        (B_ROWS, ball), (Y_PART, ys), (HEAD_ROWS, rows), (TOPS, tops), (D_ROWS, drs),
        (DY_ROWS, dyall), (DB_PART, dbs), (ROWS_ONE, one), (P_A, pas), (ROWS_TWO, two),
        (DS_A, dss), (G_OUT, xs), (D_VEC, dvec),
    ):
        sent(which, source)


def run_step(n, slots, vocab, number, ints, vec, embed_low, attn_low, expert_low):
    vocab_rows = -(-vocab // 16) * 16
    if vocab_rows != vocab:
        embed_low = jnp.pad(embed_low, ((0, vocab_rows - vocab), (0, 0)))
    row_count = ints["pick_col"].shape[0]
    hidden = expert_low.shape[3]
    shard = D // n
    all_rows = n * row_count
    wide = HEADS * row_count
    vmem = pl.BlockSpec(memory_space=pltpu.VMEM)
    low = lambda *shape: pltpu.VMEM(shape, LOW)
    wide_float = lambda *shape: pltpu.VMEM(shape, F32)
    names = (
        "id_col", "id_lane", "slot_col", "slot_lane", "pick_col", "pick_lane", "seg_rows",
        "seg_lane", "route_col", "route_all", "target_lane",
    )
    outs = pl.pallas_call(
        functools.partial(step_kernel, (n, slots, vocab, vocab_rows, hidden)),
        out_shape=(
            jax.ShapeDtypeStruct((vocab_rows, D), F32),
            jax.ShapeDtypeStruct((5, shard, D), F32),
            jax.ShapeDtypeStruct((EXPERTS, 2, D, hidden), F32),
            jax.ShapeDtypeStruct((8, D), F32),
            jax.ShapeDtypeStruct((8, 128), F32),
        ),
        in_specs=[vmem] * 15,
        out_specs=(pl.BlockSpec(memory_space=pl.ANY), vmem, vmem, vmem, vmem),
        scratch_shapes=[
            low(n, slots, D), low(n, slots, D), low(n, slots, D),
            low(n, row_count, D), low(n, row_count, D), low(n, row_count, D),
            low(n, 2, row_count, D), wide_float(n, 8, 2 * all_rows),
            low(n, 2 * row_count, D), low(n, 2 * row_count, D),
            low(n, row_count, D), low(n, row_count, D), low(n, row_count, D),
            low(n, 3, row_count, D), low(n, shard, wide), low(n, shard, wide),
            low(n, 4, row_count, D), low(n, shard, wide), low(n, shard, wide),
            wide_float(n, 8, D),
            wide_float(vocab_rows, 2 * all_rows), low(vocab_rows, 2 * all_rows),
            wide_float(EXPERTS, all_rows, hidden), low(EXPERTS, all_rows, hidden),
            low(EXPERTS, all_rows, hidden), wide_float(D, all_rows), wide_float(2, TILE, D),
            pltpu.SemaphoreType.DMA((EXCHANGES, n)),
            pltpu.SemaphoreType.DMA((EXCHANGES, n)),
            pltpu.SemaphoreType.DMA((2,)),
        ],
        compiler_params=pltpu.CompilerParams(
            collective_id=number, has_side_effects=True, vmem_limit_bytes=60 * 1024 * 1024
        ),
        name="inner_step",
    )(*[ints[name] for name in names], vec, embed_low, attn_low, expert_low)
    return (outs[0][:vocab],) + outs[1:]


def prepare(n, slots, vocab, tokens, routes, segments, loss_pos):
    steps, count = tokens.shape
    start = lax.axis_index("fsdp") * vocab
    row_count = loss_pos.shape[1]
    owner = tokens // vocab
    places = jnp.arange(count)
    earlier = places[None, None, :] < places[None, :, None]
    same = tokens[:, :, None] == tokens[:, None, :]
    first = jnp.logical_not(jnp.any(same & earlier, axis=2))
    same_owner = owner[:, :, None] == owner[:, None, :]
    rank = jnp.sum((same_owner & earlier & first[:, None, :]).astype(jnp.int32), axis=2)
    own_slot = owner * slots + rank
    slot = jnp.sum(jnp.where(same & first[:, None, :], own_slot[:, None, :], 0), axis=2)
    at_slot = (own_slot[:, :, None] == jnp.arange(n * slots)[None, None, :]) & first[:, :, None]
    ids = jnp.sum(jnp.where(at_slot, tokens[:, :, None] + 1, 0), axis=1) - 1
    picked = loss_pos[:, :, None] == places[None, None, :]
    shifted = lambda by: jnp.sum(
        jnp.where(loss_pos[:, :, None] + by == places[None, None, :], tokens[:, None, :], 0), axis=2
    )
    row_routes = jnp.sum(jnp.where(picked, routes[:, None, :], 0), axis=2)
    row_segs = jnp.sum(jnp.where(picked, segments[:, None, :], 0), axis=2)
    most = jnp.broadcast_to(jnp.max(jnp.where(first, rank, 0)), (steps, 1))
    packed = jnp.concatenate([ids, row_routes, shifted(1), shifted(2), most], axis=1)
    world = lax.all_gather(packed, ("grp", "fsdp"))
    fits = jnp.max(world[:, 0, -1]) < slots
    everyone = lax.dynamic_slice_in_dim(world, lax.axis_index("grp") * n, n, axis=0)[:, :, :-1]
    wanted = lax.dynamic_slice_in_dim(everyone, lax.axis_index("fsdp") * slots, slots, axis=2) - start
    after = n * slots
    result = []
    for s in range(steps):
        want = wanted[:, s].reshape(n * slots)
        targets = everyone[:, s, after + row_count :].reshape(1, n * 2 * row_count) - start
        result.append(
            dict(
                id_col=want[:, None],
                id_lane=want[None, :],
                slot_col=slot[s][:, None],
                slot_lane=slot[s][None, :],
                pick_col=loss_pos[s][:, None],
                pick_lane=loss_pos[s][None, :],
                seg_rows=row_segs[s][:, None],
                seg_lane=segments[s][None, :],
                route_col=row_routes[s][:, None],
                route_all=everyone[:, s, after : after + row_count].reshape(n * row_count, 1),
                target_lane=targets,
            )
        )
    return result, fits


def general_step(tokens, routes, segments, loss_pos, all_ids, inner_step, weights):
    embed_w, attn_w, expert_w, vector_w = weights
    vocab_shard = embed_w.shape[0]
    vocab_start = lax.axis_index("fsdp") * vocab_shard
    row_total = lax.axis_size("fsdp") * loss_pos.shape[2]
    logit_scale = 2.0 * D ** (-0.5)
    vocab_places = jnp.arange(vocab_shard)
    head_weights = jnp.array([1.0, SECOND_WEIGHT], jnp.float32)
    embed_low = embed_w.astype(jnp.bfloat16)
    attn_low = lax.all_gather(attn_w.astype(jnp.bfloat16), "fsdp", axis=1, tiled=True)
    expert_low = expert_w.astype(jnp.bfloat16)
    ids_group = all_ids[inner_step]
    ids_local = tokens[inner_step, 0]
    seg_ids = segments[inner_step, 0]
    route_ids = routes[inner_step, 0, :, 0]
    pick_ids = loss_pos[inner_step, 0]
    chosen = ids_group - vocab_start
    inside = (chosen >= 0) & (chosen < vocab_shard)
    looked = jnp.take(embed_low, jnp.clip(chosen, 0, vocab_shard - 1), axis=0).astype(
        jnp.float32
    )
    x_embed = lax.psum_scatter(
        jnp.where(inside[:, None], looked, 0.0).astype(jnp.bfloat16),
        "fsdp",
        scatter_dimension=0,
        tiled=True,
    ).astype(jnp.float32)
    x_attn, kept = rows_forward(attn_low, vector_w, x_embed, seg_ids, pick_ids)
    b, b_factor = norm_apply(x_attn, vector_w[1])
    router_probs = jax.nn.softmax(jnp.dot(b, vector_w[4:].T, precision=HIGH), axis=-1)
    row_routes = route_ids[pick_ids]
    onehot = (row_routes[:, None] == jnp.arange(EXPERTS)[None, :]).astype(jnp.float32)
    gating = jnp.sum(router_probs * onehot, axis=1)
    b_all = gather_rows(b.astype(jnp.bfloat16))
    routes_all = gather_rows(row_routes)
    route_mask = routes_all[None, :, None] == jnp.arange(EXPERTS)[:, None, None]
    hidden_pre = jnp.einsum("cd,edf->ecf", b_all, expert_low[:, 0], preferred_element_type=jnp.float32)
    hidden_act = jnp.where(route_mask, smooth_act(hidden_pre), 0.0).astype(jnp.bfloat16)
    y_part = jnp.einsum("ecf,edf->cd", hidden_act, expert_low[:, 1], preferred_element_type=jnp.float32)
    returned = scatter_rows(y_part)
    z_rows = x_attn + gating[:, None] * returned
    first_float, first_factor = norm_apply(z_rows, vector_w[2])
    first_rows = first_float.astype(jnp.bfloat16)
    middle = jnp.dot(first_rows, attn_low[4], preferred_element_type=jnp.float32)
    second_float, second_factor = norm_apply(middle, vector_w[3])
    targets = jnp.stack([ids_local[pick_ids + 1], ids_local[pick_ids + 2]])
    rows_all, targets_all = (
        lax.all_gather(
            jnp.stack([first_rows, second_float.astype(jnp.bfloat16)]),
            "fsdp",
            axis=1,
            tiled=True,
        ),
        lax.all_gather(targets, "fsdp", axis=1, tiled=True),
    )
    logits = (
        jnp.einsum("jrd,vd->jrv", rows_all, embed_low, preferred_element_type=jnp.float32)
        * logit_scale
    )
    relative = targets_all - vocab_start
    onehot_target = (vocab_places[None, None, :] == relative[:, :, None]).astype(jnp.float32)
    target_part = jnp.sum(onehot_target * logits, axis=-1)
    local_top = jnp.max(logits, axis=-1)
    local_sum = jnp.sum(jnp.exp(logits - local_top[:, :, None]), axis=-1)
    parts = lax.all_gather(jnp.stack([local_top, local_sum, target_part]), "fsdp")
    row_top = jnp.max(parts[:, 0], axis=0)
    sum_exp = jnp.sum(parts[:, 1] * jnp.exp(parts[:, 0] - row_top), axis=0)
    target_logit = jnp.sum(parts[:, 2], axis=0)
    logsum = row_top + jnp.log(sum_exp)
    loss = (jnp.sum(head_weights[:, None] * (logsum - target_logit)) / row_total)
    dlogits = (
        (jnp.exp(logits - logsum[:, :, None]) - onehot_target)
        * (head_weights / row_total)[:, None, None]
    ).astype(jnp.bfloat16)
    dembed = (
        jnp.einsum("jrv,jrd->vd", dlogits, rows_all, preferred_element_type=jnp.float32)
        * logit_scale
    )
    drows = (
        jnp.einsum("jrv,vd->jrd", dlogits, embed_low, preferred_element_type=jnp.float32)
        * logit_scale
    )
    drows_own = lax.psum_scatter(
        drows.astype(jnp.bfloat16), "fsdp", scatter_dimension=1, tiled=True
    ).astype(jnp.float32)
    dmiddle, gain_mtp = norm_back(middle, second_factor, vector_w[3], drows_own[1])
    dmiddle_low = dmiddle.astype(jnp.bfloat16)
    dsecond_proj = jnp.dot(first_rows.T, dmiddle_low, preferred_element_type=jnp.float32)
    dfirst = drows_own[0] + jnp.dot(
        dmiddle_low, attn_low[4].T, preferred_element_type=jnp.float32
    )
    dz_rows, gain_final = norm_back(z_rows, first_factor, vector_w[2], dfirst)
    dgating = jnp.sum(dz_rows * returned, axis=1)
    dy_all = gather_rows((gating[:, None] * dz_rows).astype(jnp.bfloat16))
    dy_masked = jnp.where(route_mask, dy_all[None], 0)
    down_grad = jnp.einsum("ecf,ecd->edf", hidden_act, dy_masked, preferred_element_type=jnp.float32)
    dhidden = jnp.einsum("ecd,edf->ecf", dy_masked, expert_low[:, 1], preferred_element_type=jnp.float32)
    unused, act_back = jax.vjp(smooth_act, hidden_pre)
    dhidden_pre = act_back(dhidden)[0].astype(jnp.bfloat16)
    up_grad = jnp.einsum("cd,ecf->edf", b_all, dhidden_pre, preferred_element_type=jnp.float32)
    dexpert = jnp.stack([up_grad, down_grad], axis=1)
    db_part = jnp.einsum("ecf,edf->cd", dhidden_pre, expert_low[:, 0], preferred_element_type=jnp.float32)
    dnormed = scatter_rows(db_part)
    prob_grad = onehot * dgating[:, None]
    dlogit = router_probs * (prob_grad - jnp.sum(router_probs * prob_grad, axis=1, keepdims=True))
    drouter = jnp.dot(dlogit.T, b, precision=HIGH)
    dnormed = dnormed + jnp.dot(dlogit, vector_w[4:], precision=HIGH)
    dx_part, gain_ffn = norm_back(x_attn, b_factor, vector_w[1], dnormed)
    dx_embed, dlayer, gain_attn = rows_backward(
        attn_low, vector_w, x_embed, kept, dz_rows + dx_part, pick_ids
    )
    dattn = scatter_rows(jnp.concatenate([dlayer, dsecond_proj[None]], axis=0), axis=1)
    gather_chosen = ids_group - vocab_start
    gather_inside = (gather_chosen >= 0) & (gather_chosen < vocab_shard)
    seg_index = jnp.where(gather_inside, gather_chosen, vocab_shard)
    added = jax.ops.segment_sum(
        lax.all_gather(dx_embed.astype(jnp.bfloat16), "fsdp", axis=0, tiled=True).astype(
            jnp.float32
        ),
        seg_index,
        num_segments=vocab_shard + 1,
    )
    dembed = dembed + added[:vocab_shard]
    dvector_part = jnp.concatenate(
        [jnp.stack([gain_attn, gain_ffn, gain_final, gain_mtp]), drouter], axis=0
    )
    squares = jnp.sum(dembed * dembed) + jnp.sum(dattn * dattn) + jnp.sum(dexpert * dexpert)
    dvector, squares_all = lax.psum((dvector_part, squares), "fsdp")
    return dembed, dattn, dexpert, dvector, squares_all, loss


def adam_update(weight, first_moment, second, gradient, step_float, rate_here, decay_here):
    first_new = BETA_ONE * first_moment + (1.0 - BETA_ONE) * gradient
    second_new = BETA_TWO * second + (1.0 - BETA_TWO) * gradient * gradient
    first_hat = first_new / (1.0 - BETA_ONE**step_float)
    second_hat = second_new / (1.0 - BETA_TWO**step_float)
    weight_new = weight - rate_here * (
        first_hat / (jnp.sqrt(second_hat) + ADAM_EPS) + decay_here * weight
    )
    return (weight_new, first_new, second_new)


def window(
    step,
    embedding,
    embedding_first,
    embedding_second,
    embedding_outer,
    attention,
    attention_first,
    attention_second,
    attention_outer,
    experts,
    experts_first,
    experts_second,
    experts_outer,
    vectors,
    vectors_first,
    vectors_second,
    vectors_outer,
    inner_count,
    row_total,
):
    group_count = lax.axis_size("grp")
    threshold = 0.05 / math.sqrt(row_total)
    vector_rates = jnp.where(jnp.arange(vectors.shape[0])[:, None] < 4, LR_GAIN, LR_ROUTER)
    rate_list = (LR_EMBED, LR_MATRIX, LR_MATRIX, vector_rates)
    decay_list = (DECAY, DECAY, DECAY, 0.0)
    weights_now = (embedding, attention, experts, vectors)
    first_now = (embedding_first[0], attention_first[0], experts_first[0], vectors_first[0])
    second_now = (embedding_second[0], attention_second[0], experts_second[0], vectors_second[0])
    loss_list = []
    norm_list = []
    for inner_step in range(inner_count):
        dembed, dattn, dexpert, dvector, squares_all, loss = step(inner_step, weights_now)
        loss_list.append(loss)
        norm_value = jnp.sqrt(squares_all + jnp.sum(dvector * dvector))
        norm_list.append(norm_value)
        factor = jnp.minimum(1.0, threshold / norm_value)
        gradients = (dembed * factor, dattn * factor, dexpert * factor, dvector * factor)
        step_float = float(STEP0 + inner_step + 1)
        results = [
            adam_update(
                weights_now[k],
                first_now[k],
                second_now[k],
                gradients[k],
                step_float,
                rate_list[k],
                decay_list[k],
            )
            for k in range(4)
        ]
        weights_now = tuple((element[0] for element in results))
        first_now = tuple((element[1] for element in results))
        second_now = tuple((element[2] for element in results))
    masters = (embedding, attention, experts, vectors)
    outers = (embedding_outer, attention_outer, experts_outer, vectors_outer)
    deltas = tuple((master - current for master, current in zip(masters, weights_now)))
    summed = jax.tree.map(
        lambda part: part.astype(jnp.float32), lax.psum(for_sending(deltas), "grp")
    )
    new_outer = []
    new_master = []
    for k in range(4):
        delta_mean = summed[k] / group_count
        outer_new = OUTER_MOMENTUM * outers[k] + delta_mean
        new_outer.append(outer_new)
        new_master.append(masters[k] - OUTER_RATE * (delta_mean + OUTER_MOMENTUM * outer_new))
    return (
        jnp.stack(loss_list)[None],
        jnp.stack(norm_list)[None],
        first_now[0][None],
        second_now[0][None],
        new_master[0],
        new_outer[0],
        new_master[0].astype(jnp.bfloat16),
        first_now[1][None],
        second_now[1][None],
        new_master[1],
        new_outer[1],
        new_master[1].astype(jnp.bfloat16),
        first_now[2][None],
        second_now[2][None],
        new_master[2],
        new_outer[2],
        new_master[2].astype(jnp.bfloat16),
        gradients[3][None],
        first_now[3][None],
        second_now[3][None],
        new_master[3],
        new_outer[3],
    )


def shards(
    tokens,
    routes,
    segments,
    loss_pos,
    embedding,
    embedding_first,
    embedding_second,
    embedding_outer,
    attention,
    attention_first,
    attention_second,
    attention_outer,
    experts,
    experts_first,
    experts_second,
    experts_outer,
    vectors,
    vectors_first,
    vectors_second,
    vectors_outer,
):
    inner_count = tokens.shape[0]
    vocab_shard = embedding.shape[0]
    n = lax.axis_size("fsdp")
    row_total = n * loss_pos.shape[2]
    slots = 48
    steps, fits = prepare(
        n, slots, vocab_shard, tokens[:, 0], routes[:, 0, :, 0], segments[:, 0], loss_pos[:, 0]
    )
    attn_start = lax.all_gather(attention.astype(jnp.bfloat16), "fsdp", axis=1, tiled=True)
    state = (
        embedding,
        embedding_first,
        embedding_second,
        embedding_outer,
        attention,
        attention_first,
        attention_second,
        attention_outer,
        experts,
        experts_first,
        experts_second,
        experts_outer,
        vectors,
        vectors_first,
        vectors_second,
        vectors_outer,
    )

    def quick(*state):
        def step(inner_step, weights):
            embed_w, attn_w, expert_w, vector_w = weights
            if inner_step == 0:
                attn_low = attn_start
            else:
                attn_low = lax.all_gather(attn_w.astype(jnp.bfloat16), "fsdp", axis=1, tiled=True)
            dembed, dattn, dexpert, dvector_all, loss = run_step(
                n, slots, vocab_shard, 1, steps[inner_step], vector_w,
                embed_w.astype(jnp.bfloat16), attn_low, expert_w.astype(jnp.bfloat16),
            )
            return dembed, dattn, dexpert, dvector_all[:6], dvector_all[6, 0], loss[0, 0]

        return window(step, *state, inner_count, row_total)

    def general(*state):
        all_ids = lax.all_gather(tokens[:, 0, :], "fsdp", axis=1, tiled=True)
        step = functools.partial(general_step, tokens, routes, segments, loss_pos, all_ids)
        return window(step, *state, inner_count, row_total)

    return lax.cond(fits, quick, general, *state)


def solution(mesh):
    return jax.shard_map(
        shards,
        mesh=mesh,
        in_specs=(
            P(None, "grp", "fsdp"),
            P(None, "grp", "fsdp", None),
            P(None, "grp", "fsdp"),
            P(None, "grp", "fsdp"),
            P("fsdp", None),
            P("grp", "fsdp", None),
            P("grp", "fsdp", None),
            P("fsdp", None),
            P(None, "fsdp", None),
            P("grp", None, "fsdp", None),
            P("grp", None, "fsdp", None),
            P(None, "fsdp", None),
            P(None, None, None, "fsdp"),
            P("grp", None, None, None, "fsdp"),
            P("grp", None, None, None, "fsdp"),
            P(None, None, None, "fsdp"),
            P(),
            P("grp", None, None),
            P("grp", None, None),
            P(),
        ),
        out_specs=(
            P("grp", None),
            P("grp", None),
            P("grp", "fsdp", None),
            P("grp", "fsdp", None),
            P("fsdp", None),
            P("fsdp", None),
            P("fsdp", None),
            P("grp", None, "fsdp", None),
            P("grp", None, "fsdp", None),
            P(None, "fsdp", None),
            P(None, "fsdp", None),
            P(None, "fsdp", None),
            P("grp", None, None, None, "fsdp"),
            P("grp", None, None, None, "fsdp"),
            P(None, None, None, "fsdp"),
            P(None, None, None, "fsdp"),
            P(None, None, None, "fsdp"),
            P("grp", None, None),
            P("grp", None, None),
            P("grp", None, None),
            P(),
            P(),
        ),
        check_vma=False,
    )
```

```python
import functools
import math

import jax
import jax.numpy as jnp
from jax import lax
from jax.experimental import pallas as pl
from jax.experimental.pallas import tpu as pltpu
from jax.sharding import PartitionSpec as P

D = 768
HEADS = 12
HEAD_DIM = 64
EXPERTS = 2
STEP0 = 5
CAP = 192


HIGH = lax.Precision.HIGHEST
EPSILON = 1e-06
ATTN_GAIN = 8.0
SECOND_WEIGHT = 0.3
BETA_ONE = 0.9
BETA_TWO = 0.95
ADAM_EPS = 1e-08
DECAY = 0.1
LR_EMBED = 0.5
LR_MATRIX = 0.012
LR_GAIN = 0.3
LR_ROUTER = 0.012
OUTER_RATE = 0.7
OUTER_MOMENTUM = 0.9


def for_sending(value):

    def short(part):
        return part.astype(jnp.bfloat16) if part.dtype == jnp.float32 else part

    return jax.tree.map(short, value)


def smooth_act(values):
    return jax.nn.gelu(values, approximate=True)


def norm_apply(x, gain_row):
    factor = lax.rsqrt(jnp.mean(x * x, axis=-1, keepdims=True) + EPSILON)
    return (x * factor * gain_row, factor)


def norm_back(x, factor, gain_row, upstream):
    normed = x * factor
    gain_grad = jnp.sum(upstream * normed, axis=0)
    scaled = upstream * gain_row
    return (
        factor * (scaled - normed * jnp.mean(scaled * normed, axis=-1, keepdims=True)),
        gain_grad,
    )


def rows_forward(attn_low, vector_w, x_embed, seg_ids, pick_ids):
    a_float, a_factor = norm_apply(x_embed, vector_w[0])
    a = a_float.astype(jnp.bfloat16)
    a_rows = a[pick_ids]
    q = jnp.dot(a_rows, attn_low[0], preferred_element_type=jnp.float32).astype(jnp.bfloat16)
    k = jnp.dot(a, attn_low[1], preferred_element_type=jnp.float32).astype(jnp.bfloat16)
    v = jnp.dot(a, attn_low[2], preferred_element_type=jnp.float32).astype(jnp.bfloat16)
    places = jnp.arange(x_embed.shape[0])
    allowed = (places[None, :] <= pick_ids[:, None]) & (
        seg_ids[pick_ids][:, None] == seg_ids[None, :]
    )
    count = pick_ids.shape[0]
    head_of = jnp.arange(D) // HEAD_DIM
    head_mask = (head_of[None, None, :] == jnp.arange(HEADS)[:, None, None])
    q_wide = jnp.where(head_mask, q[None], 0).reshape(HEADS * count, D)
    scores = jnp.einsum("rd,td->rt", q_wide, k, preferred_element_type=jnp.float32) * HEAD_DIM ** (-0.5)
    allowed = jnp.tile(allowed, (HEADS, 1))
    scores = jnp.where(allowed, scores, -1e30)
    exponent = jnp.exp(scores - jnp.max(scores, axis=-1, keepdims=True))
    probs = exponent / jnp.sum(exponent, axis=-1, keepdims=True)
    spread = jnp.dot(probs.astype(jnp.bfloat16), v, preferred_element_type=jnp.float32)
    o = jnp.sum(jnp.where(head_mask, spread.reshape(HEADS, count, D), 0.0), axis=0).astype(jnp.bfloat16)
    x_attn = x_embed[pick_ids] + ATTN_GAIN * jnp.dot(o, attn_low[3], preferred_element_type=jnp.float32)
    return x_attn, (a_factor, a, a_rows, q_wide, k, v, probs, o, head_mask)


def rows_backward(attn_low, vector_w, x_embed, kept, dx_attn, pick_ids):
    a_factor, a, a_rows, q_wide, k, v, probs, o, head_mask = kept
    count = pick_ids.shape[0]
    dbranch = dx_attn.astype(jnp.bfloat16)
    dwout = ATTN_GAIN * jnp.dot(o.T, dbranch, preferred_element_type=jnp.float32)
    do = (ATTN_GAIN * jnp.dot(dbranch, attn_low[3].T, preferred_element_type=jnp.float32)).astype(jnp.bfloat16)
    do_wide = jnp.where(head_mask, do[None], 0).reshape(HEADS * count, D)
    dprobs = jnp.einsum("rd,td->rt", do_wide, v, preferred_element_type=jnp.float32)
    dscores = (probs * (dprobs - jnp.sum(probs * dprobs, axis=-1, keepdims=True))).astype(jnp.bfloat16)
    factor_qk = HEAD_DIM ** (-0.5)
    dq = jnp.dot(dscores, k, preferred_element_type=jnp.float32).reshape(HEADS, count, D)
    dq = (jnp.sum(jnp.where(head_mask, dq, 0.0), axis=0) * factor_qk).astype(jnp.bfloat16)
    dk = (jnp.dot(dscores.T, q_wide, preferred_element_type=jnp.float32) * factor_qk).astype(jnp.bfloat16)
    dv = jnp.dot(probs.astype(jnp.bfloat16).T, do_wide, preferred_element_type=jnp.float32).astype(jnp.bfloat16)
    dlayer = jnp.stack(
        [
            jnp.dot(a_rows.T, dq, preferred_element_type=jnp.float32),
            jnp.dot(a.T, dk, preferred_element_type=jnp.float32),
            jnp.dot(a.T, dv, preferred_element_type=jnp.float32),
            dwout,
        ]
    )
    places = jnp.arange(x_embed.shape[0])
    pick_mask = (places[:, None] == pick_ids[None, :]).astype(jnp.float32)
    dinput = jnp.dot(dk, attn_low[1].T, preferred_element_type=jnp.float32)
    dinput = dinput + jnp.dot(dv, attn_low[2].T, preferred_element_type=jnp.float32)
    dq_in = jnp.dot(dq, attn_low[0].T, preferred_element_type=jnp.float32)
    dinput = dinput + jnp.dot(pick_mask, dq_in, precision=HIGH)
    dx, gain_attn = norm_back(x_embed, a_factor, vector_w[0], dinput)
    return dx + jnp.dot(pick_mask, dx_attn, precision=HIGH), dlayer, gain_attn


def gather_rows(value, axis=0):
    return lax.all_gather(value, "fsdp", axis=axis, tiled=True)


def scatter_rows(value, axis=0):
    return lax.psum_scatter(
        value.astype(jnp.bfloat16), "fsdp", scatter_dimension=axis, tiled=True
    ).astype(jnp.float32)


TILE = 512
MESH = pl.DeviceIdType.MESH
F32 = jnp.float32
LOW = jnp.bfloat16
X_IN, B_ROWS, Y_PART, HEAD_ROWS, TOPS, D_ROWS, DY_ROWS, DB_PART = range(8)
ROWS_ONE, P_A, ROWS_TWO, DS_A, G_OUT, D_VEC, EXCHANGES = range(8, 15)


def dot_nn(left, right):
    return lax.dot_general(left, right, (((1,), (0,)), ((), ())), preferred_element_type=F32)


def dot_nt(left, right):
    return lax.dot_general(left, right, (((1,), (1,)), ((), ())), preferred_element_type=F32)


def dot_tn(left, right):
    return lax.dot_general(left, right, (((0,), (0,)), ((), ())), preferred_element_type=F32)


def lanes(shape):
    return lax.broadcasted_iota(jnp.int32, shape, len(shape) - 1)


def sublanes(shape):
    return lax.broadcasted_iota(jnp.int32, shape, len(shape) - 2)


def norm_factor(x):
    return lax.rsqrt(jnp.mean(x * x, axis=-1, keepdims=True) + EPSILON)


def norm_grad(x, factor, gain_row, upstream):
    normed = x * factor
    scaled = upstream * gain_row
    back = factor * (scaled - normed * jnp.mean(scaled * normed, axis=-1, keepdims=True))
    return back, jnp.sum(upstream * normed, axis=0, keepdims=True)


GELU_C = math.sqrt(2.0 / math.pi)


def gelu_of(u):
    return 0.5 * u * (1.0 + jnp.tanh(GELU_C * (u + 0.044715 * (u * u * u))))


def gelu_slope(u):
    t = jnp.tanh(GELU_C * (u + 0.044715 * (u * u * u)))
    return 0.5 * (1.0 + t) + 0.5 * u * (1.0 - t * t) * GELU_C * (1.0 + 3.0 * 0.044715 * u * u)


class Links:
    def __init__(self, n, send, recv):
        self.n, self.send, self.recv = n, send, recv
        self.me = lax.axis_index("fsdp")

    def others(self, body):
        def one_step(k, carry):
            body(k, lax.rem(self.me + k, self.n))
            return carry

        lax.fori_loop(1, self.n, one_step, 0)

    def link(self, which, k, source, target, peer, origin):
        return pltpu.make_async_remote_copy(
            src_ref=source,
            dst_ref=target,
            send_sem=self.send.at[which, k],
            recv_sem=self.recv.at[which, origin],
            device_id={"fsdp": peer},
            device_id_type=MESH,
        )

    def greet(self, extra=0):
        barrier = pltpu.get_barrier_semaphore()
        self.others(
            lambda k, peer: pl.semaphore_signal(
                barrier, inc=1, device_id={"fsdp": peer}, device_id_type=MESH
            )
        )
        return barrier

    def spread(self, which, buffer):
        me = self.me
        self.others(
            lambda k, peer: self.link(which, k, buffer.at[me], buffer.at[me], peer, me).start()
        )

    def deal(self, which, source, target):
        me = self.me
        self.others(
            lambda k, peer: self.link(which, k, source.at[peer], target.at[me], peer, me).start()
        )

    def arrive(self, which, target):
        self.others(
            lambda k, peer: self.link(
                which, k, target.at[peer], target.at[peer], peer, peer
            ).wait_recv()
        )

    def sent(self, which, source):
        me = self.me
        self.others(
            lambda k, peer: self.link(
                which, k, source.at[peer], source.at[peer], peer, me
            ).wait_send()
        )

    def partners(self, body):
        def one_step(k, carry):
            body(k, lax.rem(self.me + 2 * k, self.n))
            return carry

        lax.fori_loop(1, self.n // 2, one_step, 0)

    def relay(self, which, buffer):
        me, twin = self.me, self.me + 1 - 2 * lax.rem(self.me, 2)
        self.link(which, self.n // 2, buffer.at[me], buffer.at[me], twin, me).start()
        self.partners(
            lambda k, peer: self.link(which, k, buffer.at[me], buffer.at[me], peer, me).start()
        )

    def relayed(self, which, buffer):
        me, twin = self.me, self.me + 1 - 2 * lax.rem(self.me, 2)
        n = self.n

        def pass_on(k, peer):
            copy = self.link(which, k, buffer.at[peer], buffer.at[peer], peer, peer)
            copy.wait_recv()
            self.link(which, n // 2 + k, buffer.at[peer], buffer.at[peer], twin, peer).start()

        self.partners(pass_on)

        def got(k, carry):
            origin = lax.rem(twin + 2 * k, n)
            self.link(which, k, buffer.at[origin], buffer.at[origin], twin, origin).wait_recv()
            return carry

        lax.fori_loop(0, n // 2, got, 0)

    def relay_sent(self, which, buffer):
        def gone(k, carry):
            peer = lax.rem(self.me + 1, self.n)
            self.link(which, k, buffer.at[0], buffer.at[0], peer, 0).wait_send()
            return carry

        lax.fori_loop(1, self.n, gone, 0)


def tiles_of(vocab_rows, body, carry):
    whole = vocab_rows // TILE
    carry = lax.fori_loop(
        0, whole, lambda i, c: body(i, pl.multiple_of(i * TILE, TILE), TILE, c), carry
    )
    if vocab_rows % TILE:
        carry = body(whole, whole * TILE, vocab_rows % TILE, carry)
    return carry


def rows_at_once(n, slots):
    return max(g for g in range(1, n + 1) if n % g == 0 and g * slots <= 512)


def share_kernel(n, groups, packed, everyone, worst, marks, send, recv, mark_send, mark_recv):
    links = Links(n, send, recv)
    me = links.me
    group = lax.axis_index("grp")

    def other_groups(body):
        for k in range(1, groups):
            body(k, lax.rem(group + k, groups))

    barrier = links.greet()
    other_groups(
        lambda k, peer: pl.semaphore_signal(
            barrier, inc=1, device_id={"grp": peer}, device_id_type=MESH
        )
    )
    pl.semaphore_wait(barrier, n - 1 + groups - 1)
    everyone[me] = packed[...]
    links.spread(0, everyone)
    links.arrive(0, everyone)
    most = everyone[0]
    for j in range(1, n):
        most = jnp.maximum(most, everyone[j])
    marks[group] = jnp.broadcast_to(most[:1, -128:], (8, 128))

    def mark(k, peer, origin):
        return pltpu.make_async_remote_copy(
            src_ref=marks.at[origin],
            dst_ref=marks.at[origin],
            send_sem=mark_send.at[k],
            recv_sem=mark_recv.at[origin],
            device_id={"grp": peer},
            device_id_type=MESH,
        )

    other_groups(lambda k, peer: mark(k, peer, group).start())
    other_groups(lambda k, peer: mark(k, peer, peer).wait_recv())
    most = marks[0]
    for j in range(1, groups):
        most = jnp.maximum(most, marks[j])
    worst[...] = most
    links.sent(0, everyone)
    other_groups(lambda k, peer: mark(k, peer, group).wait_send())


def share(n, packed):
    groups = lax.axis_size("grp")
    vmem = pl.BlockSpec(memory_space=pltpu.VMEM)
    return pl.pallas_call(
        functools.partial(share_kernel, n, groups),
        out_shape=(
            jax.ShapeDtypeStruct((n,) + packed.shape, jnp.int32),
            jax.ShapeDtypeStruct((8, 128), jnp.int32),
        ),
        in_specs=[vmem],
        out_specs=(vmem, vmem),
        scratch_shapes=[
            pltpu.VMEM((groups, 8, 128), jnp.int32),
            pltpu.SemaphoreType.DMA((1, n)),
            pltpu.SemaphoreType.DMA((1, n)),
            pltpu.SemaphoreType.DMA((groups,)),
            pltpu.SemaphoreType.DMA((groups,)),
        ],
        compiler_params=pltpu.CompilerParams(collective_id=1, has_side_effects=True),
        name="share_ids",
    )(packed)


def fetch_kernel(dims, ints, eb, x_out, id_s, xs, xr, send, recv):
    n, slots, vocab_rows, tokens, row_count = dims
    turned = ints[...].astype(F32).T.astype(jnp.int32)
    id_s[...] = turned[: n * slots, 0:1]
    slot_col = turned[:tokens, 1:2]
    links = Links(n, send, recv)
    me = links.me
    group = rows_at_once(n, slots)
    chunk = group * slots
    pl.semaphore_wait(links.greet(), n - 1)

    def look(c, carry):
        ids = id_s[pl.ds(pl.multiple_of(c * chunk, chunk), chunk), :]

        def add(i, start, size, acc):
            hit = (lanes((chunk, size)) + start == ids).astype(F32).astype(LOW)
            return acc + dot_nn(hit, eb[pl.ds(start, size), :])

        found = tiles_of(vocab_rows, add, jnp.zeros((chunk, D), F32))
        xs[pl.ds(c * group, group)] = found.astype(LOW).reshape(group, slots, D)
        return carry

    lax.fori_loop(0, n // group, look, 0)
    links.deal(0, xs, xr)
    xr[me] = xs[me]
    links.arrive(0, xr)
    x = jnp.zeros((tokens, D), F32)
    for c in range(n // group):
        hit = (lanes((tokens, chunk)) + c * chunk == slot_col).astype(F32).astype(LOW)
        x = x + dot_nn(hit, xr[c * group : (c + 1) * group].reshape(chunk, D))
    x_out[...] = x.astype(LOW)
    links.sent(0, xs)


def fetch(n, slots, sizes, ints, embed_low):
    vmem = pl.BlockSpec(memory_space=pltpu.VMEM)
    vocab_rows = embed_low.shape[0]
    return pl.pallas_call(
        functools.partial(fetch_kernel, (n, slots, vocab_rows) + sizes),
        out_shape=jax.ShapeDtypeStruct((sizes[0], D), LOW),
        in_specs=[vmem] * 2,
        out_specs=vmem,
        scratch_shapes=[
            pltpu.VMEM((n * slots, 1), jnp.int32),
            pltpu.VMEM((n, slots, D), LOW),
            pltpu.VMEM((n, slots, D), LOW),
            pltpu.SemaphoreType.DMA((1, n)),
            pltpu.SemaphoreType.DMA((1, n)),
        ],
        compiler_params=pltpu.CompilerParams(
            collective_id=2, has_side_effects=True, vmem_limit_bytes=40 * 1024 * 1024
        ),
        name="fetch_rows",
    )(ints, embed_low)


def step_kernel(
    dims,
    ints, vec, x_low, eb_in, attn_in, expw_in,
    dembed_out, dattn_out, dexp_out, dvec_out, loss_out,
    eb, attn, expw, xs, gr, ball, ys, yr, rows, tops, drs, drr, dyall, dbs, dbr,
    one, pas, par, two, dss, dsr, dvec, logit_s, dlog_s, pre_s, hid_s, dpre_s, flip_s, tile_s,
    send, recv, out_sem, load_sem,
):
    n, slots, vocab, vocab_rows, hidden, tokens, row_count = dims
    all_rows = n * row_count
    wide = HEADS * row_count
    shard = D // n
    row_total = float(all_rows)
    scale = 2.0 * D ** (-0.5)
    factor_qk = HEAD_DIM ** (-0.5)
    links = Links(n, send, recv)
    me = links.me
    spread, deal, arrive, sent = links.spread, links.deal, links.arrive, links.sent
    relay, relayed = links.relay, links.relayed
    tiled = functools.partial(tiles_of, vocab_rows)
    loads = [
        pltpu.make_async_copy(source, target, load_sem.at[i])
        for i, (source, target) in enumerate(((attn_in, attn), (expw_in, expw), (eb_in, eb)))
    ]
    for load in loads:
        load.start()

    def added(buffer):
        total = buffer[0].astype(F32)
        for j in range(1, n):
            total = total + buffer[j].astype(F32)
        return total

    pl.semaphore_wait(links.greet(), n - 1)
    group = rows_at_once(n, slots)
    chunk = group * slots
    x = x_low[...].astype(F32)
    id_lane, slot_lane, pick_lane = ints[0:1, : n * slots], ints[1:2, :tokens], ints[2:3, :row_count]
    seg_lane, target_lane = ints[4:5, :tokens], ints[7:8, : 2 * all_rows]
    turned = ints[...].astype(F32).T.astype(jnp.int32)
    pick_col, seg_rows = turned[:row_count, 2:3], turned[:row_count, 3:4]
    route_col, route_all = turned[:row_count, 5:6], turned[:all_rows, 6:7]

    gain_a, gain_b, gain_c, gain_d = (vec[i : i + 1, :] for i in range(4))
    x_factor = norm_factor(x)
    a = (x * x_factor * gain_a).astype(LOW)
    pick = (lanes((row_count, tokens)) == pick_col).astype(F32).astype(LOW)
    x_rows = dot_nn(pick, x_low[...])
    a_rows = dot_nn(pick, a).astype(LOW)
    loads[0].wait()
    q = dot_nn(a_rows, attn[0]).astype(LOW)
    k = dot_nn(a, attn[1]).astype(LOW)
    v = dot_nn(a, attn[2]).astype(LOW)
    head_mask = (
        lax.shift_right_logical(lanes((HEADS, row_count, D)), HEAD_DIM.bit_length() - 1)
        == lax.broadcasted_iota(jnp.int32, (HEADS, row_count, D), 0)
    )

    def widen(low_rows):
        return (
            jnp.where(head_mask, low_rows.astype(F32)[None], 0.0).reshape(wide, D).astype(LOW)
        )

    def narrow(values):
        return jnp.sum(jnp.where(head_mask, values.reshape(HEADS, row_count, D), 0.0), axis=0)

    q_wide = widen(q)
    scores = dot_nt(q_wide, k) * factor_qk
    allowed = (lanes((row_count, tokens)) <= pick_col) & (seg_lane == seg_rows)
    scores = jnp.where(
        allowed[None], scores.reshape(HEADS, row_count, tokens), -1e30
    ).reshape(wide, tokens)
    exponent = jnp.exp(scores - jnp.max(scores, axis=-1, keepdims=True))
    probs = exponent / jnp.sum(exponent, axis=-1, keepdims=True)
    probs_low = probs.astype(LOW)
    o = narrow(dot_nn(probs_low, v)).astype(LOW)
    x_attn = x_rows + ATTN_GAIN * dot_nn(o, attn[3])

    b_factor = norm_factor(x_attn)
    b = x_attn * b_factor * gain_b
    ball[me] = b.astype(LOW)
    spread(B_ROWS, ball)
    router_rows = [vec[4 + e : 5 + e, :] for e in range(EXPERTS)]
    router_logits = [jnp.sum(b * row, axis=-1, keepdims=True) for row in router_rows]
    highest = router_logits[0]
    for value in router_logits[1:]:
        highest = jnp.maximum(highest, value)
    router_exp = [jnp.exp(value - highest) for value in router_logits]
    router_sum = sum(router_exp[1:], router_exp[0])
    router_probs = [value / router_sum for value in router_exp]
    chosen = [(route_col == e).astype(F32) for e in range(EXPERTS)]
    gate = sum([p * c for p, c in zip(router_probs[1:], chosen[1:])], router_probs[0] * chosen[0])
    one[me] = q
    a_turned = a.astype(F32).T.astype(LOW)
    eye = (sublanes((row_count, row_count)) == lanes((row_count, row_count))).astype(F32).astype(LOW)
    flipped = lambda low_rows: dot_tn(low_rows, eye)
    pas[:, :, 0:wide] = dot_nt(a_turned, probs_low).reshape(n, shard, wide).astype(LOW)
    pas[:, :, wide : wide + row_count] = flipped(a_rows).reshape(n, shard, row_count).astype(LOW)
    pas[:, :, wide + row_count :] = flipped(o).reshape(n, shard, row_count).astype(LOW)
    arrive(B_ROWS, ball)
    loads[1].wait()
    b_all = ball[...].reshape(all_rows, D)
    y_part = jnp.zeros((all_rows, D), F32)
    for e in range(EXPERTS):
        pre = dot_nn(b_all, expw[e, 0])
        pre_s[e] = pre
        hid = jnp.where(route_all == e, gelu_of(pre), 0.0).astype(LOW)
        hid_s[e] = hid
        y_part = y_part + dot_nt(hid, expw[e, 1])
    ys[...] = y_part.astype(LOW).reshape(n, row_count, D)
    deal(Y_PART, ys, yr)
    yr[me] = ys[me]
    arrive(Y_PART, yr)
    y = added(yr)
    z = x_attn + gate * y

    z_factor = norm_factor(z)
    first = (z * z_factor * gain_c).astype(LOW)
    middle = dot_nn(first, attn[4])
    middle_factor = norm_factor(middle)
    rows[me, 0] = first
    rows[me, 1] = (middle * middle_factor * gain_d).astype(LOW)
    relay(HEAD_ROWS, rows)
    relayed(HEAD_ROWS, rows)
    deal(P_A, pas, par)
    par[me] = pas[me]
    loads[2].wait()
    loss_rows = 2 * all_rows
    head_rows = rows[...].reshape(loss_rows, D)

    def target_hit(start, size):
        return sublanes((size, loss_rows)) + start == target_lane

    def logits_tile(i, start, size, carry):
        top, total, at_target = carry
        value = dot_nt(eb[pl.ds(start, size), :], head_rows) * scale
        if vocab_rows != vocab:
            value = jnp.where(sublanes((size, loss_rows)) + start < vocab, value, -1e30)
        logit_s[pl.ds(start, size), :] = value
        hit = target_hit(start, size)
        at_target = at_target + jnp.sum(jnp.where(hit, value, 0.0), axis=0, keepdims=True)
        new_top = jnp.maximum(top, jnp.max(value, axis=0, keepdims=True))
        total = total * jnp.exp(top - new_top) + jnp.sum(
            jnp.exp(value - new_top), axis=0, keepdims=True
        )
        return new_top, total, at_target

    nothing = jnp.zeros((1, loss_rows), F32)
    top, total, at_target = tiled(logits_tile, (nothing - 1e30, nothing, nothing))
    place = sublanes((8, loss_rows))
    tops[me] = jnp.where(
        place == 0, top, jnp.where(place == 1, total, jnp.where(place == 2, at_target, 0.0))
    )
    spread(TOPS, tops)
    arrive(TOPS, tops)
    relay(ROWS_ONE, one)
    top = tops[0, 0:1]
    for j in range(1, n):
        top = jnp.maximum(top, tops[j, 0:1])
    total, at_target = nothing, nothing
    for j in range(n):
        total = total + tops[j, 1:2] * jnp.exp(tops[j, 0:1] - top)
        at_target = at_target + tops[j, 2:3]
    logsum = top + jnp.log(total)
    is_first = lax.rem(lanes((1, loss_rows)), 2 * row_count) < row_count
    weight = jnp.where(is_first, 1.0, SECOND_WEIGHT) / row_total
    loss = jnp.sum(weight * (logsum - at_target), axis=-1, keepdims=True)
    loss_out[...] = jnp.broadcast_to(loss, loss_out.shape)

    def dlogits_tile(i, start, size, acc):
        soft = jnp.exp(logit_s[pl.ds(start, size), :] - logsum)
        low = ((soft - target_hit(start, size).astype(F32)) * weight).astype(LOW)
        dlog_s[pl.ds(start, size), :] = low
        return acc + dot_tn(low, eb[pl.ds(start, size), :])

    drows = tiled(dlogits_tile, jnp.zeros((loss_rows, D), F32)) * scale
    drs[...] = drows.astype(LOW).reshape(n, 2 * row_count, D)
    deal(D_ROWS, drs, drr)
    drr[me] = drs[me]
    arrive(D_ROWS, drr)
    drow = added(drr)
    dmiddle, gain_mtp = norm_grad(middle, middle_factor, gain_d, drow[row_count:])
    dmiddle_low = dmiddle.astype(LOW)
    dfirst = drow[:row_count] + dot_nt(dmiddle_low, attn[4])
    dz, gain_final = norm_grad(z, z_factor, gain_c, dfirst)

    dgate = jnp.sum(dz * y, axis=-1, keepdims=True)
    dyall[me] = (gate * dz).astype(LOW)
    spread(DY_ROWS, dyall)
    arrive(DY_ROWS, dyall)
    dy_all = dyall[...].reshape(all_rows, D)
    db_part = jnp.zeros((all_rows, D), F32)
    for e in range(EXPERTS):
        dhid = dot_nn(dy_all, expw[e, 1])
        slope = jnp.where(route_all == e, gelu_slope(pre_s[e]), 0.0)
        dpre = (slope * dhid).astype(LOW)
        dpre_s[e] = dpre
        db_part = db_part + dot_nt(dpre, expw[e, 0])
    dbs[...] = db_part.astype(LOW).reshape(n, row_count, D)
    deal(DB_PART, dbs, dbr)
    dbr[me] = dbs[me]
    squares = jnp.zeros((1, D), F32)

    def squared(values):
        return jnp.sum(values * values, axis=0, keepdims=True)

    hidden_squares = jnp.zeros((1, hidden), F32)
    for e in range(EXPERTS):
        up = dot_tn(b_all, dpre_s[e])
        down = dot_tn(dy_all, hid_s[e])
        dexp_out[e, 0] = up
        dexp_out[e, 1] = down
        hidden_squares = hidden_squares + squared(up) + squared(down)
    arrive(DB_PART, dbr)
    prob_grads = [c * dgate for c in chosen]
    mixed = sum([p * g for p, g in zip(router_probs[1:], prob_grads[1:])], router_probs[0] * prob_grads[0])
    dlogits = [p * (g - mixed) for p, g in zip(router_probs, prob_grads)]
    drouter = [jnp.sum(g * b, axis=0, keepdims=True) for g in dlogits]
    dnormed = added(dbr)
    for g, row in zip(dlogits, router_rows):
        dnormed = dnormed + g * row
    dx_part, gain_ffn = norm_grad(x_attn, b_factor, gain_b, dnormed)
    dx_attn = dz + dx_part

    dbranch = dx_attn.astype(LOW)
    do = (ATTN_GAIN * dot_nt(dbranch, attn[3])).astype(LOW)
    do_wide = widen(do)
    dprobs = dot_nt(do_wide, v)
    dscores = (probs * (dprobs - jnp.sum(probs * dprobs, axis=-1, keepdims=True))).astype(LOW)
    dq = (narrow(dot_nn(dscores, k)) * factor_qk).astype(LOW)
    two[me, 0] = do
    two[me, 1] = dq
    two[me, 2] = dbranch
    two[me, 3] = dmiddle_low
    dk = (dot_tn(dscores, q_wide) * factor_qk).astype(LOW)
    dv = dot_tn(probs_low, do_wide).astype(LOW)
    dinput = dot_nt(dk, attn[1]) + dot_nt(dv, attn[2])
    dx, gain_attn = norm_grad(x, x_factor, gain_a, dinput)
    row_back, gain_more = norm_grad(x_rows, norm_factor(x_rows), gain_a, dot_nt(dq, attn[0]))
    spots = (sublanes((tokens, row_count)) == pick_lane).astype(F32)
    dx = dx + lax.dot_general(
        spots, row_back + dx_attn, (((1,), (0,)), ((), ())), precision=HIGH,
        preferred_element_type=F32,
    )
    dx_low = dx.astype(LOW)
    for c in range(n // group):
        hit = (sublanes((chunk, tokens)) + c * chunk == slot_lane).astype(F32).astype(LOW)
        xs[c * group : (c + 1) * group] = dot_nn(hit, dx_low).astype(LOW).reshape(group, slots, D)
    deal(G_OUT, xs, gr)
    gr[me] = xs[me]
    relay(ROWS_TWO, two)
    dss[...] = dot_nt(a_turned, dscores).reshape(n, shard, wide).astype(LOW)
    deal(DS_A, dss, dsr)
    dsr[me] = dss[me]

    relayed(ROWS_ONE, one)
    arrive(P_A, par)
    relayed(ROWS_TWO, two)
    arrive(DS_A, dsr)
    mine = pl.ds(pl.multiple_of(me * shard, 8), shard)

    def own_slices(start, right):
        total = jnp.zeros((shard, D), F32)
        for j in range(n):
            total = total + dot_nn(par[j, :, start : start + row_count], right[j])
        return total

    def own_rows(left, right):
        flip_s[...] = left.astype(F32).reshape(all_rows, D).T
        return dot_nn(flip_s[mine, :].astype(LOW), right.reshape(all_rows, D))

    dkey = jnp.zeros((shard, D), F32)
    dvalue = jnp.zeros((shard, D), F32)
    for j in range(n):
        dkey = dkey + dot_nn(dsr[j], widen(one[j]))
        dvalue = dvalue + dot_nn(par[j, :, 0:wide], widen(two[j, 0]))
    parts = (
        own_slices(wide, two[:, 1]),
        dkey * factor_qk,
        dvalue,
        ATTN_GAIN * own_slices(wide + row_count, two[:, 2]),
        own_rows(rows[:, 0], two[:, 3]),
    )
    for i, part in enumerate(parts):
        dattn_out[i] = part
        squares = squares + squared(part)

    arrive(G_OUT, gr)
    whole = vocab_rows // TILE

    def leave(i, start, size):
        slot = lax.rem(i, 2)
        return pltpu.make_async_copy(
            tile_s.at[slot, pl.ds(0, size)], dembed_out.at[pl.ds(start, size)], out_sem.at[slot]
        )

    def dembed_tile(i, start, size, acc):
        value = scale * dot_nn(dlog_s[pl.ds(start, size), :], head_rows)
        for c in range(n // group):
            ids = id_lane[:, c * chunk : (c + 1) * chunk]
            hit = (sublanes((size, chunk)) + start == ids).astype(F32).astype(LOW)
            value = value + dot_nn(hit, gr[c * group : (c + 1) * group].reshape(chunk, D))

        def free():
            leave(i - 2, start - 2 * TILE, TILE).wait()

        if isinstance(i, int):
            if i >= 2:
                free()
        else:
            pl.when(i >= 2)(free)
        tile_s[lax.rem(i, 2), pl.ds(0, size)] = value
        leave(i, start, size).start()
        return acc + squared(value)

    squares = tiled(dembed_tile, squares)
    tiles = [(i, i * TILE, TILE) for i in range(whole)]
    if vocab_rows % TILE:
        tiles.append((whole, whole * TILE, vocab_rows % TILE))
    total_squares = jnp.sum(squares, axis=-1, keepdims=True) + jnp.sum(
        hidden_squares, axis=-1, keepdims=True
    )
    line = sublanes((8, D))
    share = jnp.broadcast_to(total_squares, (8, D))
    for i, value in enumerate([gain_attn + gain_more, gain_ffn, gain_final, gain_mtp] + drouter):
        share = jnp.where(line == i, value, share)
    dvec[me] = share
    spread(D_VEC, dvec)
    arrive(D_VEC, dvec)
    dvec_out[...] = added(dvec)
    for i, start, size in tiles[-2:]:
        leave(i, start, size).wait()
    for which, source in (
        (B_ROWS, ball), (Y_PART, ys), (TOPS, tops), (D_ROWS, drs), (DY_ROWS, dyall),
        (DB_PART, dbs), (P_A, pas), (DS_A, dss), (G_OUT, xs), (D_VEC, dvec),
    ):
        sent(which, source)
    for which, source in ((HEAD_ROWS, rows), (ROWS_ONE, one), (ROWS_TWO, two)):
        links.relay_sent(which, source)


def run_step(n, slots, vocab, sizes, ints, vec, x_low, embed_low, attn_low, expert_low):
    vocab_rows = embed_low.shape[0]
    row_count = sizes[1]
    hidden = expert_low.shape[3]
    shard = D // n
    all_rows = n * row_count
    wide = HEADS * row_count
    vmem = pl.BlockSpec(memory_space=pltpu.VMEM)
    anywhere = pl.BlockSpec(memory_space=pl.ANY)
    low = lambda *shape: pltpu.VMEM(shape, LOW)
    wide_float = lambda *shape: pltpu.VMEM(shape, F32)
    outs = pl.pallas_call(
        functools.partial(step_kernel, (n, slots, vocab, vocab_rows, hidden) + sizes),
        out_shape=(
            jax.ShapeDtypeStruct((vocab_rows, D), F32),
            jax.ShapeDtypeStruct((5, shard, D), F32),
            jax.ShapeDtypeStruct((EXPERTS, 2, D, hidden), F32),
            jax.ShapeDtypeStruct((8, D), F32),
            jax.ShapeDtypeStruct((8, 128), F32),
        ),
        in_specs=[vmem] * 3 + [anywhere] * 3,
        out_specs=(anywhere, vmem, vmem, vmem, vmem),
        scratch_shapes=[
            low(vocab_rows, D), low(5, D, D), low(EXPERTS, 2, D, hidden),
            low(n, slots, D), low(n, slots, D),
            low(n, row_count, D), low(n, row_count, D), low(n, row_count, D),
            low(n, 2, row_count, D), wide_float(n, 8, 2 * all_rows),
            low(n, 2 * row_count, D), low(n, 2 * row_count, D),
            low(n, row_count, D), low(n, row_count, D), low(n, row_count, D),
            low(n, row_count, D), low(n, shard, wide + 2 * row_count),
            low(n, shard, wide + 2 * row_count),
            low(n, 4, row_count, D), low(n, shard, wide), low(n, shard, wide),
            wide_float(n, 8, D),
            wide_float(vocab_rows, 2 * all_rows), low(vocab_rows, 2 * all_rows),
            wide_float(EXPERTS, all_rows, hidden), low(EXPERTS, all_rows, hidden),
            low(EXPERTS, all_rows, hidden), wide_float(D, all_rows), wide_float(2, TILE, D),
            pltpu.SemaphoreType.DMA((EXCHANGES, n)),
            pltpu.SemaphoreType.DMA((EXCHANGES, n)),
            pltpu.SemaphoreType.DMA((2,)),
            pltpu.SemaphoreType.DMA((3,)),
        ],
        compiler_params=pltpu.CompilerParams(
            collective_id=3, has_side_effects=True, vmem_limit_bytes=60 * 1024 * 1024
        ),
        name="inner_step",
    )(ints, vec, x_low, embed_low, attn_low, expert_low)
    return (outs[0][:vocab],) + outs[1:]


def sum_kernel(dims, value, vector, total, vector_total, held, first_in, second_in, rest, flat, *sems):
    rows, quarter, pieces = dims
    one_s, one_r, two_s, two_r, three_s, three_r, four_s, four_r, rest_s, rest_r = sems
    group = lax.axis_index("grp")
    size, width = quarter // pieces, D // 2
    bits = (lax.rem(group, 2), lax.div(group, 2))
    flip = lambda bit: group + (1 - 2 * bits[bit]) * (1 + bit)
    barrier = pltpu.get_barrier_semaphore()
    for k in range(1, 4):
        pl.semaphore_signal(
            barrier, inc=1, device_id={"grp": lax.rem(group + k, 4)}, device_id_type=MESH
        )
    pl.semaphore_wait(barrier, 3)

    def place(side, first_bit, second_bit, piece):
        owner = first_bit + 2 * second_bit if side == 0 else second_bit + 2 * first_bit
        start = pl.multiple_of((owner * pieces + piece) * size, 16)
        return pl.ds(start, size), pl.ds(side * width, width)

    def copy(source, target, send, recv, peer):
        return pltpu.make_async_remote_copy(
            src_ref=source, dst_ref=target, send_sem=send, recv_sem=recv,
            device_id={"grp": peer}, device_id_type=MESH,
        )

    units = [(side, piece) for piece in range(pieces) for side in range(2)]

    def stage_one(u, turn):
        side, piece = units[u]
        here, there = bits[side], bits[1 - side]
        second = there if turn else 1 - there
        out = place(side, 1 - here, second, piece)
        return copy(value.at[out], first_in.at[u, turn], one_s.at[u, turn], one_r.at[u, turn], flip(side))

    def stage_two(u):
        side, piece = units[u]
        return copy(held.at[u, 0], second_in.at[u], two_s.at[u], two_r.at[u], flip(1 - side))

    def stage_three(u):
        side, piece = units[u]
        own = place(side, bits[side], bits[1 - side], piece)
        return copy(total.at[own], total.at[own], three_s.at[u], three_r.at[u], flip(1 - side))

    def stage_four(u, turn):
        side, piece = units[u]
        there = bits[1 - side]
        own = place(side, bits[side], there if turn == 0 else 1 - there, piece)
        return copy(total.at[own], total.at[own], four_s.at[u, turn], four_r.at[u, turn], flip(side))

    main = 4 * quarter
    spare = rows - main
    flat[group] = vector[...]
    if spare:
        rest[group, 0:spare] = value[main:rows]

    def small(which, k, peer, origin):
        buffer = (rest, flat)[which]
        return copy(
            buffer.at[origin], buffer.at[origin], rest_s.at[which, k], rest_r.at[which, origin], peer
        )

    for u in range(len(units)):
        stage_one(u, 0).start()
    for u in range(len(units)):
        stage_one(u, 1).start()
    smalls = (0, 1) if spare else (1,)
    for which in smalls:
        for k in range(1, 4):
            small(which, k, lax.rem(group + k, 4), group).start()
    for u, (side, piece) in enumerate(units):
        stage_one(u, 0).wait_recv()
        passed = place(side, bits[side], 1 - bits[1 - side], piece)
        held[u, 0] = (value[passed].astype(F32) + first_in[u, 0].astype(F32)).astype(LOW)
        stage_two(u).start()
    for u, (side, piece) in enumerate(units):
        stage_one(u, 1).wait_recv()
        kept = place(side, bits[side], bits[1 - side], piece)
        held[u, 1] = (value[kept].astype(F32) + first_in[u, 1].astype(F32)).astype(LOW)
    for u, (side, piece) in enumerate(units):
        stage_two(u).wait_recv()
        kept = place(side, bits[side], bits[1 - side], piece)
        total[kept] = (held[u, 1].astype(F32) + second_in[u].astype(F32)).astype(LOW)
        stage_three(u).start()
        stage_four(u, 0).start()
    for u, (side, piece) in enumerate(units):
        come = place(side, bits[side], 1 - bits[1 - side], piece)
        copy(total.at[come], total.at[come], three_s.at[u], three_r.at[u], flip(1 - side)).wait_recv()
        stage_four(u, 1).start()
    for which in smalls:
        for k in range(1, 4):
            origin = lax.rem(group + k, 4)
            small(which, k, origin, origin).wait_recv()
    added = lambda buffer: (buffer[0].astype(F32) + buffer[1].astype(F32)) + (
        buffer[2].astype(F32) + buffer[3].astype(F32)
    )
    vector_total[...] = added(flat)
    if spare:
        total[main:rows] = added(rest)[0:spare].astype(LOW)
    for u, (side, piece) in enumerate(units):
        there = bits[1 - side]
        for turn in range(2):
            come = place(side, 1 - bits[side], there if turn == 0 else 1 - there, piece)
            copy(
                total.at[come], total.at[come], four_s.at[u, turn], four_r.at[u, turn], flip(side)
            ).wait_recv()
    for u in range(len(units)):
        stage_one(u, 0).wait_send()
        stage_one(u, 1).wait_send()
        stage_two(u).wait_send()
        stage_three(u).wait_send()
        stage_four(u, 0).wait_send()
        stage_four(u, 1).wait_send()
    for which in smalls:
        for k in range(1, 4):
            small(which, k, lax.rem(group + k, 4), group).wait_send()


def sum_over_groups(value, vector):
    rows = value.shape[0]
    quarter = rows // 64 * 16
    pieces = 2 if quarter % 32 == 0 else 1
    spare = -(-(rows - 4 * quarter) // 16) * 16
    size, units = quarter // pieces, 2 * pieces
    vmem = pl.BlockSpec(memory_space=pltpu.VMEM)
    block = lambda *lead: pltpu.VMEM(lead + (size, D // 2), LOW)
    dma = pltpu.SemaphoreType.DMA
    return pl.pallas_call(
        functools.partial(sum_kernel, (rows, quarter, pieces)),
        out_shape=(
            jax.ShapeDtypeStruct(value.shape, LOW),
            jax.ShapeDtypeStruct(vector.shape, F32),
        ),
        in_specs=[vmem, vmem],
        out_specs=(vmem, vmem),
        scratch_shapes=[
            block(units, 2), block(units, 2), block(units),
            pltpu.VMEM((4, max(spare, 16), D), LOW), pltpu.VMEM((4,) + vector.shape, F32),
            dma((units, 2)), dma((units, 2)), dma((units,)), dma((units,)), dma((units,)),
            dma((units,)), dma((units, 2)), dma((units, 2)), dma((2, 4)), dma((2, 4)),
        ],
        compiler_params=pltpu.CompilerParams(
            collective_id=4, has_side_effects=True, vmem_limit_bytes=48 * 1024 * 1024
        ),
        cost_estimate=pl.CostEstimate(flops=0, bytes_accessed=300_000_000, transcendentals=0),
        name="sum_groups",
    )(value, vector)


def prepare(n, slots, vocab, tokens, routes, segments, loss_pos):
    steps, count = tokens.shape
    start = lax.axis_index("fsdp") * vocab
    row_count = loss_pos.shape[1]
    owner = tokens // vocab
    places = jnp.arange(count)
    earlier = places[None, None, :] < places[None, :, None]
    same = tokens[:, :, None] == tokens[:, None, :]
    first = jnp.logical_not(jnp.any(same & earlier, axis=2))
    same_owner = owner[:, :, None] == owner[:, None, :]
    rank = jnp.sum((same_owner & earlier & first[:, None, :]).astype(jnp.int32), axis=2)
    own_slot = owner * slots + rank
    slot = jnp.sum(jnp.where(same & first[:, None, :], own_slot[:, None, :], 0), axis=2)
    at_slot = (own_slot[:, :, None] == jnp.arange(n * slots)[None, None, :]) & first[:, :, None]
    ids = jnp.sum(jnp.where(at_slot, tokens[:, :, None] + 1, 0), axis=1) - 1
    picked = loss_pos[:, :, None] == places[None, None, :]
    shifted = lambda by: jnp.sum(
        jnp.where(loss_pos[:, :, None] + by == places[None, None, :], tokens[:, None, :], 0), axis=2
    )
    row_routes = jnp.sum(jnp.where(picked, routes[:, None, :], 0), axis=2)
    row_segs = jnp.sum(jnp.where(picked, segments[:, None, :], 0), axis=2)
    most = jnp.broadcast_to(jnp.max(jnp.where(first, rank, 0)), (steps, 128))
    filler = jnp.zeros((steps, -(n * slots + 3 * row_count) % 128), jnp.int32)
    packed = jnp.concatenate([ids, row_routes, shifted(1), shifted(2), filler, most], axis=1)
    everyone, worst = share(n, packed)
    fits = worst[0, 127] < slots
    wanted = lax.dynamic_slice_in_dim(everyone, lax.axis_index("fsdp") * slots, slots, axis=2) - start
    after = n * slots
    rows = lambda part: jnp.swapaxes(part, 0, 1).reshape(steps, -1)
    lines = [
        rows(wanted),
        slot,
        loss_pos,
        row_segs,
        segments,
        row_routes,
        rows(everyone[:, :, after : after + row_count]),
        rows(everyone[:, :, after + row_count : after + 3 * row_count]) - start,
    ]
    longest = -(-max(line.shape[1] for line in lines) // 128) * 128
    fill = lambda line: jnp.pad(line, ((0, 0), (0, longest - line.shape[1])))
    result = jnp.stack([fill(line) for line in lines], axis=1)
    return result, fits


def general_step(tokens, routes, segments, loss_pos, all_ids, inner_step, weights):
    embed_w, attn_w, expert_w, vector_w = weights
    vocab_shard = embed_w.shape[0]
    vocab_start = lax.axis_index("fsdp") * vocab_shard
    row_total = lax.axis_size("fsdp") * loss_pos.shape[2]
    logit_scale = 2.0 * D ** (-0.5)
    vocab_places = jnp.arange(vocab_shard)
    head_weights = jnp.array([1.0, SECOND_WEIGHT], jnp.float32)
    embed_low = embed_w.astype(jnp.bfloat16)
    attn_low = lax.all_gather(attn_w.astype(jnp.bfloat16), "fsdp", axis=1, tiled=True)
    expert_low = expert_w.astype(jnp.bfloat16)
    ids_group = all_ids[inner_step]
    ids_local = tokens[inner_step, 0]
    seg_ids = segments[inner_step, 0]
    route_ids = routes[inner_step, 0, :, 0]
    pick_ids = loss_pos[inner_step, 0]
    chosen = ids_group - vocab_start
    inside = (chosen >= 0) & (chosen < vocab_shard)
    looked = jnp.take(embed_low, jnp.clip(chosen, 0, vocab_shard - 1), axis=0).astype(
        jnp.float32
    )
    x_embed = lax.psum_scatter(
        jnp.where(inside[:, None], looked, 0.0).astype(jnp.bfloat16),
        "fsdp",
        scatter_dimension=0,
        tiled=True,
    ).astype(jnp.float32)
    x_attn, kept = rows_forward(attn_low, vector_w, x_embed, seg_ids, pick_ids)
    b, b_factor = norm_apply(x_attn, vector_w[1])
    router_probs = jax.nn.softmax(jnp.dot(b, vector_w[4:].T, precision=HIGH), axis=-1)
    row_routes = route_ids[pick_ids]
    onehot = (row_routes[:, None] == jnp.arange(EXPERTS)[None, :]).astype(jnp.float32)
    gating = jnp.sum(router_probs * onehot, axis=1)
    b_all = gather_rows(b.astype(jnp.bfloat16))
    routes_all = gather_rows(row_routes)
    route_mask = routes_all[None, :, None] == jnp.arange(EXPERTS)[:, None, None]
    hidden_pre = jnp.einsum("cd,edf->ecf", b_all, expert_low[:, 0], preferred_element_type=jnp.float32)
    hidden_act = jnp.where(route_mask, smooth_act(hidden_pre), 0.0).astype(jnp.bfloat16)
    y_part = jnp.einsum("ecf,edf->cd", hidden_act, expert_low[:, 1], preferred_element_type=jnp.float32)
    returned = scatter_rows(y_part)
    z_rows = x_attn + gating[:, None] * returned
    first_float, first_factor = norm_apply(z_rows, vector_w[2])
    first_rows = first_float.astype(jnp.bfloat16)
    middle = jnp.dot(first_rows, attn_low[4], preferred_element_type=jnp.float32)
    second_float, second_factor = norm_apply(middle, vector_w[3])
    targets = jnp.stack([ids_local[pick_ids + 1], ids_local[pick_ids + 2]])
    rows_all, targets_all = (
        lax.all_gather(
            jnp.stack([first_rows, second_float.astype(jnp.bfloat16)]),
            "fsdp",
            axis=1,
            tiled=True,
        ),
        lax.all_gather(targets, "fsdp", axis=1, tiled=True),
    )
    logits = (
        jnp.einsum("jrd,vd->jrv", rows_all, embed_low, preferred_element_type=jnp.float32)
        * logit_scale
    )
    relative = targets_all - vocab_start
    onehot_target = (vocab_places[None, None, :] == relative[:, :, None]).astype(jnp.float32)
    target_part = jnp.sum(onehot_target * logits, axis=-1)
    local_top = jnp.max(logits, axis=-1)
    local_sum = jnp.sum(jnp.exp(logits - local_top[:, :, None]), axis=-1)
    parts = lax.all_gather(jnp.stack([local_top, local_sum, target_part]), "fsdp")
    row_top = jnp.max(parts[:, 0], axis=0)
    sum_exp = jnp.sum(parts[:, 1] * jnp.exp(parts[:, 0] - row_top), axis=0)
    target_logit = jnp.sum(parts[:, 2], axis=0)
    logsum = row_top + jnp.log(sum_exp)
    loss = (jnp.sum(head_weights[:, None] * (logsum - target_logit)) / row_total)
    dlogits = (
        (jnp.exp(logits - logsum[:, :, None]) - onehot_target)
        * (head_weights / row_total)[:, None, None]
    ).astype(jnp.bfloat16)
    dembed = (
        jnp.einsum("jrv,jrd->vd", dlogits, rows_all, preferred_element_type=jnp.float32)
        * logit_scale
    )
    drows = (
        jnp.einsum("jrv,vd->jrd", dlogits, embed_low, preferred_element_type=jnp.float32)
        * logit_scale
    )
    drows_own = lax.psum_scatter(
        drows.astype(jnp.bfloat16), "fsdp", scatter_dimension=1, tiled=True
    ).astype(jnp.float32)
    dmiddle, gain_mtp = norm_back(middle, second_factor, vector_w[3], drows_own[1])
    dmiddle_low = dmiddle.astype(jnp.bfloat16)
    dsecond_proj = jnp.dot(first_rows.T, dmiddle_low, preferred_element_type=jnp.float32)
    dfirst = drows_own[0] + jnp.dot(
        dmiddle_low, attn_low[4].T, preferred_element_type=jnp.float32
    )
    dz_rows, gain_final = norm_back(z_rows, first_factor, vector_w[2], dfirst)
    dgating = jnp.sum(dz_rows * returned, axis=1)
    dy_all = gather_rows((gating[:, None] * dz_rows).astype(jnp.bfloat16))
    dy_masked = jnp.where(route_mask, dy_all[None], 0)
    down_grad = jnp.einsum("ecf,ecd->edf", hidden_act, dy_masked, preferred_element_type=jnp.float32)
    dhidden = jnp.einsum("ecd,edf->ecf", dy_masked, expert_low[:, 1], preferred_element_type=jnp.float32)
    unused, act_back = jax.vjp(smooth_act, hidden_pre)
    dhidden_pre = act_back(dhidden)[0].astype(jnp.bfloat16)
    up_grad = jnp.einsum("cd,ecf->edf", b_all, dhidden_pre, preferred_element_type=jnp.float32)
    dexpert = jnp.stack([up_grad, down_grad], axis=1)
    db_part = jnp.einsum("ecf,edf->cd", dhidden_pre, expert_low[:, 0], preferred_element_type=jnp.float32)
    dnormed = scatter_rows(db_part)
    prob_grad = onehot * dgating[:, None]
    dlogit = router_probs * (prob_grad - jnp.sum(router_probs * prob_grad, axis=1, keepdims=True))
    drouter = jnp.dot(dlogit.T, b, precision=HIGH)
    dnormed = dnormed + jnp.dot(dlogit, vector_w[4:], precision=HIGH)
    dx_part, gain_ffn = norm_back(x_attn, b_factor, vector_w[1], dnormed)
    dx_embed, dlayer, gain_attn = rows_backward(
        attn_low, vector_w, x_embed, kept, dz_rows + dx_part, pick_ids
    )
    dattn = scatter_rows(jnp.concatenate([dlayer, dsecond_proj[None]], axis=0), axis=1)
    gather_chosen = ids_group - vocab_start
    gather_inside = (gather_chosen >= 0) & (gather_chosen < vocab_shard)
    seg_index = jnp.where(gather_inside, gather_chosen, vocab_shard)
    added = jax.ops.segment_sum(
        lax.all_gather(dx_embed.astype(jnp.bfloat16), "fsdp", axis=0, tiled=True).astype(
            jnp.float32
        ),
        seg_index,
        num_segments=vocab_shard + 1,
    )
    dembed = dembed + added[:vocab_shard]
    dvector_part = jnp.concatenate(
        [jnp.stack([gain_attn, gain_ffn, gain_final, gain_mtp]), drouter], axis=0
    )
    squares = jnp.sum(dembed * dembed) + jnp.sum(dattn * dattn) + jnp.sum(dexpert * dexpert)
    dvector, squares_all = lax.psum((dvector_part, squares), "fsdp")
    return dembed, dattn, dexpert, dvector, squares_all, loss


def adam_update(weight, first_moment, second, gradient, step_float, rate_here, decay_here):
    first_new = BETA_ONE * first_moment + (1.0 - BETA_ONE) * gradient
    second_new = BETA_TWO * second + (1.0 - BETA_TWO) * gradient * gradient
    first_hat = first_new / (1.0 - BETA_ONE**step_float)
    second_hat = second_new / (1.0 - BETA_TWO**step_float)
    weight_new = weight - rate_here * (
        first_hat / (jnp.sqrt(second_hat) + ADAM_EPS) + decay_here * weight
    )
    return (weight_new, first_new, second_new)


def window(
    step,
    embedding,
    embedding_first,
    embedding_second,
    embedding_outer,
    attention,
    attention_first,
    attention_second,
    attention_outer,
    experts,
    experts_first,
    experts_second,
    experts_outer,
    vectors,
    vectors_first,
    vectors_second,
    vectors_outer,
    inner_count,
    row_total,
):
    group_count = lax.axis_size("grp")
    threshold = 0.05 / math.sqrt(row_total)
    vector_rates = jnp.where(jnp.arange(vectors.shape[0])[:, None] < 4, LR_GAIN, LR_ROUTER)
    rate_list = (LR_EMBED, LR_MATRIX, LR_MATRIX, vector_rates)
    decay_list = (DECAY, DECAY, DECAY, 0.0)
    weights_now = (embedding, attention, experts, vectors)
    first_now = (embedding_first[0], attention_first[0], experts_first[0], vectors_first[0])
    second_now = (embedding_second[0], attention_second[0], experts_second[0], vectors_second[0])
    loss_list = []
    norm_list = []
    for inner_step in range(inner_count):
        dembed, dattn, dexpert, dvector, squares_all, loss = step(inner_step, weights_now)
        loss_list.append(loss)
        norm_value = jnp.sqrt(squares_all + jnp.sum(dvector * dvector))
        norm_list.append(norm_value)
        factor = jnp.minimum(1.0, threshold / norm_value)
        gradients = (dembed * factor, dattn * factor, dexpert * factor, dvector * factor)
        step_float = float(STEP0 + inner_step + 1)
        results = [
            adam_update(
                weights_now[k],
                first_now[k],
                second_now[k],
                gradients[k],
                step_float,
                rate_list[k],
                decay_list[k],
            )
            for k in range(4)
        ]
        weights_now = tuple((element[0] for element in results))
        first_now = tuple((element[1] for element in results))
        second_now = tuple((element[2] for element in results))
    masters = (embedding, attention, experts, vectors)
    outers = (embedding_outer, attention_outer, experts_outer, vectors_outer)
    deltas = tuple((master - current for master, current in zip(masters, weights_now)))
    summed = jax.tree.map(
        lambda part: part.astype(jnp.float32), lax.psum(for_sending(deltas), "grp")
    )
    new_outer = []
    new_master = []
    for k in range(4):
        delta_mean = summed[k] / group_count
        outer_new = OUTER_MOMENTUM * outers[k] + delta_mean
        new_outer.append(outer_new)
        new_master.append(masters[k] - OUTER_RATE * (delta_mean + OUTER_MOMENTUM * outer_new))
    return (
        jnp.stack(loss_list)[None],
        jnp.stack(norm_list)[None],
        first_now[0][None],
        second_now[0][None],
        new_master[0],
        new_outer[0],
        new_master[0].astype(jnp.bfloat16),
        first_now[1][None],
        second_now[1][None],
        new_master[1],
        new_outer[1],
        new_master[1].astype(jnp.bfloat16),
        first_now[2][None],
        second_now[2][None],
        new_master[2],
        new_outer[2],
        new_master[2].astype(jnp.bfloat16),
        gradients[3][None],
        first_now[3][None],
        second_now[3][None],
        new_master[3],
        new_outer[3],
    )


def adam_quick(weight, first_moment, second, gradient, step_float, rate_here, decay_here):
    first_new = BETA_ONE * first_moment + (1.0 - BETA_ONE) * gradient
    second_new = BETA_TWO * second + (1.0 - BETA_TWO) * gradient * gradient
    first_hat = first_new * (1.0 / (1.0 - BETA_ONE**step_float))
    second_hat = second_new * (1.0 / (1.0 - BETA_TWO**step_float))
    weight_new = weight - rate_here * (
        first_hat / (jnp.sqrt(second_hat) + ADAM_EPS) + decay_here * weight
    )
    return (weight_new, first_new, second_new)


def quick_window(n, slots, sizes, steps, x_start, lows, masters, firsts, seconds, outers, row_total):
    embedding, attention, experts, vectors = masters
    vocab = embedding.shape[0]
    threshold = 0.05 / math.sqrt(row_total)
    vector_rates = jnp.where(jnp.arange(vectors.shape[0])[:, None] < 4, LR_GAIN, LR_ROUTER)
    rate_list = (LR_EMBED, LR_MATRIX, LR_MATRIX, vector_rates)
    decay_list = (DECAY, DECAY, DECAY, 0.0)
    taken = []

    def replay(k, factors):
        state = (masters[k], firsts[k], seconds[k])
        for s, factor in enumerate(factors):
            gradient = taken[s][k] * factor
            state = adam_quick(
                *state, gradient, float(STEP0 + s + 1), rate_list[k], decay_list[k]
            )
        return state

    loss_list, norm_list, factor_list = [], [], []
    vector_state = (vectors, firsts[3], seconds[3])
    for s in range(steps.shape[0]):
        ints = steps[s]
        if s:
            again = lax.optimization_barrier(tuple(factor_list))
            attn_low = lax.all_gather(
                replay(1, again)[0].astype(jnp.bfloat16), "fsdp", axis=1, tiled=True
            )
            expert_low = replay(2, again)[0].astype(jnp.bfloat16)
            embed_low = padded(replay(0, again)[0].astype(jnp.bfloat16))
            x_low = fetch(n, slots, sizes, ints, embed_low)
        else:
            (embed_low, attn_low, expert_low), x_low = lows, x_start
        *grads, shared, loss = run_step(
            n, slots, vocab, sizes, ints, vector_state[0], x_low, embed_low, attn_low, expert_low
        )
        dvector = shared[: vectors.shape[0]]
        norm_value = jnp.sqrt(shared[6, 0] + jnp.sum(dvector * dvector))
        factor = jnp.minimum(1.0, threshold / norm_value)
        taken.append(grads)
        loss_list.append(loss[0, 0])
        norm_list.append(norm_value)
        factor_list.append(factor)
        vector_gradient = dvector * factor
        vector_state = adam_quick(
            *vector_state, vector_gradient, float(STEP0 + s + 1), vector_rates, 0.0
        )
    again = lax.optimization_barrier(tuple(factor_list))
    states = [replay(k, again) for k in range(3)] + [vector_state]
    deltas = [master - state[0] for master, state in zip(masters, states)]
    matrix_sums = lax.psum(for_sending((deltas[1], deltas[2])), "grp")
    embed_sum, vector_sum = sum_over_groups(
        deltas[0].astype(jnp.bfloat16), jnp.pad(deltas[3], ((0, 2), (0, 0)))
    )
    sums = (embed_sum, matrix_sums[0], matrix_sums[1], vector_sum[: vectors.shape[0]])
    results = [jnp.stack(loss_list)[None], jnp.stack(norm_list)[None]]
    for k in range(4):
        delta_mean = sums[k].astype(jnp.float32) / lax.axis_size("grp")
        outer_new = OUTER_MOMENTUM * outers[k] + delta_mean
        master_new = masters[k] - OUTER_RATE * (delta_mean + OUTER_MOMENTUM * outer_new)
        if k == 3:
            results.append(vector_gradient[None])
        results += [states[k][1][None], states[k][2][None], master_new, outer_new]
        if k < 3:
            results.append(master_new.astype(jnp.bfloat16))
    return tuple(results)


def padded(embed_low):
    extra = -embed_low.shape[0] % 16
    return jnp.pad(embed_low, ((0, extra), (0, 0))) if extra else embed_low


def shards(
    tokens,
    routes,
    segments,
    loss_pos,
    embedding,
    embedding_first,
    embedding_second,
    embedding_outer,
    attention,
    attention_first,
    attention_second,
    attention_outer,
    experts,
    experts_first,
    experts_second,
    experts_outer,
    vectors,
    vectors_first,
    vectors_second,
    vectors_outer,
):
    inner_count = tokens.shape[0]
    vocab_shard = embedding.shape[0]
    n = lax.axis_size("fsdp")
    row_total = n * loss_pos.shape[2]
    slots = 48
    steps, fits = prepare(
        n, slots, vocab_shard, tokens[:, 0], routes[:, 0, :, 0], segments[:, 0], loss_pos[:, 0]
    )
    lows = (
        padded(embedding.astype(jnp.bfloat16)),
        lax.all_gather(attention.astype(jnp.bfloat16), "fsdp", axis=1, tiled=True),
        experts.astype(jnp.bfloat16),
    )
    sizes = (tokens.shape[2], loss_pos.shape[2])
    x_start = fetch(n, slots, sizes, steps[0], lows[0])
    state = (
        embedding,
        embedding_first,
        embedding_second,
        embedding_outer,
        attention,
        attention_first,
        attention_second,
        attention_outer,
        experts,
        experts_first,
        experts_second,
        experts_outer,
        vectors,
        vectors_first,
        vectors_second,
        vectors_outer,
    )

    def quick(*state):
        masters, firsts, seconds, outers = (
            [state[4 * k + part] for k in range(4)] for part in range(4)
        )
        firsts, seconds = [value[0] for value in firsts], [value[0] for value in seconds]
        return quick_window(
            n, slots, sizes, steps, x_start, lows, masters, firsts, seconds, outers, row_total
        )

    def general(*state):
        all_ids = lax.all_gather(tokens[:, 0, :], "fsdp", axis=1, tiled=True)
        step = functools.partial(general_step, tokens, routes, segments, loss_pos, all_ids)
        return window(step, *state, inner_count, row_total)

    return lax.cond(fits, quick, general, *state)


def solution(mesh):
    return jax.shard_map(
        shards,
        mesh=mesh,
        in_specs=(
            P(None, "grp", "fsdp"),
            P(None, "grp", "fsdp", None),
            P(None, "grp", "fsdp"),
            P(None, "grp", "fsdp"),
            P("fsdp", None),
            P("grp", "fsdp", None),
            P("grp", "fsdp", None),
            P("fsdp", None),
            P(None, "fsdp", None),
            P("grp", None, "fsdp", None),
            P("grp", None, "fsdp", None),
            P(None, "fsdp", None),
            P(None, None, None, "fsdp"),
            P("grp", None, None, None, "fsdp"),
            P("grp", None, None, None, "fsdp"),
            P(None, None, None, "fsdp"),
            P(),
            P("grp", None, None),
            P("grp", None, None),
            P(),
        ),
        out_specs=(
            P("grp", None),
            P("grp", None),
            P("grp", "fsdp", None),
            P("grp", "fsdp", None),
            P("fsdp", None),
            P("fsdp", None),
            P("fsdp", None),
            P("grp", None, "fsdp", None),
            P("grp", None, "fsdp", None),
            P(None, "fsdp", None),
            P(None, "fsdp", None),
            P(None, "fsdp", None),
            P("grp", None, None, None, "fsdp"),
            P("grp", None, None, None, "fsdp"),
            P(None, None, None, "fsdp"),
            P(None, None, None, "fsdp"),
            P(None, None, None, "fsdp"),
            P("grp", None, None),
            P("grp", None, None),
            P("grp", None, None),
            P(),
            P(),
        ),
        check_vma=False,
    )
```

```python
import functools
import math

import jax
import jax.numpy as jnp
from jax import lax
from jax.experimental import pallas as pl
from jax.experimental.pallas import tpu as pltpu
from jax.sharding import PartitionSpec as P

D = 768
HEADS = 12
HEAD_DIM = 64
EXPERTS = 2
STEP0 = 5
CAP = 192


HIGH = lax.Precision.HIGHEST
EPSILON = 1e-06
ATTN_GAIN = 8.0
SECOND_WEIGHT = 0.3
BETA_ONE = 0.9
BETA_TWO = 0.95
ADAM_EPS = 1e-08
DECAY = 0.1
LR_EMBED = 0.5
LR_MATRIX = 0.012
LR_GAIN = 0.3
LR_ROUTER = 0.012
OUTER_RATE = 0.7
OUTER_MOMENTUM = 0.9


def for_sending(value):

    def short(part):
        return part.astype(jnp.bfloat16) if part.dtype == jnp.float32 else part

    return jax.tree.map(short, value)


def smooth_act(values):
    return jax.nn.gelu(values, approximate=True)


def norm_apply(x, gain_row):
    factor = lax.rsqrt(jnp.mean(x * x, axis=-1, keepdims=True) + EPSILON)
    return (x * factor * gain_row, factor)


def norm_back(x, factor, gain_row, upstream):
    normed = x * factor
    gain_grad = jnp.sum(upstream * normed, axis=0)
    scaled = upstream * gain_row
    return (
        factor * (scaled - normed * jnp.mean(scaled * normed, axis=-1, keepdims=True)),
        gain_grad,
    )


def rows_forward(attn_low, vector_w, x_embed, seg_ids, pick_ids):
    a_float, a_factor = norm_apply(x_embed, vector_w[0])
    a = a_float.astype(jnp.bfloat16)
    a_rows = a[pick_ids]
    q = jnp.dot(a_rows, attn_low[0], preferred_element_type=jnp.float32).astype(jnp.bfloat16)
    k = jnp.dot(a, attn_low[1], preferred_element_type=jnp.float32).astype(jnp.bfloat16)
    v = jnp.dot(a, attn_low[2], preferred_element_type=jnp.float32).astype(jnp.bfloat16)
    places = jnp.arange(x_embed.shape[0])
    allowed = (places[None, :] <= pick_ids[:, None]) & (
        seg_ids[pick_ids][:, None] == seg_ids[None, :]
    )
    count = pick_ids.shape[0]
    head_of = jnp.arange(D) // HEAD_DIM
    head_mask = (head_of[None, None, :] == jnp.arange(HEADS)[:, None, None])
    q_wide = jnp.where(head_mask, q[None], 0).reshape(HEADS * count, D)
    scores = jnp.einsum("rd,td->rt", q_wide, k, preferred_element_type=jnp.float32) * HEAD_DIM ** (-0.5)
    allowed = jnp.tile(allowed, (HEADS, 1))
    scores = jnp.where(allowed, scores, -1e30)
    exponent = jnp.exp(scores - jnp.max(scores, axis=-1, keepdims=True))
    probs = exponent / jnp.sum(exponent, axis=-1, keepdims=True)
    spread = jnp.dot(probs.astype(jnp.bfloat16), v, preferred_element_type=jnp.float32)
    o = jnp.sum(jnp.where(head_mask, spread.reshape(HEADS, count, D), 0.0), axis=0).astype(jnp.bfloat16)
    x_attn = x_embed[pick_ids] + ATTN_GAIN * jnp.dot(o, attn_low[3], preferred_element_type=jnp.float32)
    return x_attn, (a_factor, a, a_rows, q_wide, k, v, probs, o, head_mask)


def rows_backward(attn_low, vector_w, x_embed, kept, dx_attn, pick_ids):
    a_factor, a, a_rows, q_wide, k, v, probs, o, head_mask = kept
    count = pick_ids.shape[0]
    dbranch = dx_attn.astype(jnp.bfloat16)
    dwout = ATTN_GAIN * jnp.dot(o.T, dbranch, preferred_element_type=jnp.float32)
    do = (ATTN_GAIN * jnp.dot(dbranch, attn_low[3].T, preferred_element_type=jnp.float32)).astype(jnp.bfloat16)
    do_wide = jnp.where(head_mask, do[None], 0).reshape(HEADS * count, D)
    dprobs = jnp.einsum("rd,td->rt", do_wide, v, preferred_element_type=jnp.float32)
    dscores = (probs * (dprobs - jnp.sum(probs * dprobs, axis=-1, keepdims=True))).astype(jnp.bfloat16)
    factor_qk = HEAD_DIM ** (-0.5)
    dq = jnp.dot(dscores, k, preferred_element_type=jnp.float32).reshape(HEADS, count, D)
    dq = (jnp.sum(jnp.where(head_mask, dq, 0.0), axis=0) * factor_qk).astype(jnp.bfloat16)
    dk = (jnp.dot(dscores.T, q_wide, preferred_element_type=jnp.float32) * factor_qk).astype(jnp.bfloat16)
    dv = jnp.dot(probs.astype(jnp.bfloat16).T, do_wide, preferred_element_type=jnp.float32).astype(jnp.bfloat16)
    dlayer = jnp.stack(
        [
            jnp.dot(a_rows.T, dq, preferred_element_type=jnp.float32),
            jnp.dot(a.T, dk, preferred_element_type=jnp.float32),
            jnp.dot(a.T, dv, preferred_element_type=jnp.float32),
            dwout,
        ]
    )
    places = jnp.arange(x_embed.shape[0])
    pick_mask = (places[:, None] == pick_ids[None, :]).astype(jnp.float32)
    dinput = jnp.dot(dk, attn_low[1].T, preferred_element_type=jnp.float32)
    dinput = dinput + jnp.dot(dv, attn_low[2].T, preferred_element_type=jnp.float32)
    dq_in = jnp.dot(dq, attn_low[0].T, preferred_element_type=jnp.float32)
    dinput = dinput + jnp.dot(pick_mask, dq_in, precision=HIGH)
    dx, gain_attn = norm_back(x_embed, a_factor, vector_w[0], dinput)
    return dx + jnp.dot(pick_mask, dx_attn, precision=HIGH), dlayer, gain_attn


def gather_rows(value, axis=0):
    return lax.all_gather(value, "fsdp", axis=axis, tiled=True)


def scatter_rows(value, axis=0):
    return lax.psum_scatter(
        value.astype(jnp.bfloat16), "fsdp", scatter_dimension=axis, tiled=True
    ).astype(jnp.float32)


TILE = 512
MESH = pl.DeviceIdType.MESH
F32 = jnp.float32
LOW = jnp.bfloat16
B_ROWS, Y_PART, HEAD_ROWS, TOPS, D_ROWS, DY_ROWS, DB_PART = range(7)
Q_ROWS, P_A, MIDDLE_ROWS, BRANCH_ROWS, DQ_ROWS, DS_A, G_OUT, D_VEC, SQUARES, EXCHANGES = range(7, 17)


def dot_nn(left, right):
    return lax.dot_general(left, right, (((1,), (0,)), ((), ())), preferred_element_type=F32)


def dot_nt(left, right):
    return lax.dot_general(left, right, (((1,), (1,)), ((), ())), preferred_element_type=F32)


def dot_tn(left, right):
    return lax.dot_general(left, right, (((0,), (0,)), ((), ())), preferred_element_type=F32)


def lanes(shape):
    return lax.broadcasted_iota(jnp.int32, shape, len(shape) - 1)


def sublanes(shape):
    return lax.broadcasted_iota(jnp.int32, shape, len(shape) - 2)


def norm_factor(x):
    return lax.rsqrt(jnp.mean(x * x, axis=-1, keepdims=True) + EPSILON)


def norm_grad(x, factor, gain_row, upstream):
    normed = x * factor
    scaled = upstream * gain_row
    back = factor * (scaled - normed * jnp.mean(scaled * normed, axis=-1, keepdims=True))
    return back, jnp.sum(upstream * normed, axis=0, keepdims=True)


GELU_C = math.sqrt(2.0 / math.pi)


def gelu_of(u):
    return 0.5 * u * (1.0 + jnp.tanh(GELU_C * (u + 0.044715 * (u * u * u))))


def gelu_slope(u):
    t = jnp.tanh(GELU_C * (u + 0.044715 * (u * u * u)))
    return 0.5 * (1.0 + t) + 0.5 * u * (1.0 - t * t) * GELU_C * (1.0 + 3.0 * 0.044715 * u * u)


class Links:
    def __init__(self, n, send, recv):
        self.n, self.send, self.recv = n, send, recv
        self.me = lax.axis_index("fsdp")

    def others(self, body):
        def one_step(k, carry):
            body(k, lax.rem(self.me + k, self.n))
            return carry

        lax.fori_loop(1, self.n, one_step, 0)

    def link(self, which, k, source, target, peer, origin):
        return pltpu.make_async_remote_copy(
            src_ref=source,
            dst_ref=target,
            send_sem=self.send.at[which, k],
            recv_sem=self.recv.at[which, origin],
            device_id={"fsdp": peer},
            device_id_type=MESH,
        )

    def greet(self, extra=0):
        barrier = pltpu.get_barrier_semaphore()
        self.others(
            lambda k, peer: pl.semaphore_signal(
                barrier, inc=1, device_id={"fsdp": peer}, device_id_type=MESH
            )
        )
        return barrier

    def spread(self, which, buffer):
        me = self.me
        self.others(
            lambda k, peer: self.link(which, k, buffer.at[me], buffer.at[me], peer, me).start()
        )

    def deal(self, which, source, target):
        me = self.me
        self.others(
            lambda k, peer: self.link(which, k, source.at[peer], target.at[me], peer, me).start()
        )

    def arrive(self, which, target):
        self.others(
            lambda k, peer: self.link(
                which, k, target.at[peer], target.at[peer], peer, peer
            ).wait_recv()
        )

    def sent(self, which, source):
        me = self.me
        self.others(
            lambda k, peer: self.link(
                which, k, source.at[peer], source.at[peer], peer, me
            ).wait_send()
        )

    def partners(self, body):
        def one_step(k, carry):
            body(k, lax.rem(self.me + 2 * k, self.n))
            return carry

        lax.fori_loop(1, self.n // 2, one_step, 0)

    def relay(self, which, buffer):
        me, twin = self.me, self.me + 1 - 2 * lax.rem(self.me, 2)
        self.link(which, self.n // 2, buffer.at[me], buffer.at[me], twin, me).start()
        self.partners(
            lambda k, peer: self.link(which, k, buffer.at[me], buffer.at[me], peer, me).start()
        )

    def relayed(self, which, buffer):
        me, twin = self.me, self.me + 1 - 2 * lax.rem(self.me, 2)
        n = self.n

        def pass_on(k, peer):
            copy = self.link(which, k, buffer.at[peer], buffer.at[peer], peer, peer)
            copy.wait_recv()
            self.link(which, n // 2 + k, buffer.at[peer], buffer.at[peer], twin, peer).start()

        self.partners(pass_on)

        def got(k, carry):
            origin = lax.rem(twin + 2 * k, n)
            self.link(which, k, buffer.at[origin], buffer.at[origin], twin, origin).wait_recv()
            return carry

        lax.fori_loop(0, n // 2, got, 0)

    def relay_sent(self, which, buffer):
        def gone(k, carry):
            peer = lax.rem(self.me + 1, self.n)
            self.link(which, k, buffer.at[0], buffer.at[0], peer, 0).wait_send()
            return carry

        lax.fori_loop(1, self.n, gone, 0)


def tiles_of(vocab_rows, body, carry):
    whole = vocab_rows // TILE
    carry = lax.fori_loop(
        0, whole, lambda i, c: body(i, pl.multiple_of(i * TILE, TILE), TILE, c), carry
    )
    if vocab_rows % TILE:
        carry = body(whole, whole * TILE, vocab_rows % TILE, carry)
    return carry


def rows_at_once(n, slots):
    return max(g for g in range(1, n + 1) if n % g == 0 and g * slots <= 512)


def share_kernel(n, groups, packed, everyone, worst, marks, send, recv, mark_send, mark_recv):
    links = Links(n, send, recv)
    me = links.me
    group = lax.axis_index("grp")

    def other_groups(body):
        for k in range(1, groups):
            body(k, lax.rem(group + k, groups))

    barrier = links.greet()
    other_groups(
        lambda k, peer: pl.semaphore_signal(
            barrier, inc=1, device_id={"grp": peer}, device_id_type=MESH
        )
    )
    pl.semaphore_wait(barrier, n - 1 + groups - 1)
    everyone[me] = packed[...]
    links.spread(0, everyone)
    links.arrive(0, everyone)
    most = everyone[0]
    for j in range(1, n):
        most = jnp.maximum(most, everyone[j])
    marks[group] = jnp.broadcast_to(most[:1, -128:], (8, 128))

    def mark(k, peer, origin):
        return pltpu.make_async_remote_copy(
            src_ref=marks.at[origin],
            dst_ref=marks.at[origin],
            send_sem=mark_send.at[k],
            recv_sem=mark_recv.at[origin],
            device_id={"grp": peer},
            device_id_type=MESH,
        )

    other_groups(lambda k, peer: mark(k, peer, group).start())
    other_groups(lambda k, peer: mark(k, peer, peer).wait_recv())
    most = marks[0]
    for j in range(1, groups):
        most = jnp.maximum(most, marks[j])
    worst[...] = most
    links.sent(0, everyone)
    other_groups(lambda k, peer: mark(k, peer, group).wait_send())


def share(n, packed):
    groups = lax.axis_size("grp")
    vmem = pl.BlockSpec(memory_space=pltpu.VMEM)
    return pl.pallas_call(
        functools.partial(share_kernel, n, groups),
        out_shape=(
            jax.ShapeDtypeStruct((n,) + packed.shape, jnp.int32),
            jax.ShapeDtypeStruct((8, 128), jnp.int32),
        ),
        in_specs=[vmem],
        out_specs=(vmem, vmem),
        scratch_shapes=[
            pltpu.VMEM((groups, 8, 128), jnp.int32),
            pltpu.SemaphoreType.DMA((1, n)),
            pltpu.SemaphoreType.DMA((1, n)),
            pltpu.SemaphoreType.DMA((groups,)),
            pltpu.SemaphoreType.DMA((groups,)),
        ],
        compiler_params=pltpu.CompilerParams(collective_id=1, has_side_effects=True),
        name="share_ids",
    )(packed)


def fetch_kernel(dims, ints, eb, x_out, id_s, xs, xr, send, recv):
    n, slots, vocab_rows, tokens, row_count = dims
    turned = ints[...].astype(F32).T.astype(jnp.int32)
    id_s[...] = turned[: n * slots, 0:1]
    slot_col = turned[:tokens, 1:2]
    links = Links(n, send, recv)
    me = links.me
    group = rows_at_once(n, slots)
    chunk = group * slots
    pl.semaphore_wait(links.greet(), n - 1)

    def look(c, carry):
        ids = id_s[pl.ds(pl.multiple_of(c * chunk, chunk), chunk), :]

        def add(i, start, size, acc):
            hit = (lanes((chunk, size)) + start == ids).astype(F32).astype(LOW)
            return acc + dot_nn(hit, eb[pl.ds(start, size), :])

        found = tiles_of(vocab_rows, add, jnp.zeros((chunk, D), F32))
        xs[pl.ds(c * group, group)] = found.astype(LOW).reshape(group, slots, D)
        return carry

    lax.fori_loop(0, n // group, look, 0)
    links.deal(0, xs, xr)
    xr[me] = xs[me]
    links.arrive(0, xr)
    x = jnp.zeros((tokens, D), F32)
    for c in range(n // group):
        hit = (lanes((tokens, chunk)) + c * chunk == slot_col).astype(F32).astype(LOW)
        x = x + dot_nn(hit, xr[c * group : (c + 1) * group].reshape(chunk, D))
    x_out[...] = x.astype(LOW)
    links.sent(0, xs)


def fetch(n, slots, sizes, ints, embed_low):
    vmem = pl.BlockSpec(memory_space=pltpu.VMEM)
    vocab_rows = embed_low.shape[0]
    return pl.pallas_call(
        functools.partial(fetch_kernel, (n, slots, vocab_rows) + sizes),
        out_shape=jax.ShapeDtypeStruct((sizes[0], D), LOW),
        in_specs=[vmem] * 2,
        out_specs=vmem,
        scratch_shapes=[
            pltpu.VMEM((n * slots, 1), jnp.int32),
            pltpu.VMEM((n, slots, D), LOW),
            pltpu.VMEM((n, slots, D), LOW),
            pltpu.SemaphoreType.DMA((1, n)),
            pltpu.SemaphoreType.DMA((1, n)),
        ],
        compiler_params=pltpu.CompilerParams(
            collective_id=2, has_side_effects=True, vmem_limit_bytes=40 * 1024 * 1024
        ),
        name="fetch_rows",
    )(ints, embed_low)


def step_kernel(
    dims,
    ints, vec, x_low, eb_in, attn_in, expw_in,
    dembed_out, dattn_out, dexp_out, dvec_out, loss_out, norm_out, factor_out,
    eb, attn, expw, xs, gr, ball, ys, yr, rows, tops, drs, drr, dyall, dbs, dbr,
    q_all, pas, par, middle_all, branch_all, dq_all, dss, dsr, dvec, sums, logit_s, dlog_s, pre_s, hid_s, dpre_s, flip_s, tile_s, part_s, hit_s,
    send, recv, out_sem, load_sem,
):
    n, slots, vocab, vocab_rows, hidden, tokens, row_count = dims
    all_rows = n * row_count
    wide = HEADS * row_count
    shard = D // n
    row_total = float(all_rows)
    scale = 2.0 * D ** (-0.5)
    factor_qk = HEAD_DIM ** (-0.5)
    links = Links(n, send, recv)
    me = links.me
    spread, deal, arrive, sent = links.spread, links.deal, links.arrive, links.sent
    relay, relayed = links.relay, links.relayed
    tiled = functools.partial(tiles_of, vocab_rows)
    loads = [
        pltpu.make_async_copy(source, target, load_sem.at[i])
        for i, (source, target) in enumerate(((attn_in, attn), (expw_in, expw), (eb_in, eb)))
    ]
    for load in loads:
        load.start()

    def added(buffer):
        total = buffer[0].astype(F32)
        for j in range(1, n):
            total = total + buffer[j].astype(F32)
        return total

    pl.semaphore_wait(links.greet(), n - 1)
    group = rows_at_once(n, slots)
    chunk = group * slots
    x = x_low[...].astype(F32)
    id_lane, slot_lane, pick_lane = ints[0:1, : n * slots], ints[1:2, :tokens], ints[2:3, :row_count]
    seg_lane, target_lane = ints[4:5, :tokens], ints[7:8, : 2 * all_rows]
    turned = ints[...].astype(F32).T.astype(jnp.int32)
    pick_col, seg_rows = turned[:row_count, 2:3], turned[:row_count, 3:4]
    route_col, route_all = turned[:row_count, 5:6], turned[:all_rows, 6:7]

    gain_a, gain_b, gain_c, gain_d = (vec[i : i + 1, :] for i in range(4))
    x_factor = norm_factor(x)
    a = (x * x_factor * gain_a).astype(LOW)
    pick = (lanes((row_count, tokens)) == pick_col).astype(F32).astype(LOW)
    x_rows = dot_nn(pick, x_low[...])
    a_rows = dot_nn(pick, a).astype(LOW)
    loads[0].wait()
    q = dot_nn(a_rows, attn[0]).astype(LOW)
    k = dot_nn(a, attn[1]).astype(LOW)
    v = dot_nn(a, attn[2]).astype(LOW)
    head_mask = (
        lax.shift_right_logical(lanes((HEADS, row_count, D)), HEAD_DIM.bit_length() - 1)
        == lax.broadcasted_iota(jnp.int32, (HEADS, row_count, D), 0)
    )

    def widen(low_rows):
        return (
            jnp.where(head_mask, low_rows.astype(F32)[None], 0.0).reshape(wide, D).astype(LOW)
        )

    def narrow(values):
        return jnp.sum(jnp.where(head_mask, values.reshape(HEADS, row_count, D), 0.0), axis=0)

    q_wide = widen(q)
    scores = dot_nt(q_wide, k) * factor_qk
    allowed = (lanes((row_count, tokens)) <= pick_col) & (seg_lane == seg_rows)
    scores = jnp.where(
        allowed[None], scores.reshape(HEADS, row_count, tokens), -1e30
    ).reshape(wide, tokens)
    exponent = jnp.exp(scores - jnp.max(scores, axis=-1, keepdims=True))
    probs = exponent / jnp.sum(exponent, axis=-1, keepdims=True)
    probs_low = probs.astype(LOW)
    o = narrow(dot_nn(probs_low, v)).astype(LOW)
    x_attn = x_rows + ATTN_GAIN * dot_nn(o, attn[3])

    b_factor = norm_factor(x_attn)
    b = x_attn * b_factor * gain_b
    ball[me] = b.astype(LOW)
    spread(B_ROWS, ball)
    router_rows = [vec[4 + e : 5 + e, :] for e in range(EXPERTS)]
    router_logits = [jnp.sum(b * row, axis=-1, keepdims=True) for row in router_rows]
    highest = router_logits[0]
    for value in router_logits[1:]:
        highest = jnp.maximum(highest, value)
    router_exp = [jnp.exp(value - highest) for value in router_logits]
    router_sum = sum(router_exp[1:], router_exp[0])
    router_probs = [value / router_sum for value in router_exp]
    chosen = [(route_col == e).astype(F32) for e in range(EXPERTS)]
    gate = sum([p * c for p, c in zip(router_probs[1:], chosen[1:])], router_probs[0] * chosen[0])
    q_all[me] = q
    a_turned = a.astype(F32).T.astype(LOW)
    eye = (sublanes((row_count, row_count)) == lanes((row_count, row_count))).astype(F32).astype(LOW)
    flipped = lambda low_rows: dot_tn(low_rows, eye)
    pas[:, :, 0:wide] = dot_nt(a_turned, probs_low).reshape(n, shard, wide).astype(LOW)
    pas[:, :, wide : wide + row_count] = flipped(a_rows).reshape(n, shard, row_count).astype(LOW)
    pas[:, :, wide + row_count :] = flipped(o).reshape(n, shard, row_count).astype(LOW)
    arrive(B_ROWS, ball)
    loads[1].wait()
    b_all = ball[...].reshape(all_rows, D)
    y_part = jnp.zeros((all_rows, D), F32)
    for e in range(EXPERTS):
        pre = dot_nn(b_all, expw[e, 0])
        pre_s[e] = pre
        hid = jnp.where(route_all == e, gelu_of(pre), 0.0).astype(LOW)
        hid_s[e] = hid
        y_part = y_part + dot_nt(hid, expw[e, 1])
    ys[...] = y_part.astype(LOW).reshape(n, row_count, D)
    deal(Y_PART, ys, yr)
    yr[me] = ys[me]
    arrive(Y_PART, yr)
    y = added(yr)
    z = x_attn + gate * y

    z_factor = norm_factor(z)
    first = (z * z_factor * gain_c).astype(LOW)
    middle = dot_nn(first, attn[4])
    middle_factor = norm_factor(middle)
    rows[me, 0] = first
    rows[me, 1] = (middle * middle_factor * gain_d).astype(LOW)
    relay(HEAD_ROWS, rows)
    relayed(HEAD_ROWS, rows)
    deal(P_A, pas, par)
    par[me] = pas[me]
    loads[2].wait()
    loss_rows = 2 * all_rows
    head_rows = rows[...].reshape(loss_rows, D)

    def target_hit(start, size):
        return sublanes((size, loss_rows)) + start == target_lane

    def logits_tile(i, start, size, carry):
        top, total, at_target = carry
        value = dot_nt(eb[pl.ds(start, size), :], head_rows) * scale
        if vocab_rows != vocab:
            value = jnp.where(sublanes((size, loss_rows)) + start < vocab, value, -1e30)
        logit_s[pl.ds(start, size), :] = value
        hit = target_hit(start, size)
        at_target = at_target + jnp.sum(jnp.where(hit, value, 0.0), axis=0, keepdims=True)
        new_top = jnp.maximum(top, jnp.max(value, axis=0, keepdims=True))
        total = total * jnp.exp(top - new_top) + jnp.sum(
            jnp.exp(value - new_top), axis=0, keepdims=True
        )
        return new_top, total, at_target

    nothing = jnp.zeros((1, loss_rows), F32)
    top, total, at_target = tiled(logits_tile, (nothing - 1e30, nothing, nothing))
    place = sublanes((8, loss_rows))
    tops[me] = jnp.where(
        place == 0, top, jnp.where(place == 1, total, jnp.where(place == 2, at_target, 0.0))
    )
    spread(TOPS, tops)
    arrive(TOPS, tops)
    relay(Q_ROWS, q_all)
    top = tops[0, 0:1]
    for j in range(1, n):
        top = jnp.maximum(top, tops[j, 0:1])
    total, at_target = nothing, nothing
    for j in range(n):
        total = total + tops[j, 1:2] * jnp.exp(tops[j, 0:1] - top)
        at_target = at_target + tops[j, 2:3]
    logsum = top + jnp.log(total)
    is_first = lax.rem(lanes((1, loss_rows)), 2 * row_count) < row_count
    weight = jnp.where(is_first, 1.0, SECOND_WEIGHT) / row_total
    loss = jnp.sum(weight * (logsum - at_target), axis=-1, keepdims=True)
    loss_out[...] = loss

    def dlogits_tile(i, start, size, acc):
        soft = jnp.exp(logit_s[pl.ds(start, size), :] - logsum)
        low = ((soft - target_hit(start, size).astype(F32)) * weight).astype(LOW)
        dlog_s[pl.ds(start, size), :] = low
        return acc + dot_tn(low, eb[pl.ds(start, size), :])

    drows = tiled(dlogits_tile, jnp.zeros((loss_rows, D), F32)) * scale
    drs[...] = drows.astype(LOW).reshape(n, 2 * row_count, D)
    deal(D_ROWS, drs, drr)
    drr[me] = drs[me]
    arrive(D_ROWS, drr)
    drow = added(drr)
    dmiddle, gain_mtp = norm_grad(middle, middle_factor, gain_d, drow[row_count:])
    dmiddle_low = dmiddle.astype(LOW)
    dfirst = drow[:row_count] + dot_nt(dmiddle_low, attn[4])
    dz, gain_final = norm_grad(z, z_factor, gain_c, dfirst)

    dgate = jnp.sum(dz * y, axis=-1, keepdims=True)
    dyall[me] = (gate * dz).astype(LOW)
    spread(DY_ROWS, dyall)
    arrive(DY_ROWS, dyall)
    middle_all[me] = dmiddle_low
    relay(MIDDLE_ROWS, middle_all)
    dy_all = dyall[...].reshape(all_rows, D)
    db_part = jnp.zeros((all_rows, D), F32)
    for e in range(EXPERTS):
        dhid = dot_nn(dy_all, expw[e, 1])
        slope = jnp.where(route_all == e, gelu_slope(pre_s[e]), 0.0)
        dpre = (slope * dhid).astype(LOW)
        dpre_s[e] = dpre
        db_part = db_part + dot_nt(dpre, expw[e, 0])
    dbs[...] = db_part.astype(LOW).reshape(n, row_count, D)
    deal(DB_PART, dbs, dbr)
    dbr[me] = dbs[me]
    squares = jnp.zeros((1, D), F32)

    def squared(values):
        return jnp.sum(values * values, axis=0, keepdims=True)

    hidden_squares = jnp.zeros((1, hidden), F32)
    for e in range(EXPERTS):
        up = dot_tn(b_all, dpre_s[e])
        down = dot_tn(dy_all, hid_s[e])
        dexp_out[e, 0] = up.astype(LOW)
        dexp_out[e, 1] = down.astype(LOW)
        hidden_squares = hidden_squares + squared(up) + squared(down)
    arrive(DB_PART, dbr)
    prob_grads = [c * dgate for c in chosen]
    mixed = sum([p * g for p, g in zip(router_probs[1:], prob_grads[1:])], router_probs[0] * prob_grads[0])
    dlogits = [p * (g - mixed) for p, g in zip(router_probs, prob_grads)]
    drouter = [jnp.sum(g * b, axis=0, keepdims=True) for g in dlogits]
    dnormed = added(dbr)
    for g, row in zip(dlogits, router_rows):
        dnormed = dnormed + g * row
    dx_part, gain_ffn = norm_grad(x_attn, b_factor, gain_b, dnormed)
    dx_attn = dz + dx_part

    dbranch = dx_attn.astype(LOW)
    branch_all[me] = dbranch
    relay(BRANCH_ROWS, branch_all)
    do = (ATTN_GAIN * dot_nt(dbranch, attn[3])).astype(LOW)
    do_wide = widen(do)
    dprobs = dot_nt(do_wide, v)
    dscores = (probs * (dprobs - jnp.sum(probs * dprobs, axis=-1, keepdims=True))).astype(LOW)
    dq = (narrow(dot_nn(dscores, k)) * factor_qk).astype(LOW)
    dq_all[me] = dq
    relay(DQ_ROWS, dq_all)
    dk = (dot_tn(dscores, q_wide) * factor_qk).astype(LOW)
    dv = dot_tn(probs_low, do_wide).astype(LOW)
    dinput = dot_nt(dk, attn[1]) + dot_nt(dv, attn[2])
    dx, gain_attn = norm_grad(x, x_factor, gain_a, dinput)
    row_back, gain_more = norm_grad(x_rows, norm_factor(x_rows), gain_a, dot_nt(dq, attn[0]))
    spots = (sublanes((tokens, row_count)) == pick_lane).astype(F32)
    dx = dx + lax.dot_general(
        spots, row_back + dx_attn, (((1,), (0,)), ((), ())), precision=HIGH,
        preferred_element_type=F32,
    )
    dx_low = dx.astype(LOW)
    for c in range(n // group):
        hit = (sublanes((chunk, tokens)) + c * chunk == slot_lane).astype(F32).astype(LOW)
        xs[c * group : (c + 1) * group] = dot_nn(hit, dx_low).astype(LOW).reshape(group, slots, D)
    deal(G_OUT, xs, gr)
    gr[me] = xs[me]
    line = sublanes((8, D))
    shares = jnp.zeros((8, D), F32)
    for i, value in enumerate([gain_attn + gain_more, gain_ffn, gain_final, gain_mtp] + drouter):
        shares = jnp.where(line == i, value, shares)
    dvec[me] = shares
    relay(D_VEC, dvec)
    dss[...] = dot_nt(a_turned, dscores).reshape(n, shard, wide).astype(LOW)
    deal(DS_A, dss, dsr)
    dsr[me] = dss[me]

    mine = pl.ds(pl.multiple_of(me * shard, 8), shard)

    def own_slices(start, right):
        total = jnp.zeros((shard, D), F32)
        for j in range(n):
            total = total + dot_nn(par[j, :, start : start + row_count], right[j])
        return total

    def own_rows(left, right):
        flip_s[...] = left.astype(F32).reshape(all_rows, D).T
        return dot_nn(flip_s[mine, :].astype(LOW), right.reshape(all_rows, D))

    def keep(i, part):
        dattn_out[i] = part.astype(LOW)
        return squared(part)

    arrive(P_A, par)
    relayed(MIDDLE_ROWS, middle_all)
    squares = squares + keep(4, own_rows(rows[:, 0], middle_all[...]))
    relayed(BRANCH_ROWS, branch_all)
    squares = squares + keep(3, ATTN_GAIN * own_slices(wide + row_count, branch_all))
    do_all = ATTN_GAIN * dot_nt(branch_all[...].reshape(all_rows, D), attn[3])
    dvalue = jnp.zeros((shard, D), F32)
    for j in range(n):
        do_one = do_all[j * row_count : (j + 1) * row_count].astype(LOW)
        dvalue = dvalue + dot_nn(par[j, :, 0:wide], widen(do_one))
    squares = squares + keep(2, dvalue)

    def ready_tile(i, start, size, carry):
        part_s[pl.ds(start, size), :] = scale * dot_nn(dlog_s[pl.ds(start, size), :], head_rows)
        hit = (sublanes((size, n * slots)) + start == id_lane).astype(F32)
        hit_s[pl.ds(start, size), :] = hit.astype(LOW)
        return carry

    tiled(ready_tile, 0)
    arrive(G_OUT, gr)
    whole = vocab_rows // TILE

    def leave(i, start, size):
        slot = lax.rem(i, 2)
        return pltpu.make_async_copy(
            tile_s.at[slot, pl.ds(0, size)], dembed_out.at[pl.ds(start, size)], out_sem.at[slot]
        )

    def dembed_tile(i, start, size, acc):
        value = part_s[pl.ds(start, size), :] + dot_nn(
            hit_s[pl.ds(start, size), :], gr[...].reshape(n * slots, D)
        )

        def free():
            leave(i - 2, start - 2 * TILE, TILE).wait()

        if isinstance(i, int):
            if i >= 2:
                free()
        else:
            pl.when(i >= 2)(free)
        tile_s[lax.rem(i, 2), pl.ds(0, size)] = value.astype(LOW)
        leave(i, start, size).start()
        return acc + squared(value)

    squares = tiled(dembed_tile, squares)
    relayed(Q_ROWS, q_all)
    relayed(DQ_ROWS, dq_all)
    squares = squares + keep(0, own_slices(wide, dq_all))
    arrive(DS_A, dsr)
    dkey = jnp.zeros((shard, D), F32)
    for j in range(n):
        dkey = dkey + dot_nn(dsr[j], widen(q_all[j]))
    squares = squares + keep(1, dkey * factor_qk)
    tiles = [(i, i * TILE, TILE) for i in range(whole)]
    if vocab_rows % TILE:
        tiles.append((whole, whole * TILE, vocab_rows % TILE))
    total_squares = jnp.sum(squares, axis=-1, keepdims=True) + jnp.sum(
        hidden_squares, axis=-1, keepdims=True
    )
    sums[me] = jnp.broadcast_to(total_squares, (8, 128))
    spread(SQUARES, sums)
    relayed(D_VEC, dvec)
    arrive(SQUARES, sums)
    shared = added(dvec)
    dvector = shared[0 : 4 + EXPERTS]
    dvec_out[...] = dvector
    own = jnp.sum(squared(dvector), axis=-1, keepdims=True)
    norm = jnp.sqrt(added(sums)[0:1, 0:1] + own)
    norm_out[...] = norm
    factor_out[...] = jnp.minimum(1.0, 0.05 / math.sqrt(row_total) / norm)
    for i, start, size in tiles[-2:]:
        leave(i, start, size).wait()
    for which, source in (
        (B_ROWS, ball), (Y_PART, ys), (TOPS, tops), (D_ROWS, drs), (DY_ROWS, dyall),
        (DB_PART, dbs), (P_A, pas), (DS_A, dss), (G_OUT, xs), (SQUARES, sums),
    ):
        sent(which, source)
    for which, source in (
        (HEAD_ROWS, rows), (Q_ROWS, q_all), (MIDDLE_ROWS, middle_all),
        (BRANCH_ROWS, branch_all), (DQ_ROWS, dq_all), (D_VEC, dvec),
    ):
        links.relay_sent(which, source)


def run_step(n, slots, vocab, sizes, ints, vec, x_low, embed_low, attn_low, expert_low):
    vocab_rows = embed_low.shape[0]
    row_count = sizes[1]
    hidden = expert_low.shape[3]
    shard = D // n
    all_rows = n * row_count
    wide = HEADS * row_count
    vmem = pl.BlockSpec(memory_space=pltpu.VMEM)
    anywhere = pl.BlockSpec(memory_space=pl.ANY)
    low = lambda *shape: pltpu.VMEM(shape, LOW)
    wide_float = lambda *shape: pltpu.VMEM(shape, F32)
    outs = pl.pallas_call(
        functools.partial(step_kernel, (n, slots, vocab, vocab_rows, hidden) + sizes),
        out_shape=(
            jax.ShapeDtypeStruct((vocab_rows, D), LOW),
            jax.ShapeDtypeStruct((5, shard, D), LOW),
            jax.ShapeDtypeStruct((EXPERTS, 2, D, hidden), LOW),
            jax.ShapeDtypeStruct((4 + EXPERTS, D), F32),
            jax.ShapeDtypeStruct((1, 1), F32),
            jax.ShapeDtypeStruct((1, 1), F32),
            jax.ShapeDtypeStruct((1, 1), F32),
        ),
        in_specs=[vmem] * 3 + [anywhere] * 3,
        out_specs=(anywhere, vmem, vmem, vmem, vmem, vmem, vmem),
        scratch_shapes=[
            low(vocab_rows, D), low(5, D, D), low(EXPERTS, 2, D, hidden),
            low(n, slots, D), low(n, slots, D),
            low(n, row_count, D), low(n, row_count, D), low(n, row_count, D),
            low(n, 2, row_count, D), wide_float(n, 8, 2 * all_rows),
            low(n, 2 * row_count, D), low(n, 2 * row_count, D),
            low(n, row_count, D), low(n, row_count, D), low(n, row_count, D),
            low(n, row_count, D), low(n, shard, wide + 2 * row_count),
            low(n, shard, wide + 2 * row_count),
            low(n, row_count, D), low(n, row_count, D), low(n, row_count, D),
            low(n, shard, wide), low(n, shard, wide),
            wide_float(n, 8, D), wide_float(n, 8, 128),
            wide_float(vocab_rows, 2 * all_rows), low(vocab_rows, 2 * all_rows),
            wide_float(EXPERTS, all_rows, hidden), low(EXPERTS, all_rows, hidden),
            low(EXPERTS, all_rows, hidden), wide_float(D, all_rows), low(2, TILE, D),
            wide_float(vocab_rows, D), low(vocab_rows, n * slots),
            pltpu.SemaphoreType.DMA((EXCHANGES, n)),
            pltpu.SemaphoreType.DMA((EXCHANGES, n)),
            pltpu.SemaphoreType.DMA((2,)),
            pltpu.SemaphoreType.DMA((3,)),
        ],
        compiler_params=pltpu.CompilerParams(
            collective_id=3, has_side_effects=True, vmem_limit_bytes=60 * 1024 * 1024
        ),
        name="inner_step",
    )(ints, vec, x_low, embed_low, attn_low, expert_low)
    return (outs[0][:vocab],) + outs[1:]


def sum_kernel(shapes, *refs):
    count = len(shapes)
    values, vector, refs = refs[:count], refs[count], refs[count + 1 :]
    totals, vector_total, refs = refs[:count], refs[count], refs[count + 1 :]
    helds, first_ins, second_ins, rests = (refs[i * count : (i + 1) * count] for i in range(4))
    flat, *sems = refs[4 * count :]
    one_s, one_r, two_s, two_r, three_s, three_r, four_s, four_r, rest_s, rest_r = sems
    group = lax.axis_index("grp")
    width = D // 2
    bits = (lax.rem(group, 2), lax.div(group, 2))
    flip = lambda bit: group + (1 - 2 * bits[bit]) * (1 + bit)
    barrier = pltpu.get_barrier_semaphore()
    for k in range(1, 4):
        pl.semaphore_signal(
            barrier, inc=1, device_id={"grp": lax.rem(group + k, 4)}, device_id_type=MESH
        )
    pl.semaphore_wait(barrier, 3)
    units = [
        (array, side, piece, piece * 2 + side)
        for array, (rows, quarter, pieces) in enumerate(shapes)
        for piece in range(pieces)
        for side in range(2)
    ]

    def place(u, first_bit, second_bit):
        array, side, piece, slot = units[u]
        rows, quarter, pieces = shapes[array]
        size = quarter // pieces
        owner = first_bit + 2 * second_bit if side == 0 else second_bit + 2 * first_bit
        start = pl.multiple_of((owner * pieces + piece) * size, 16)
        return pl.ds(start, size), pl.ds(side * width, width)

    def copy(source, target, send, recv, peer):
        return pltpu.make_async_remote_copy(
            src_ref=source, dst_ref=target, send_sem=send, recv_sem=recv,
            device_id={"grp": peer}, device_id_type=MESH,
        )

    def stage_one(u, turn):
        array, side, piece, slot = units[u]
        here, there = bits[side], bits[1 - side]
        out = place(u, 1 - here, there if turn else 1 - there)
        return copy(
            values[array].at[out], first_ins[array].at[slot, turn],
            one_s.at[u, turn], one_r.at[u, turn], flip(side),
        )

    def stage_two(u):
        array, side, piece, slot = units[u]
        return copy(
            helds[array].at[slot, 0], second_ins[array].at[slot], two_s.at[u], two_r.at[u], flip(1 - side)
        )

    def stage_three(u, other=False):
        array, side, piece, slot = units[u]
        there = bits[1 - side]
        block = totals[array].at[place(u, bits[side], 1 - there if other else there)]
        return copy(block, block, three_s.at[u], three_r.at[u], flip(1 - side))

    def stage_four(u, turn, other=False):
        array, side, piece, slot = units[u]
        here, there = bits[side], bits[1 - side]
        block = totals[array].at[
            place(u, 1 - here if other else here, there if turn == 0 else 1 - there)
        ]
        return copy(block, block, four_s.at[u, turn], four_r.at[u, turn], flip(side))

    flat[group] = vector[...]
    smalls = [(count, flat)]
    for array, (rows, quarter, pieces) in enumerate(shapes):
        spare = rows - 4 * quarter
        if spare:
            rests[array][group, 0:spare] = values[array][4 * quarter : rows]
            smalls.append((array, rests[array]))

    def small(which, buffer, k, peer, origin):
        return copy(
            buffer.at[origin], buffer.at[origin], rest_s.at[which, k], rest_r.at[which, origin], peer
        )

    every = range(len(units))
    for turn in range(2):
        for u in every:
            stage_one(u, turn).start()
    for which, buffer in smalls:
        for k in range(1, 4):
            small(which, buffer, k, lax.rem(group + k, 4), group).start()
    for turn in range(2):
        for u in every:
            array, side, piece, slot = units[u]
            there = bits[1 - side]
            stage_one(u, turn).wait_recv()
            mine = place(u, bits[side], there if turn else 1 - there)
            helds[array][slot, turn] = (
                values[array][mine].astype(F32) + first_ins[array][slot, turn].astype(F32)
            ).astype(LOW)
            if turn == 0:
                stage_two(u).start()
    for u in every:
        array, side, piece, slot = units[u]
        stage_two(u).wait_recv()
        mine = place(u, bits[side], bits[1 - side])
        totals[array][mine] = (
            helds[array][slot, 1].astype(F32) + second_ins[array][slot].astype(F32)
        ).astype(LOW)
        stage_three(u).start()
        stage_four(u, 0).start()
    for u in every:
        stage_three(u, True).wait_recv()
        stage_four(u, 1).start()
    for which, buffer in smalls:
        for k in range(1, 4):
            origin = lax.rem(group + k, 4)
            small(which, buffer, k, origin, origin).wait_recv()
    added = lambda buffer: (buffer[0].astype(F32) + buffer[1].astype(F32)) + (
        buffer[2].astype(F32) + buffer[3].astype(F32)
    )
    vector_total[...] = added(flat)
    for array, buffer in smalls[1:]:
        rows, quarter, pieces = shapes[array]
        totals[array][4 * quarter : rows] = added(buffer)[0 : rows - 4 * quarter].astype(LOW)
    for u in every:
        for turn in range(2):
            stage_four(u, turn, True).wait_recv()
    for u in every:
        stage_two(u).wait_send()
        stage_three(u).wait_send()
        for turn in range(2):
            stage_one(u, turn).wait_send()
            stage_four(u, turn).wait_send()
    for which, buffer in smalls:
        for k in range(1, 4):
            small(which, buffer, k, lax.rem(group + k, 4), group).wait_send()


def sum_over_groups(values, vector):
    shapes = []
    for value in values:
        rows = value.shape[0]
        quarter = rows // 64 * 16
        shapes.append((rows, quarter, 2 if quarter % 32 == 0 and quarter > 256 else 1))
    units = sum(2 * pieces for rows, quarter, pieces in shapes)
    vmem = pl.BlockSpec(memory_space=pltpu.VMEM)
    scratch = []
    for lead in ((2,), (2,), ()):
        for rows, quarter, pieces in shapes:
            scratch.append(pltpu.VMEM((2 * pieces,) + lead + (quarter // pieces, D // 2), LOW))
    for rows, quarter, pieces in shapes:
        spare = -(-(rows - 4 * quarter) // 16) * 16
        scratch.append(pltpu.VMEM((4, max(spare, 16), D), LOW))
    dma = pltpu.SemaphoreType.DMA
    count = len(values)
    *totals, vector_total = pl.pallas_call(
        functools.partial(sum_kernel, tuple(shapes)),
        out_shape=[jax.ShapeDtypeStruct(value.shape, LOW) for value in values]
        + [jax.ShapeDtypeStruct(vector.shape, F32)],
        in_specs=[vmem] * (count + 1),
        out_specs=[vmem] * (count + 1),
        scratch_shapes=scratch
        + [
            pltpu.VMEM((4,) + vector.shape, F32),
            dma((units, 2)), dma((units, 2)), dma((units,)), dma((units,)), dma((units,)),
            dma((units,)), dma((units, 2)), dma((units, 2)), dma((count + 1, 4)), dma((count + 1, 4)),
        ],
        compiler_params=pltpu.CompilerParams(
            collective_id=4, has_side_effects=True, vmem_limit_bytes=52 * 1024 * 1024
        ),
        cost_estimate=pl.CostEstimate(flops=0, bytes_accessed=300_000_000, transcendentals=0),
        name="sum_groups",
    )(*values, vector)
    return totals, vector_total


def prepare(n, slots, vocab, tokens, routes, segments, loss_pos):
    steps, count = tokens.shape
    start = lax.axis_index("fsdp") * vocab
    row_count = loss_pos.shape[1]
    owner = tokens // vocab
    places = jnp.arange(count)
    earlier = places[None, None, :] < places[None, :, None]
    same = tokens[:, :, None] == tokens[:, None, :]
    first = jnp.logical_not(jnp.any(same & earlier, axis=2))
    same_owner = owner[:, :, None] == owner[:, None, :]
    rank = jnp.sum((same_owner & earlier & first[:, None, :]).astype(jnp.int32), axis=2)
    own_slot = owner * slots + rank
    slot = jnp.sum(jnp.where(same & first[:, None, :], own_slot[:, None, :], 0), axis=2)
    at_slot = (own_slot[:, :, None] == jnp.arange(n * slots)[None, None, :]) & first[:, :, None]
    ids = jnp.sum(jnp.where(at_slot, tokens[:, :, None] + 1, 0), axis=1) - 1
    picked = loss_pos[:, :, None] == places[None, None, :]
    shifted = lambda by: jnp.sum(
        jnp.where(loss_pos[:, :, None] + by == places[None, None, :], tokens[:, None, :], 0), axis=2
    )
    row_routes = jnp.sum(jnp.where(picked, routes[:, None, :], 0), axis=2)
    row_segs = jnp.sum(jnp.where(picked, segments[:, None, :], 0), axis=2)
    most = jnp.broadcast_to(jnp.max(jnp.where(first, rank, 0)), (steps, 128))
    filler = jnp.zeros((steps, -(n * slots + 3 * row_count) % 128), jnp.int32)
    packed = jnp.concatenate([ids, row_routes, shifted(1), shifted(2), filler, most], axis=1)
    everyone, worst = share(n, packed)
    fits = worst[0, 127] < slots
    wanted = lax.dynamic_slice_in_dim(everyone, lax.axis_index("fsdp") * slots, slots, axis=2) - start
    after = n * slots
    rows = lambda part: jnp.swapaxes(part, 0, 1).reshape(steps, -1)
    lines = [
        rows(wanted),
        slot,
        loss_pos,
        row_segs,
        segments,
        row_routes,
        rows(everyone[:, :, after : after + row_count]),
        rows(everyone[:, :, after + row_count : after + 3 * row_count]) - start,
    ]
    longest = -(-max(line.shape[1] for line in lines) // 128) * 128
    fill = lambda line: jnp.pad(line, ((0, 0), (0, longest - line.shape[1])))
    result = jnp.stack([fill(line) for line in lines], axis=1)
    return result, fits


def general_step(tokens, routes, segments, loss_pos, all_ids, inner_step, weights):
    embed_w, attn_w, expert_w, vector_w = weights
    vocab_shard = embed_w.shape[0]
    vocab_start = lax.axis_index("fsdp") * vocab_shard
    row_total = lax.axis_size("fsdp") * loss_pos.shape[2]
    logit_scale = 2.0 * D ** (-0.5)
    vocab_places = jnp.arange(vocab_shard)
    head_weights = jnp.array([1.0, SECOND_WEIGHT], jnp.float32)
    embed_low = embed_w.astype(jnp.bfloat16)
    attn_low = lax.all_gather(attn_w.astype(jnp.bfloat16), "fsdp", axis=1, tiled=True)
    expert_low = expert_w.astype(jnp.bfloat16)
    ids_group = all_ids[inner_step]
    ids_local = tokens[inner_step, 0]
    seg_ids = segments[inner_step, 0]
    route_ids = routes[inner_step, 0, :, 0]
    pick_ids = loss_pos[inner_step, 0]
    chosen = ids_group - vocab_start
    inside = (chosen >= 0) & (chosen < vocab_shard)
    looked = jnp.take(embed_low, jnp.clip(chosen, 0, vocab_shard - 1), axis=0).astype(
        jnp.float32
    )
    x_embed = lax.psum_scatter(
        jnp.where(inside[:, None], looked, 0.0).astype(jnp.bfloat16),
        "fsdp",
        scatter_dimension=0,
        tiled=True,
    ).astype(jnp.float32)
    x_attn, kept = rows_forward(attn_low, vector_w, x_embed, seg_ids, pick_ids)
    b, b_factor = norm_apply(x_attn, vector_w[1])
    router_probs = jax.nn.softmax(jnp.dot(b, vector_w[4:].T, precision=HIGH), axis=-1)
    row_routes = route_ids[pick_ids]
    onehot = (row_routes[:, None] == jnp.arange(EXPERTS)[None, :]).astype(jnp.float32)
    gating = jnp.sum(router_probs * onehot, axis=1)
    b_all = gather_rows(b.astype(jnp.bfloat16))
    routes_all = gather_rows(row_routes)
    route_mask = routes_all[None, :, None] == jnp.arange(EXPERTS)[:, None, None]
    hidden_pre = jnp.einsum("cd,edf->ecf", b_all, expert_low[:, 0], preferred_element_type=jnp.float32)
    hidden_act = jnp.where(route_mask, smooth_act(hidden_pre), 0.0).astype(jnp.bfloat16)
    y_part = jnp.einsum("ecf,edf->cd", hidden_act, expert_low[:, 1], preferred_element_type=jnp.float32)
    returned = scatter_rows(y_part)
    z_rows = x_attn + gating[:, None] * returned
    first_float, first_factor = norm_apply(z_rows, vector_w[2])
    first_rows = first_float.astype(jnp.bfloat16)
    middle = jnp.dot(first_rows, attn_low[4], preferred_element_type=jnp.float32)
    second_float, second_factor = norm_apply(middle, vector_w[3])
    targets = jnp.stack([ids_local[pick_ids + 1], ids_local[pick_ids + 2]])
    rows_all, targets_all = (
        lax.all_gather(
            jnp.stack([first_rows, second_float.astype(jnp.bfloat16)]),
            "fsdp",
            axis=1,
            tiled=True,
        ),
        lax.all_gather(targets, "fsdp", axis=1, tiled=True),
    )
    logits = (
        jnp.einsum("jrd,vd->jrv", rows_all, embed_low, preferred_element_type=jnp.float32)
        * logit_scale
    )
    relative = targets_all - vocab_start
    onehot_target = (vocab_places[None, None, :] == relative[:, :, None]).astype(jnp.float32)
    target_part = jnp.sum(onehot_target * logits, axis=-1)
    local_top = jnp.max(logits, axis=-1)
    local_sum = jnp.sum(jnp.exp(logits - local_top[:, :, None]), axis=-1)
    parts = lax.all_gather(jnp.stack([local_top, local_sum, target_part]), "fsdp")
    row_top = jnp.max(parts[:, 0], axis=0)
    sum_exp = jnp.sum(parts[:, 1] * jnp.exp(parts[:, 0] - row_top), axis=0)
    target_logit = jnp.sum(parts[:, 2], axis=0)
    logsum = row_top + jnp.log(sum_exp)
    loss = (jnp.sum(head_weights[:, None] * (logsum - target_logit)) / row_total)
    dlogits = (
        (jnp.exp(logits - logsum[:, :, None]) - onehot_target)
        * (head_weights / row_total)[:, None, None]
    ).astype(jnp.bfloat16)
    dembed = (
        jnp.einsum("jrv,jrd->vd", dlogits, rows_all, preferred_element_type=jnp.float32)
        * logit_scale
    )
    drows = (
        jnp.einsum("jrv,vd->jrd", dlogits, embed_low, preferred_element_type=jnp.float32)
        * logit_scale
    )
    drows_own = lax.psum_scatter(
        drows.astype(jnp.bfloat16), "fsdp", scatter_dimension=1, tiled=True
    ).astype(jnp.float32)
    dmiddle, gain_mtp = norm_back(middle, second_factor, vector_w[3], drows_own[1])
    dmiddle_low = dmiddle.astype(jnp.bfloat16)
    dsecond_proj = jnp.dot(first_rows.T, dmiddle_low, preferred_element_type=jnp.float32)
    dfirst = drows_own[0] + jnp.dot(
        dmiddle_low, attn_low[4].T, preferred_element_type=jnp.float32
    )
    dz_rows, gain_final = norm_back(z_rows, first_factor, vector_w[2], dfirst)
    dgating = jnp.sum(dz_rows * returned, axis=1)
    dy_all = gather_rows((gating[:, None] * dz_rows).astype(jnp.bfloat16))
    dy_masked = jnp.where(route_mask, dy_all[None], 0)
    down_grad = jnp.einsum("ecf,ecd->edf", hidden_act, dy_masked, preferred_element_type=jnp.float32)
    dhidden = jnp.einsum("ecd,edf->ecf", dy_masked, expert_low[:, 1], preferred_element_type=jnp.float32)
    unused, act_back = jax.vjp(smooth_act, hidden_pre)
    dhidden_pre = act_back(dhidden)[0].astype(jnp.bfloat16)
    up_grad = jnp.einsum("cd,ecf->edf", b_all, dhidden_pre, preferred_element_type=jnp.float32)
    dexpert = jnp.stack([up_grad, down_grad], axis=1)
    db_part = jnp.einsum("ecf,edf->cd", dhidden_pre, expert_low[:, 0], preferred_element_type=jnp.float32)
    dnormed = scatter_rows(db_part)
    prob_grad = onehot * dgating[:, None]
    dlogit = router_probs * (prob_grad - jnp.sum(router_probs * prob_grad, axis=1, keepdims=True))
    drouter = jnp.dot(dlogit.T, b, precision=HIGH)
    dnormed = dnormed + jnp.dot(dlogit, vector_w[4:], precision=HIGH)
    dx_part, gain_ffn = norm_back(x_attn, b_factor, vector_w[1], dnormed)
    dx_embed, dlayer, gain_attn = rows_backward(
        attn_low, vector_w, x_embed, kept, dz_rows + dx_part, pick_ids
    )
    dattn = scatter_rows(jnp.concatenate([dlayer, dsecond_proj[None]], axis=0), axis=1)
    gather_chosen = ids_group - vocab_start
    gather_inside = (gather_chosen >= 0) & (gather_chosen < vocab_shard)
    seg_index = jnp.where(gather_inside, gather_chosen, vocab_shard)
    added = jax.ops.segment_sum(
        lax.all_gather(dx_embed.astype(jnp.bfloat16), "fsdp", axis=0, tiled=True).astype(
            jnp.float32
        ),
        seg_index,
        num_segments=vocab_shard + 1,
    )
    dembed = dembed + added[:vocab_shard]
    dvector_part = jnp.concatenate(
        [jnp.stack([gain_attn, gain_ffn, gain_final, gain_mtp]), drouter], axis=0
    )
    squares = jnp.sum(dembed * dembed) + jnp.sum(dattn * dattn) + jnp.sum(dexpert * dexpert)
    dvector, squares_all = lax.psum((dvector_part, squares), "fsdp")
    return dembed, dattn, dexpert, dvector, squares_all, loss


def adam_update(weight, first_moment, second, gradient, step_float, rate_here, decay_here):
    first_new = BETA_ONE * first_moment + (1.0 - BETA_ONE) * gradient
    second_new = BETA_TWO * second + (1.0 - BETA_TWO) * gradient * gradient
    first_hat = first_new / (1.0 - BETA_ONE**step_float)
    second_hat = second_new / (1.0 - BETA_TWO**step_float)
    weight_new = weight - rate_here * (
        first_hat / (jnp.sqrt(second_hat) + ADAM_EPS) + decay_here * weight
    )
    return (weight_new, first_new, second_new)


def window(
    step,
    embedding,
    embedding_first,
    embedding_second,
    embedding_outer,
    attention,
    attention_first,
    attention_second,
    attention_outer,
    experts,
    experts_first,
    experts_second,
    experts_outer,
    vectors,
    vectors_first,
    vectors_second,
    vectors_outer,
    inner_count,
    row_total,
):
    group_count = lax.axis_size("grp")
    threshold = 0.05 / math.sqrt(row_total)
    vector_rates = jnp.where(jnp.arange(vectors.shape[0])[:, None] < 4, LR_GAIN, LR_ROUTER)
    rate_list = (LR_EMBED, LR_MATRIX, LR_MATRIX, vector_rates)
    decay_list = (DECAY, DECAY, DECAY, 0.0)
    weights_now = (embedding, attention, experts, vectors)
    first_now = (embedding_first[0], attention_first[0], experts_first[0], vectors_first[0])
    second_now = (embedding_second[0], attention_second[0], experts_second[0], vectors_second[0])
    loss_list = []
    norm_list = []
    for inner_step in range(inner_count):
        dembed, dattn, dexpert, dvector, squares_all, loss = step(inner_step, weights_now)
        loss_list.append(loss)
        norm_value = jnp.sqrt(squares_all + jnp.sum(dvector * dvector))
        norm_list.append(norm_value)
        factor = jnp.minimum(1.0, threshold / norm_value)
        gradients = (dembed * factor, dattn * factor, dexpert * factor, dvector * factor)
        step_float = float(STEP0 + inner_step + 1)
        results = [
            adam_update(
                weights_now[k],
                first_now[k],
                second_now[k],
                gradients[k],
                step_float,
                rate_list[k],
                decay_list[k],
            )
            for k in range(4)
        ]
        weights_now = tuple((element[0] for element in results))
        first_now = tuple((element[1] for element in results))
        second_now = tuple((element[2] for element in results))
    masters = (embedding, attention, experts, vectors)
    outers = (embedding_outer, attention_outer, experts_outer, vectors_outer)
    deltas = tuple((master - current for master, current in zip(masters, weights_now)))
    summed = jax.tree.map(
        lambda part: part.astype(jnp.float32), lax.psum(for_sending(deltas), "grp")
    )
    new_outer = []
    new_master = []
    for k in range(4):
        delta_mean = summed[k] / group_count
        outer_new = OUTER_MOMENTUM * outers[k] + delta_mean
        new_outer.append(outer_new)
        new_master.append(masters[k] - OUTER_RATE * (delta_mean + OUTER_MOMENTUM * outer_new))
    return (
        jnp.stack(loss_list)[None],
        jnp.stack(norm_list)[None],
        first_now[0][None],
        second_now[0][None],
        new_master[0],
        new_outer[0],
        new_master[0].astype(jnp.bfloat16),
        first_now[1][None],
        second_now[1][None],
        new_master[1],
        new_outer[1],
        new_master[1].astype(jnp.bfloat16),
        first_now[2][None],
        second_now[2][None],
        new_master[2],
        new_outer[2],
        new_master[2].astype(jnp.bfloat16),
        gradients[3][None],
        first_now[3][None],
        second_now[3][None],
        new_master[3],
        new_outer[3],
    )


def adam_quick(weight, first_moment, second, gradient, step_float, rate_here, decay_here):
    first_new = BETA_ONE * first_moment + (1.0 - BETA_ONE) * gradient
    second_new = BETA_TWO * second + (1.0 - BETA_TWO) * gradient * gradient
    first_hat = first_new * (1.0 / (1.0 - BETA_ONE**step_float))
    second_hat = second_new * (1.0 / (1.0 - BETA_TWO**step_float))
    weight_new = weight - rate_here * (
        first_hat / (jnp.sqrt(second_hat) + ADAM_EPS) + decay_here * weight
    )
    return (weight_new, first_new, second_new)


def quick_window(n, slots, sizes, steps, x_start, lows, masters, firsts, seconds, outers):
    embedding, attention, experts, vectors = masters
    vocab = embedding.shape[0]
    vector_rates = jnp.where(jnp.arange(vectors.shape[0])[:, None] < 4, LR_GAIN, LR_ROUTER)
    rate_list = (LR_EMBED, LR_MATRIX, LR_MATRIX, vector_rates)
    decay_list = (DECAY, DECAY, DECAY, 0.0)
    taken = []

    def replay(k, factors):
        state = (masters[k], firsts[k], seconds[k])
        for s, factor in enumerate(factors):
            gradient = taken[s][k].astype(jnp.float32) * factor
            state = adam_quick(
                *state, gradient, float(STEP0 + s + 1), rate_list[k], decay_list[k]
            )
        return state

    loss_list, norm_list, factor_list = [], [], []
    vector_state = (vectors, firsts[3], seconds[3])
    for s in range(steps.shape[0]):
        ints = steps[s]
        if s:
            again = lax.optimization_barrier(tuple(factor_list))
            attn_low = lax.all_gather(
                replay(1, again)[0].astype(jnp.bfloat16), "fsdp", axis=1, tiled=True
            )
            expert_low = replay(2, again)[0].astype(jnp.bfloat16)
            embed_low = padded(replay(0, again)[0].astype(jnp.bfloat16))
            x_low = fetch(n, slots, sizes, ints, embed_low)
        else:
            (embed_low, attn_low, expert_low), x_low = lows, x_start
        *grads, dvector, loss, norm_value, factor = run_step(
            n, slots, vocab, sizes, ints, vector_state[0], x_low, embed_low, attn_low, expert_low
        )
        loss, norm_value, factor = loss[0, 0], norm_value[0, 0], factor[0, 0]
        taken.append(grads)
        loss_list.append(loss)
        norm_list.append(norm_value)
        factor_list.append(factor)
        vector_gradient = dvector * factor
        vector_state = adam_quick(
            *vector_state, vector_gradient, float(STEP0 + s + 1), vector_rates, 0.0
        )
    again = lax.optimization_barrier(tuple(factor_list))
    low_delta = lambda k, state: (masters[k] - state[0]).astype(jnp.bfloat16)
    expert_state = replay(2, again)
    expert_delta = low_delta(2, expert_state)
    expert_sum = lax.psum(expert_delta, "grp")
    *again, expert_delta = lax.optimization_barrier((*again, expert_delta))
    states = [replay(0, again), replay(1, again), expert_state, vector_state]
    attn_delta = low_delta(1, states[1])
    (embed_sum, attn_sum), vector_sum = sum_over_groups(
        (low_delta(0, states[0]), attn_delta.reshape(-1, D)), vectors - vector_state[0]
    )
    sums = (embed_sum, attn_sum.reshape(attn_delta.shape), expert_sum, vector_sum)
    results = [jnp.stack(loss_list)[None], jnp.stack(norm_list)[None]]
    for k in range(4):
        delta_mean = sums[k].astype(jnp.float32) / lax.axis_size("grp")
        outer_new = OUTER_MOMENTUM * outers[k] + delta_mean
        master_new = masters[k] - OUTER_RATE * (delta_mean + OUTER_MOMENTUM * outer_new)
        if k == 3:
            results.append(vector_gradient[None])
        results += [states[k][1][None], states[k][2][None], master_new, outer_new]
        if k < 3:
            results.append(master_new.astype(jnp.bfloat16))
    return tuple(results)


def padded(embed_low):
    extra = -embed_low.shape[0] % 16
    return jnp.pad(embed_low, ((0, extra), (0, 0))) if extra else embed_low


def shards(
    tokens,
    routes,
    segments,
    loss_pos,
    embedding,
    embedding_first,
    embedding_second,
    embedding_outer,
    attention,
    attention_first,
    attention_second,
    attention_outer,
    experts,
    experts_first,
    experts_second,
    experts_outer,
    vectors,
    vectors_first,
    vectors_second,
    vectors_outer,
):
    inner_count = tokens.shape[0]
    vocab_shard = embedding.shape[0]
    n = lax.axis_size("fsdp")
    row_total = n * loss_pos.shape[2]
    slots = 48
    steps, fits = prepare(
        n, slots, vocab_shard, tokens[:, 0], routes[:, 0, :, 0], segments[:, 0], loss_pos[:, 0]
    )
    lows = (
        padded(embedding.astype(jnp.bfloat16)),
        lax.all_gather(attention.astype(jnp.bfloat16), "fsdp", axis=1, tiled=True),
        experts.astype(jnp.bfloat16),
    )
    sizes = (tokens.shape[2], loss_pos.shape[2])
    x_start = fetch(n, slots, sizes, steps[0], lows[0])
    state = (
        embedding,
        embedding_first,
        embedding_second,
        embedding_outer,
        attention,
        attention_first,
        attention_second,
        attention_outer,
        experts,
        experts_first,
        experts_second,
        experts_outer,
        vectors,
        vectors_first,
        vectors_second,
        vectors_outer,
    )

    def quick(*state):
        masters, firsts, seconds, outers = (
            [state[4 * k + part] for k in range(4)] for part in range(4)
        )
        firsts, seconds = [value[0] for value in firsts], [value[0] for value in seconds]
        return quick_window(
            n, slots, sizes, steps, x_start, lows, masters, firsts, seconds, outers
        )

    def general(*state):
        all_ids = lax.all_gather(tokens[:, 0, :], "fsdp", axis=1, tiled=True)
        step = functools.partial(general_step, tokens, routes, segments, loss_pos, all_ids)
        return window(step, *state, inner_count, row_total)

    return lax.cond(fits, quick, general, *state)


def solution(mesh):
    return jax.shard_map(
        shards,
        mesh=mesh,
        in_specs=(
            P(None, "grp", "fsdp"),
            P(None, "grp", "fsdp", None),
            P(None, "grp", "fsdp"),
            P(None, "grp", "fsdp"),
            P("fsdp", None),
            P("grp", "fsdp", None),
            P("grp", "fsdp", None),
            P("fsdp", None),
            P(None, "fsdp", None),
            P("grp", None, "fsdp", None),
            P("grp", None, "fsdp", None),
            P(None, "fsdp", None),
            P(None, None, None, "fsdp"),
            P("grp", None, None, None, "fsdp"),
            P("grp", None, None, None, "fsdp"),
            P(None, None, None, "fsdp"),
            P(),
            P("grp", None, None),
            P("grp", None, None),
            P(),
        ),
        out_specs=(
            P("grp", None),
            P("grp", None),
            P("grp", "fsdp", None),
            P("grp", "fsdp", None),
            P("fsdp", None),
            P("fsdp", None),
            P("fsdp", None),
            P("grp", None, "fsdp", None),
            P("grp", None, "fsdp", None),
            P(None, "fsdp", None),
            P(None, "fsdp", None),
            P(None, "fsdp", None),
            P("grp", None, None, None, "fsdp"),
            P("grp", None, None, None, "fsdp"),
            P(None, None, None, "fsdp"),
            P(None, None, None, "fsdp"),
            P(None, None, None, "fsdp"),
            P("grp", None, None),
            P("grp", None, None),
            P("grp", None, None),
            P(),
            P(),
        ),
        check_vma=False,
    )
```

```python
import functools
import math

import jax
import jax.numpy as jnp
from jax import lax
from jax.experimental import pallas as pl
from jax.experimental.pallas import tpu as pltpu
from jax.sharding import PartitionSpec as P

D = 768
HEADS = 12
HEAD_DIM = 64
EXPERTS = 2
STEP0 = 5
CAP = 192


HIGH = lax.Precision.HIGHEST
EPSILON = 1e-06
ATTN_GAIN = 8.0
SECOND_WEIGHT = 0.3
BETA_ONE = 0.9
BETA_TWO = 0.95
ADAM_EPS = 1e-08
DECAY = 0.1
LR_EMBED = 0.5
LR_MATRIX = 0.012
LR_GAIN = 0.3
LR_ROUTER = 0.012
OUTER_RATE = 0.7
OUTER_MOMENTUM = 0.9


def for_sending(value):

    def short(part):
        return part.astype(jnp.bfloat16) if part.dtype == jnp.float32 else part

    return jax.tree.map(short, value)


def smooth_act(values):
    return jax.nn.gelu(values, approximate=True)


def norm_apply(x, gain_row):
    factor = lax.rsqrt(jnp.mean(x * x, axis=-1, keepdims=True) + EPSILON)
    return (x * factor * gain_row, factor)


def norm_back(x, factor, gain_row, upstream):
    normed = x * factor
    gain_grad = jnp.sum(upstream * normed, axis=0)
    scaled = upstream * gain_row
    return (
        factor * (scaled - normed * jnp.mean(scaled * normed, axis=-1, keepdims=True)),
        gain_grad,
    )


def rows_forward(attn_low, vector_w, x_embed, seg_ids, pick_ids):
    a_float, a_factor = norm_apply(x_embed, vector_w[0])
    a = a_float.astype(jnp.bfloat16)
    a_rows = a[pick_ids]
    q = jnp.dot(a_rows, attn_low[0], preferred_element_type=jnp.float32).astype(jnp.bfloat16)
    k = jnp.dot(a, attn_low[1], preferred_element_type=jnp.float32).astype(jnp.bfloat16)
    v = jnp.dot(a, attn_low[2], preferred_element_type=jnp.float32).astype(jnp.bfloat16)
    places = jnp.arange(x_embed.shape[0])
    allowed = (places[None, :] <= pick_ids[:, None]) & (
        seg_ids[pick_ids][:, None] == seg_ids[None, :]
    )
    count = pick_ids.shape[0]
    head_of = jnp.arange(D) // HEAD_DIM
    head_mask = (head_of[None, None, :] == jnp.arange(HEADS)[:, None, None])
    q_wide = jnp.where(head_mask, q[None], 0).reshape(HEADS * count, D)
    scores = jnp.einsum("rd,td->rt", q_wide, k, preferred_element_type=jnp.float32) * HEAD_DIM ** (-0.5)
    allowed = jnp.tile(allowed, (HEADS, 1))
    scores = jnp.where(allowed, scores, -1e30)
    exponent = jnp.exp(scores - jnp.max(scores, axis=-1, keepdims=True))
    probs = exponent / jnp.sum(exponent, axis=-1, keepdims=True)
    spread = jnp.dot(probs.astype(jnp.bfloat16), v, preferred_element_type=jnp.float32)
    o = jnp.sum(jnp.where(head_mask, spread.reshape(HEADS, count, D), 0.0), axis=0).astype(jnp.bfloat16)
    x_attn = x_embed[pick_ids] + ATTN_GAIN * jnp.dot(o, attn_low[3], preferred_element_type=jnp.float32)
    return x_attn, (a_factor, a, a_rows, q_wide, k, v, probs, o, head_mask)


def rows_backward(attn_low, vector_w, x_embed, kept, dx_attn, pick_ids):
    a_factor, a, a_rows, q_wide, k, v, probs, o, head_mask = kept
    count = pick_ids.shape[0]
    dbranch = dx_attn.astype(jnp.bfloat16)
    dwout = ATTN_GAIN * jnp.dot(o.T, dbranch, preferred_element_type=jnp.float32)
    do = (ATTN_GAIN * jnp.dot(dbranch, attn_low[3].T, preferred_element_type=jnp.float32)).astype(jnp.bfloat16)
    do_wide = jnp.where(head_mask, do[None], 0).reshape(HEADS * count, D)
    dprobs = jnp.einsum("rd,td->rt", do_wide, v, preferred_element_type=jnp.float32)
    dscores = (probs * (dprobs - jnp.sum(probs * dprobs, axis=-1, keepdims=True))).astype(jnp.bfloat16)
    factor_qk = HEAD_DIM ** (-0.5)
    dq = jnp.dot(dscores, k, preferred_element_type=jnp.float32).reshape(HEADS, count, D)
    dq = (jnp.sum(jnp.where(head_mask, dq, 0.0), axis=0) * factor_qk).astype(jnp.bfloat16)
    dk = (jnp.dot(dscores.T, q_wide, preferred_element_type=jnp.float32) * factor_qk).astype(jnp.bfloat16)
    dv = jnp.dot(probs.astype(jnp.bfloat16).T, do_wide, preferred_element_type=jnp.float32).astype(jnp.bfloat16)
    dlayer = jnp.stack(
        [
            jnp.dot(a_rows.T, dq, preferred_element_type=jnp.float32),
            jnp.dot(a.T, dk, preferred_element_type=jnp.float32),
            jnp.dot(a.T, dv, preferred_element_type=jnp.float32),
            dwout,
        ]
    )
    places = jnp.arange(x_embed.shape[0])
    pick_mask = (places[:, None] == pick_ids[None, :]).astype(jnp.float32)
    dinput = jnp.dot(dk, attn_low[1].T, preferred_element_type=jnp.float32)
    dinput = dinput + jnp.dot(dv, attn_low[2].T, preferred_element_type=jnp.float32)
    dq_in = jnp.dot(dq, attn_low[0].T, preferred_element_type=jnp.float32)
    dinput = dinput + jnp.dot(pick_mask, dq_in, precision=HIGH)
    dx, gain_attn = norm_back(x_embed, a_factor, vector_w[0], dinput)
    return dx + jnp.dot(pick_mask, dx_attn, precision=HIGH), dlayer, gain_attn


def gather_rows(value, axis=0):
    return lax.all_gather(value, "fsdp", axis=axis, tiled=True)


def scatter_rows(value, axis=0):
    return lax.psum_scatter(
        value.astype(jnp.bfloat16), "fsdp", scatter_dimension=axis, tiled=True
    ).astype(jnp.float32)


TILE = 512
MESH = pl.DeviceIdType.MESH
F32 = jnp.float32
LOW = jnp.bfloat16
B_ROWS, Y_PART, HEAD_ROWS, TOPS, D_ROWS, DY_ROWS, DB_PART = range(7)
Q_ROWS, P_A, MIDDLE_ROWS, BRANCH_ROWS, DQ_ROWS, DS_A, G_OUT, D_VEC, SQUARES, EXCHANGES = range(7, 17)


def dot_nn(left, right):
    return lax.dot_general(left, right, (((1,), (0,)), ((), ())), preferred_element_type=F32)


def dot_nt(left, right):
    return lax.dot_general(left, right, (((1,), (1,)), ((), ())), preferred_element_type=F32)


def dot_tn(left, right):
    return lax.dot_general(left, right, (((0,), (0,)), ((), ())), preferred_element_type=F32)


def lanes(shape):
    return lax.broadcasted_iota(jnp.int32, shape, len(shape) - 1)


def sublanes(shape):
    return lax.broadcasted_iota(jnp.int32, shape, len(shape) - 2)


def norm_factor(x):
    return lax.rsqrt(jnp.mean(x * x, axis=-1, keepdims=True) + EPSILON)


def norm_grad(x, factor, gain_row, upstream):
    normed = x * factor
    scaled = upstream * gain_row
    back = factor * (scaled - normed * jnp.mean(scaled * normed, axis=-1, keepdims=True))
    return back, jnp.sum(upstream * normed, axis=0, keepdims=True)


GELU_C = math.sqrt(2.0 / math.pi)


def gelu_of(u):
    return 0.5 * u * (1.0 + jnp.tanh(GELU_C * (u + 0.044715 * (u * u * u))))


def gelu_slope(u):
    t = jnp.tanh(GELU_C * (u + 0.044715 * (u * u * u)))
    return 0.5 * (1.0 + t) + 0.5 * u * (1.0 - t * t) * GELU_C * (1.0 + 3.0 * 0.044715 * u * u)


class Links:
    def __init__(self, n, send, recv):
        self.n, self.send, self.recv = n, send, recv
        self.me = lax.axis_index("fsdp")

    def others(self, body):
        def one_step(k, carry):
            body(k, lax.rem(self.me + k, self.n))
            return carry

        lax.fori_loop(1, self.n, one_step, 0)

    def link(self, which, k, source, target, peer, origin):
        return pltpu.make_async_remote_copy(
            src_ref=source,
            dst_ref=target,
            send_sem=self.send.at[which, k],
            recv_sem=self.recv.at[which, origin],
            device_id={"fsdp": peer},
            device_id_type=MESH,
        )

    def greet(self, extra=0):
        barrier = pltpu.get_barrier_semaphore()
        self.others(
            lambda k, peer: pl.semaphore_signal(
                barrier, inc=1, device_id={"fsdp": peer}, device_id_type=MESH
            )
        )
        return barrier

    def spread(self, which, buffer):
        me = self.me
        self.others(
            lambda k, peer: self.link(which, k, buffer.at[me], buffer.at[me], peer, me).start()
        )

    def deal(self, which, source, target):
        me = self.me
        self.others(
            lambda k, peer: self.link(which, k, source.at[peer], target.at[me], peer, me).start()
        )

    def arrive(self, which, target):
        self.others(
            lambda k, peer: self.link(
                which, k, target.at[peer], target.at[peer], peer, peer
            ).wait_recv()
        )

    def sent(self, which, source):
        me = self.me
        self.others(
            lambda k, peer: self.link(
                which, k, source.at[peer], source.at[peer], peer, me
            ).wait_send()
        )

    def partners(self, body):
        def one_step(k, carry):
            body(k, lax.rem(self.me + 2 * k, self.n))
            return carry

        lax.fori_loop(1, self.n // 2, one_step, 0)

    def relay(self, which, buffer):
        me, twin = self.me, self.me + 1 - 2 * lax.rem(self.me, 2)
        self.link(which, self.n // 2, buffer.at[me], buffer.at[me], twin, me).start()
        self.partners(
            lambda k, peer: self.link(which, k, buffer.at[me], buffer.at[me], peer, me).start()
        )

    def relayed(self, which, buffer):
        me, twin = self.me, self.me + 1 - 2 * lax.rem(self.me, 2)
        n = self.n

        def pass_on(k, peer):
            copy = self.link(which, k, buffer.at[peer], buffer.at[peer], peer, peer)
            copy.wait_recv()
            self.link(which, n // 2 + k, buffer.at[peer], buffer.at[peer], twin, peer).start()

        self.partners(pass_on)

        def got(k, carry):
            origin = lax.rem(twin + 2 * k, n)
            self.link(which, k, buffer.at[origin], buffer.at[origin], twin, origin).wait_recv()
            return carry

        lax.fori_loop(0, n // 2, got, 0)

    def relay_sent(self, which, buffer):
        def gone(k, carry):
            peer = lax.rem(self.me + 1, self.n)
            self.link(which, k, buffer.at[0], buffer.at[0], peer, 0).wait_send()
            return carry

        lax.fori_loop(1, self.n, gone, 0)


def tiles_of(vocab_rows, body, carry):
    whole = vocab_rows // TILE
    carry = lax.fori_loop(
        0, whole, lambda i, c: body(i, pl.multiple_of(i * TILE, TILE), TILE, c), carry
    )
    if vocab_rows % TILE:
        carry = body(whole, whole * TILE, vocab_rows % TILE, carry)
    return carry


def rows_at_once(n, slots):
    return max(g for g in range(1, n + 1) if n % g == 0 and g * slots <= 512)


def share_kernel(n, groups, packed, everyone, worst, marks, send, recv, mark_send, mark_recv):
    links = Links(n, send, recv)
    me = links.me
    group = lax.axis_index("grp")

    def other_groups(body):
        for k in range(1, groups):
            body(k, lax.rem(group + k, groups))

    barrier = links.greet()
    other_groups(
        lambda k, peer: pl.semaphore_signal(
            barrier, inc=1, device_id={"grp": peer}, device_id_type=MESH
        )
    )
    pl.semaphore_wait(barrier, n - 1 + groups - 1)
    everyone[me] = packed[...]
    links.spread(0, everyone)
    links.arrive(0, everyone)
    most = everyone[0]
    for j in range(1, n):
        most = jnp.maximum(most, everyone[j])
    marks[group] = jnp.broadcast_to(most[:1, -128:], (8, 128))

    def mark(k, peer, origin):
        return pltpu.make_async_remote_copy(
            src_ref=marks.at[origin],
            dst_ref=marks.at[origin],
            send_sem=mark_send.at[k],
            recv_sem=mark_recv.at[origin],
            device_id={"grp": peer},
            device_id_type=MESH,
        )

    other_groups(lambda k, peer: mark(k, peer, group).start())
    other_groups(lambda k, peer: mark(k, peer, peer).wait_recv())
    most = marks[0]
    for j in range(1, groups):
        most = jnp.maximum(most, marks[j])
    worst[...] = most
    links.sent(0, everyone)
    other_groups(lambda k, peer: mark(k, peer, group).wait_send())


def share(n, packed):
    groups = lax.axis_size("grp")
    vmem = pl.BlockSpec(memory_space=pltpu.VMEM)
    return pl.pallas_call(
        functools.partial(share_kernel, n, groups),
        out_shape=(
            jax.ShapeDtypeStruct((n,) + packed.shape, jnp.int32),
            jax.ShapeDtypeStruct((8, 128), jnp.int32),
        ),
        in_specs=[vmem],
        out_specs=(vmem, vmem),
        scratch_shapes=[
            pltpu.VMEM((groups, 8, 128), jnp.int32),
            pltpu.SemaphoreType.DMA((1, n)),
            pltpu.SemaphoreType.DMA((1, n)),
            pltpu.SemaphoreType.DMA((groups,)),
            pltpu.SemaphoreType.DMA((groups,)),
        ],
        compiler_params=pltpu.CompilerParams(collective_id=1, has_side_effects=True),
        name="share_ids",
    )(packed)


def fetch_kernel(dims, ints, eb, x_out, id_s, xs, xr, send, recv):
    n, slots, vocab_rows, tokens, row_count = dims
    turned = ints[...].astype(F32).T.astype(jnp.int32)
    id_s[...] = turned[: n * slots, 0:1]
    slot_col = turned[:tokens, 1:2]
    links = Links(n, send, recv)
    me = links.me
    group = rows_at_once(n, slots)
    chunk = group * slots
    pl.semaphore_wait(links.greet(), n - 1)

    def look(c, carry):
        ids = id_s[pl.ds(pl.multiple_of(c * chunk, chunk), chunk), :]

        def add(i, start, size, acc):
            hit = (lanes((chunk, size)) + start == ids).astype(F32).astype(LOW)
            return acc + dot_nn(hit, eb[pl.ds(start, size), :])

        found = tiles_of(vocab_rows, add, jnp.zeros((chunk, D), F32))
        xs[pl.ds(c * group, group)] = found.astype(LOW).reshape(group, slots, D)
        return carry

    lax.fori_loop(0, n // group, look, 0)
    links.deal(0, xs, xr)
    xr[me] = xs[me]
    links.arrive(0, xr)
    x = jnp.zeros((tokens, D), F32)
    for c in range(n // group):
        hit = (lanes((tokens, chunk)) + c * chunk == slot_col).astype(F32).astype(LOW)
        x = x + dot_nn(hit, xr[c * group : (c + 1) * group].reshape(chunk, D))
    x_out[...] = x.astype(LOW)
    links.sent(0, xs)


def fetch(n, slots, sizes, ints, embed_low):
    vmem = pl.BlockSpec(memory_space=pltpu.VMEM)
    vocab_rows = embed_low.shape[0]
    return pl.pallas_call(
        functools.partial(fetch_kernel, (n, slots, vocab_rows) + sizes),
        out_shape=jax.ShapeDtypeStruct((sizes[0], D), LOW),
        in_specs=[vmem] * 2,
        out_specs=vmem,
        scratch_shapes=[
            pltpu.VMEM((n * slots, 1), jnp.int32),
            pltpu.VMEM((n, slots, D), LOW),
            pltpu.VMEM((n, slots, D), LOW),
            pltpu.SemaphoreType.DMA((1, n)),
            pltpu.SemaphoreType.DMA((1, n)),
        ],
        compiler_params=pltpu.CompilerParams(
            collective_id=2, has_side_effects=True, vmem_limit_bytes=40 * 1024 * 1024
        ),
        name="fetch_rows",
    )(ints, embed_low)


def packs(shard, wide):
    return wide == 192 and shard % 32 == 0


def step_kernel(
    dims,
    ints, vec, x_low, eb_in, attn_in, expw_in,
    dembed_out, dattn_out, dexp_out, dvec_out, loss_out, norm_out, factor_out,
    eb, attn, expw, xs, gr, ball, ys, yr, rows, tops, drs, drr, dyall, dbs, dbr,
    q_all, pas, par, middle_all, branch_all, dq_all, dss, dsr, dvec, sums, logit_s, dlog_s, pre_s, hid_s, dpre_s, flip_s, tile_s, part_s, hit_s,
    send, recv, out_sem, load_sem,
):
    n, slots, vocab, vocab_rows, hidden, tokens, row_count = dims
    all_rows = n * row_count
    wide = HEADS * row_count
    shard = D // n
    packed = packs(shard, wide)
    row_total = float(all_rows)
    scale = 2.0 * D ** (-0.5)
    factor_qk = HEAD_DIM ** (-0.5)
    links = Links(n, send, recv)
    me = links.me
    spread, deal, arrive, sent = links.spread, links.deal, links.arrive, links.sent
    relay, relayed = links.relay, links.relayed
    tiled = functools.partial(tiles_of, vocab_rows)
    loads = [
        pltpu.make_async_copy(source, target, load_sem.at[i])
        for i, (source, target) in enumerate(((attn_in, attn), (expw_in, expw), (eb_in, eb)))
    ]
    for load in loads:
        load.start()

    def added(buffer):
        total = buffer[0].astype(F32)
        for j in range(1, n):
            total = total + buffer[j].astype(F32)
        return total

    pl.semaphore_wait(links.greet(), n - 1)
    group = rows_at_once(n, slots)
    chunk = group * slots
    x = x_low[...].astype(F32)
    id_lane, slot_lane, pick_lane = ints[0:1, : n * slots], ints[1:2, :tokens], ints[2:3, :row_count]
    seg_lane, target_lane = ints[4:5, :tokens], ints[7:8, : 2 * all_rows]
    turned = ints[...].astype(F32).T.astype(jnp.int32)
    pick_col, seg_rows = turned[:row_count, 2:3], turned[:row_count, 3:4]
    route_col, route_all = turned[:row_count, 5:6], turned[:all_rows, 6:7]

    gain_a, gain_b, gain_c, gain_d = (vec[i : i + 1, :] for i in range(4))
    x_factor = norm_factor(x)
    a = (x * x_factor * gain_a).astype(LOW)
    pick = (lanes((row_count, tokens)) == pick_col).astype(F32).astype(LOW)
    x_rows = dot_nn(pick, x_low[...])
    a_rows = dot_nn(pick, a).astype(LOW)
    loads[0].wait()
    q = dot_nn(a_rows, attn[0]).astype(LOW)
    k = dot_nn(a, attn[1]).astype(LOW)
    v = dot_nn(a, attn[2]).astype(LOW)
    head_mask = (
        lax.shift_right_logical(lanes((HEADS, row_count, D)), HEAD_DIM.bit_length() - 1)
        == lax.broadcasted_iota(jnp.int32, (HEADS, row_count, D), 0)
    )

    def widen(low_rows):
        return (
            jnp.where(head_mask, low_rows.astype(F32)[None], 0.0).reshape(wide, D).astype(LOW)
        )

    def narrow(values):
        return jnp.sum(jnp.where(head_mask, values.reshape(HEADS, row_count, D), 0.0), axis=0)

    q_wide = widen(q)
    scores = dot_nt(q_wide, k) * factor_qk
    allowed = (lanes((row_count, tokens)) <= pick_col) & (seg_lane == seg_rows)
    scores = jnp.where(
        allowed[None], scores.reshape(HEADS, row_count, tokens), -1e30
    ).reshape(wide, tokens)
    exponent = jnp.exp(scores - jnp.max(scores, axis=-1, keepdims=True))
    probs = exponent / jnp.sum(exponent, axis=-1, keepdims=True)
    probs_low = probs.astype(LOW)
    o = narrow(dot_nn(probs_low, v)).astype(LOW)
    x_attn = x_rows + ATTN_GAIN * dot_nn(o, attn[3])

    b_factor = norm_factor(x_attn)
    b = x_attn * b_factor * gain_b
    ball[me] = b.astype(LOW)
    spread(B_ROWS, ball)
    router_rows = [vec[4 + e : 5 + e, :] for e in range(EXPERTS)]
    router_logits = [jnp.sum(b * row, axis=-1, keepdims=True) for row in router_rows]
    highest = router_logits[0]
    for value in router_logits[1:]:
        highest = jnp.maximum(highest, value)
    router_exp = [jnp.exp(value - highest) for value in router_logits]
    router_sum = sum(router_exp[1:], router_exp[0])
    router_probs = [value / router_sum for value in router_exp]
    chosen = [(route_col == e).astype(F32) for e in range(EXPERTS)]
    gate = sum([p * c for p, c in zip(router_probs[1:], chosen[1:])], router_probs[0] * chosen[0])
    q_all[me] = q
    a_turned = a.astype(F32).T.astype(LOW)
    eye = (sublanes((row_count, row_count)) == lanes((row_count, row_count))).astype(F32).astype(LOW)
    flipped = lambda low_rows: dot_tn(low_rows, eye)
    pas[:, :, 0:wide] = dot_nt(a_turned, probs_low).reshape(n, shard, wide).astype(LOW)
    pas[:, :, wide : wide + row_count] = flipped(a_rows).reshape(n, shard, row_count).astype(LOW)
    pas[:, :, wide + row_count :] = flipped(o).reshape(n, shard, row_count).astype(LOW)
    arrive(B_ROWS, ball)
    loads[1].wait()
    b_all = ball[...].reshape(all_rows, D)
    y_part = jnp.zeros((all_rows, D), F32)
    for e in range(EXPERTS):
        pre = dot_nn(b_all, expw[e, 0])
        pre_s[e] = pre
        hid = jnp.where(route_all == e, gelu_of(pre), 0.0).astype(LOW)
        hid_s[e] = hid
        y_part = y_part + dot_nt(hid, expw[e, 1])
    ys[...] = y_part.astype(LOW).reshape(n, row_count, D)
    deal(Y_PART, ys, yr)
    yr[me] = ys[me]
    arrive(Y_PART, yr)
    y = added(yr)
    z = x_attn + gate * y

    z_factor = norm_factor(z)
    first = (z * z_factor * gain_c).astype(LOW)
    middle = dot_nn(first, attn[4])
    middle_factor = norm_factor(middle)
    rows[me, 0] = first
    rows[me, 1] = (middle * middle_factor * gain_d).astype(LOW)
    relay(HEAD_ROWS, rows)
    relayed(HEAD_ROWS, rows)
    deal(P_A, pas, par)
    par[me] = pas[me]
    loads[2].wait()
    loss_rows = 2 * all_rows
    head_rows = rows[...].reshape(loss_rows, D)

    def target_hit(start, size):
        return sublanes((size, loss_rows)) + start == target_lane

    def logits_tile(i, start, size, carry):
        top, total, at_target = carry
        value = dot_nt(eb[pl.ds(start, size), :], head_rows) * scale
        if vocab_rows != vocab:
            value = jnp.where(sublanes((size, loss_rows)) + start < vocab, value, -1e30)
        logit_s[pl.ds(start, size), :] = value
        hit = target_hit(start, size)
        at_target = at_target + jnp.sum(jnp.where(hit, value, 0.0), axis=0, keepdims=True)
        new_top = jnp.maximum(top, jnp.max(value, axis=0, keepdims=True))
        total = total * jnp.exp(top - new_top) + jnp.sum(
            jnp.exp(value - new_top), axis=0, keepdims=True
        )
        return new_top, total, at_target

    nothing = jnp.zeros((1, loss_rows), F32)
    top, total, at_target = tiled(logits_tile, (nothing - 1e30, nothing, nothing))
    place = sublanes((8, loss_rows))
    tops[me] = jnp.where(
        place == 0, top, jnp.where(place == 1, total, jnp.where(place == 2, at_target, 0.0))
    )
    spread(TOPS, tops)
    arrive(TOPS, tops)
    relay(Q_ROWS, q_all)
    top = tops[0, 0:1]
    for j in range(1, n):
        top = jnp.maximum(top, tops[j, 0:1])
    total, at_target = nothing, nothing
    for j in range(n):
        total = total + tops[j, 1:2] * jnp.exp(tops[j, 0:1] - top)
        at_target = at_target + tops[j, 2:3]
    logsum = top + jnp.log(total)
    is_first = lax.rem(lanes((1, loss_rows)), 2 * row_count) < row_count
    weight = jnp.where(is_first, 1.0, SECOND_WEIGHT) / row_total
    loss = jnp.sum(weight * (logsum - at_target), axis=-1, keepdims=True)
    loss_out[...] = loss

    def dlogits_tile(i, start, size, acc):
        soft = jnp.exp(logit_s[pl.ds(start, size), :] - logsum)
        low = ((soft - target_hit(start, size).astype(F32)) * weight).astype(LOW)
        dlog_s[pl.ds(start, size), :] = low
        return acc + dot_tn(low, eb[pl.ds(start, size), :])

    drows = tiled(dlogits_tile, jnp.zeros((loss_rows, D), F32)) * scale
    drs[...] = drows.astype(LOW).reshape(n, 2 * row_count, D)
    deal(D_ROWS, drs, drr)
    drr[me] = drs[me]
    arrive(D_ROWS, drr)
    drow = added(drr)
    dmiddle, gain_mtp = norm_grad(middle, middle_factor, gain_d, drow[row_count:])
    dmiddle_low = dmiddle.astype(LOW)
    dfirst = drow[:row_count] + dot_nt(dmiddle_low, attn[4])
    dz, gain_final = norm_grad(z, z_factor, gain_c, dfirst)

    dgate = jnp.sum(dz * y, axis=-1, keepdims=True)
    dyall[me] = (gate * dz).astype(LOW)
    spread(DY_ROWS, dyall)
    arrive(DY_ROWS, dyall)
    middle_all[me] = dmiddle_low
    relay(MIDDLE_ROWS, middle_all)
    dy_all = dyall[...].reshape(all_rows, D)
    db_part = jnp.zeros((all_rows, D), F32)
    for e in range(EXPERTS):
        dhid = dot_nn(dy_all, expw[e, 1])
        slope = jnp.where(route_all == e, gelu_slope(pre_s[e]), 0.0)
        dpre = (slope * dhid).astype(LOW)
        dpre_s[e] = dpre
        db_part = db_part + dot_nt(dpre, expw[e, 0])
    dbs[...] = db_part.astype(LOW).reshape(n, row_count, D)
    deal(DB_PART, dbs, dbr)
    dbr[me] = dbs[me]
    squares = jnp.zeros((1, D), F32)

    def squared(values):
        return jnp.sum(values * values, axis=0, keepdims=True)

    hidden_squares = jnp.zeros((1, hidden), F32)
    for e in range(EXPERTS):
        up = dot_tn(b_all, dpre_s[e])
        down = dot_tn(dy_all, hid_s[e])
        dexp_out[e, 0] = up.astype(LOW)
        dexp_out[e, 1] = down.astype(LOW)
        hidden_squares = hidden_squares + squared(up) + squared(down)
    arrive(DB_PART, dbr)
    prob_grads = [c * dgate for c in chosen]
    mixed = sum([p * g for p, g in zip(router_probs[1:], prob_grads[1:])], router_probs[0] * prob_grads[0])
    dlogits = [p * (g - mixed) for p, g in zip(router_probs, prob_grads)]
    drouter = [jnp.sum(g * b, axis=0, keepdims=True) for g in dlogits]
    dnormed = added(dbr)
    for g, row in zip(dlogits, router_rows):
        dnormed = dnormed + g * row
    dx_part, gain_ffn = norm_grad(x_attn, b_factor, gain_b, dnormed)
    dx_attn = dz + dx_part

    dbranch = dx_attn.astype(LOW)
    branch_all[me] = dbranch
    relay(BRANCH_ROWS, branch_all)
    do = (ATTN_GAIN * dot_nt(dbranch, attn[3])).astype(LOW)
    do_wide = widen(do)
    dprobs = dot_nt(do_wide, v)
    dscores = (probs * (dprobs - jnp.sum(probs * dprobs, axis=-1, keepdims=True))).astype(LOW)
    dq = (narrow(dot_nn(dscores, k)) * factor_qk).astype(LOW)
    dq_all[me] = dq
    relay(DQ_ROWS, dq_all)
    dk = (dot_tn(dscores, q_wide) * factor_qk).astype(LOW)
    dv = dot_tn(probs_low, do_wide).astype(LOW)
    dinput = dot_nt(dk, attn[1]) + dot_nt(dv, attn[2])
    dx, gain_attn = norm_grad(x, x_factor, gain_a, dinput)
    row_back, gain_more = norm_grad(x_rows, norm_factor(x_rows), gain_a, dot_nt(dq, attn[0]))
    spots = (sublanes((tokens, row_count)) == pick_lane).astype(F32)
    dx = dx + lax.dot_general(
        spots, row_back + dx_attn, (((1,), (0,)), ((), ())), precision=HIGH,
        preferred_element_type=F32,
    )
    dx_low = dx.astype(LOW)
    for c in range(n // group):
        hit = (sublanes((chunk, tokens)) + c * chunk == slot_lane).astype(F32).astype(LOW)
        xs[c * group : (c + 1) * group] = dot_nn(hit, dx_low).astype(LOW).reshape(group, slots, D)
    deal(G_OUT, xs, gr)
    gr[me] = xs[me]
    line = sublanes((8, D))
    shares = jnp.zeros((8, D), F32)
    for i, value in enumerate([gain_attn + gain_more, gain_ffn, gain_final, gain_mtp] + drouter):
        shares = jnp.where(line == i, value, shares)
    dvec[me] = shares
    relay(D_VEC, dvec)
    turned_scores = dot_nt(a_turned, dscores).reshape(n, shard, wide)
    if packed:
        dss[:, 0:shard] = turned_scores[:, :, 0:128].astype(LOW)
        dss[:, shard:, 0 : wide - 128] = turned_scores[:, : shard // 2, 128:].astype(LOW)
        dss[:, shard:, wide - 128 :] = turned_scores[:, shard // 2 :, 128:].astype(LOW)
    else:
        dss[...] = turned_scores.astype(LOW)
    deal(DS_A, dss, dsr)
    dsr[me] = dss[me]

    mine = pl.ds(pl.multiple_of(me * shard, 8), shard)

    def own_slices(start, right):
        total = jnp.zeros((shard, D), F32)
        for j in range(n):
            total = total + dot_nn(par[j, :, start : start + row_count], right[j])
        return total

    def own_rows(left, right):
        flip_s[...] = left.astype(F32).reshape(all_rows, D).T
        return dot_nn(flip_s[mine, :].astype(LOW), right.reshape(all_rows, D))

    def keep(i, part):
        dattn_out[i] = part.astype(LOW)
        return squared(part)

    arrive(P_A, par)
    relayed(MIDDLE_ROWS, middle_all)
    squares = squares + keep(4, own_rows(rows[:, 0], middle_all[...]))
    relayed(BRANCH_ROWS, branch_all)
    squares = squares + keep(3, ATTN_GAIN * own_slices(wide + row_count, branch_all))
    do_all = ATTN_GAIN * dot_nt(branch_all[...].reshape(all_rows, D), attn[3])
    dvalue = jnp.zeros((shard, D), F32)
    for j in range(n):
        do_one = do_all[j * row_count : (j + 1) * row_count].astype(LOW)
        dvalue = dvalue + dot_nn(par[j, :, 0:wide], widen(do_one))
    squares = squares + keep(2, dvalue)

    def ready_tile(i, start, size, carry):
        part_s[pl.ds(start, size), :] = scale * dot_nn(dlog_s[pl.ds(start, size), :], head_rows)
        hit = (sublanes((size, n * slots)) + start == id_lane).astype(F32)
        hit_s[pl.ds(start, size), :] = hit.astype(LOW)
        return carry

    tiled(ready_tile, 0)
    arrive(G_OUT, gr)
    whole = vocab_rows // TILE

    def leave(i, start, size):
        slot = lax.rem(i, 2)
        return pltpu.make_async_copy(
            tile_s.at[slot, pl.ds(0, size)], dembed_out.at[pl.ds(start, size)], out_sem.at[slot]
        )

    def dembed_tile(i, start, size, acc):
        value = part_s[pl.ds(start, size), :] + dot_nn(
            hit_s[pl.ds(start, size), :], gr[...].reshape(n * slots, D)
        )

        def free():
            leave(i - 2, start - 2 * TILE, TILE).wait()

        if isinstance(i, int):
            if i >= 2:
                free()
        else:
            pl.when(i >= 2)(free)
        tile_s[lax.rem(i, 2), pl.ds(0, size)] = value.astype(LOW)
        leave(i, start, size).start()
        return acc + squared(value)

    squares = tiled(dembed_tile, squares)
    relayed(Q_ROWS, q_all)
    relayed(DQ_ROWS, dq_all)
    squares = squares + keep(0, own_slices(wide, dq_all))
    arrive(DS_A, dsr)
    dkey = jnp.zeros((shard, D), F32)
    for j in range(n):
        q_one = widen(q_all[j])
        if packed:
            tail = q_one[128:wide]
            upper = dot_nn(dsr[j, shard:, 0 : wide - 128], tail)
            lower = dot_nn(dsr[j, shard:, wide - 128 :], tail)
            dkey = dkey + dot_nn(dsr[j, 0:shard], q_one[0:128])
            dkey = dkey + jnp.concatenate([upper, lower], axis=0)
        else:
            dkey = dkey + dot_nn(dsr[j], q_one)
    squares = squares + keep(1, dkey * factor_qk)
    tiles = [(i, i * TILE, TILE) for i in range(whole)]
    if vocab_rows % TILE:
        tiles.append((whole, whole * TILE, vocab_rows % TILE))
    total_squares = jnp.sum(squares, axis=-1, keepdims=True) + jnp.sum(
        hidden_squares, axis=-1, keepdims=True
    )
    sums[me] = jnp.broadcast_to(total_squares, (8, 128))
    spread(SQUARES, sums)
    relayed(D_VEC, dvec)
    arrive(SQUARES, sums)
    shared = added(dvec)
    dvector = shared[0 : 4 + EXPERTS]
    dvec_out[...] = dvector
    own = jnp.sum(squared(dvector), axis=-1, keepdims=True)
    norm = jnp.sqrt(added(sums)[0:1, 0:1] + own)
    norm_out[...] = norm
    factor_out[...] = jnp.minimum(1.0, 0.05 / math.sqrt(row_total) / norm)
    for i, start, size in tiles[-2:]:
        leave(i, start, size).wait()
    for which, source in (
        (B_ROWS, ball), (Y_PART, ys), (TOPS, tops), (D_ROWS, drs), (DY_ROWS, dyall),
        (DB_PART, dbs), (P_A, pas), (DS_A, dss), (G_OUT, xs), (SQUARES, sums),
    ):
        sent(which, source)
    for which, source in (
        (HEAD_ROWS, rows), (Q_ROWS, q_all), (MIDDLE_ROWS, middle_all),
        (BRANCH_ROWS, branch_all), (DQ_ROWS, dq_all), (D_VEC, dvec),
    ):
        links.relay_sent(which, source)


def run_step(n, slots, vocab, sizes, ints, vec, x_low, embed_low, attn_low, expert_low):
    vocab_rows = embed_low.shape[0]
    row_count = sizes[1]
    hidden = expert_low.shape[3]
    shard = D // n
    all_rows = n * row_count
    wide = HEADS * row_count
    score_shape = (n, shard + shard // 2, 128) if packs(shard, wide) else (n, shard, wide)
    vmem = pl.BlockSpec(memory_space=pltpu.VMEM)
    anywhere = pl.BlockSpec(memory_space=pl.ANY)
    low = lambda *shape: pltpu.VMEM(shape, LOW)
    wide_float = lambda *shape: pltpu.VMEM(shape, F32)
    outs = pl.pallas_call(
        functools.partial(step_kernel, (n, slots, vocab, vocab_rows, hidden) + sizes),
        out_shape=(
            jax.ShapeDtypeStruct((vocab_rows, D), LOW),
            jax.ShapeDtypeStruct((5, shard, D), LOW),
            jax.ShapeDtypeStruct((EXPERTS, 2, D, hidden), LOW),
            jax.ShapeDtypeStruct((4 + EXPERTS, D), F32),
            jax.ShapeDtypeStruct((1, 1), F32),
            jax.ShapeDtypeStruct((1, 1), F32),
            jax.ShapeDtypeStruct((1, 1), F32),
        ),
        in_specs=[vmem] * 3 + [anywhere] * 3,
        out_specs=(anywhere, vmem, vmem, vmem, vmem, vmem, vmem),
        scratch_shapes=[
            low(vocab_rows, D), low(5, D, D), low(EXPERTS, 2, D, hidden),
            low(n, slots, D), low(n, slots, D),
            low(n, row_count, D), low(n, row_count, D), low(n, row_count, D),
            low(n, 2, row_count, D), wide_float(n, 8, 2 * all_rows),
            low(n, 2 * row_count, D), low(n, 2 * row_count, D),
            low(n, row_count, D), low(n, row_count, D), low(n, row_count, D),
            low(n, row_count, D), low(n, shard, wide + 2 * row_count),
            low(n, shard, wide + 2 * row_count),
            low(n, row_count, D), low(n, row_count, D), low(n, row_count, D),
            low(*score_shape), low(*score_shape),
            wide_float(n, 8, D), wide_float(n, 8, 128),
            wide_float(vocab_rows, 2 * all_rows), low(vocab_rows, 2 * all_rows),
            wide_float(EXPERTS, all_rows, hidden), low(EXPERTS, all_rows, hidden),
            low(EXPERTS, all_rows, hidden), wide_float(D, all_rows), low(2, TILE, D),
            wide_float(vocab_rows, D), low(vocab_rows, n * slots),
            pltpu.SemaphoreType.DMA((EXCHANGES, n)),
            pltpu.SemaphoreType.DMA((EXCHANGES, n)),
            pltpu.SemaphoreType.DMA((2,)),
            pltpu.SemaphoreType.DMA((3,)),
        ],
        compiler_params=pltpu.CompilerParams(
            collective_id=3, has_side_effects=True, vmem_limit_bytes=60 * 1024 * 1024
        ),
        name="inner_step",
    )(ints, vec, x_low, embed_low, attn_low, expert_low)
    return (outs[0][:vocab],) + outs[1:]


def sum_kernel(shapes, *refs):
    count = len(shapes)
    values, vector, refs = refs[:count], refs[count], refs[count + 1 :]
    totals, vector_total, refs = refs[:count], refs[count], refs[count + 1 :]
    helds, first_ins, second_ins, rests, nears = (
        refs[i * count : (i + 1) * count] for i in range(5)
    )
    flat, load_sem, *sems = refs[5 * count :]
    loads = [
        pltpu.make_async_copy(value, near, load_sem.at[array])
        for array, (value, near) in enumerate(zip(values, nears))
    ]
    for load in loads:
        load.start()
    one_s, one_r, two_s, two_r, three_s, three_r, four_s, four_r, rest_s, rest_r = sems
    group = lax.axis_index("grp")
    width = D // 2
    bits = (lax.rem(group, 2), lax.div(group, 2))
    flip = lambda bit: group + (1 - 2 * bits[bit]) * (1 + bit)
    barrier = pltpu.get_barrier_semaphore()
    for k in range(1, 4):
        pl.semaphore_signal(
            barrier, inc=1, device_id={"grp": lax.rem(group + k, 4)}, device_id_type=MESH
        )
    pl.semaphore_wait(barrier, 3)
    units = [
        (array, side, piece, piece * 2 + side)
        for array, (rows, quarter, pieces) in enumerate(shapes)
        for piece in range(pieces)
        for side in range(2)
    ]

    def place(u, first_bit, second_bit):
        array, side, piece, slot = units[u]
        rows, quarter, pieces = shapes[array]
        size = quarter // pieces
        owner = first_bit + 2 * second_bit if side == 0 else second_bit + 2 * first_bit
        start = pl.multiple_of((owner * pieces + piece) * size, 16)
        return pl.ds(start, size), pl.ds(side * width, width)

    def copy(source, target, send, recv, peer):
        return pltpu.make_async_remote_copy(
            src_ref=source, dst_ref=target, send_sem=send, recv_sem=recv,
            device_id={"grp": peer}, device_id_type=MESH,
        )

    def stage_one(u, turn):
        array, side, piece, slot = units[u]
        here, there = bits[side], bits[1 - side]
        out = place(u, 1 - here, there if turn else 1 - there)
        return copy(
            values[array].at[out], first_ins[array].at[slot, turn],
            one_s.at[u, turn], one_r.at[u, turn], flip(side),
        )

    def stage_two(u):
        array, side, piece, slot = units[u]
        return copy(
            helds[array].at[slot, 0], second_ins[array].at[slot], two_s.at[u], two_r.at[u], flip(1 - side)
        )

    def stage_three(u, other=False):
        array, side, piece, slot = units[u]
        there = bits[1 - side]
        block = totals[array].at[place(u, bits[side], 1 - there if other else there)]
        return copy(block, block, three_s.at[u], three_r.at[u], flip(1 - side))

    def stage_four(u, turn, other=False):
        array, side, piece, slot = units[u]
        here, there = bits[side], bits[1 - side]
        block = totals[array].at[
            place(u, 1 - here if other else here, there if turn == 0 else 1 - there)
        ]
        return copy(block, block, four_s.at[u, turn], four_r.at[u, turn], flip(side))

    every = range(len(units))
    for turn in range(2):
        for u in every:
            stage_one(u, turn).start()
    for load in loads:
        load.wait()
    flat[group] = vector[...]
    smalls = [(count, flat)]
    for array, (rows, quarter, pieces) in enumerate(shapes):
        spare = rows - 4 * quarter
        if spare:
            rests[array][group, 0:spare] = nears[array][4 * quarter : rows]
            smalls.append((array, rests[array]))

    def small(which, buffer, k, peer, origin):
        return copy(
            buffer.at[origin], buffer.at[origin], rest_s.at[which, k], rest_r.at[which, origin], peer
        )

    for which, buffer in smalls:
        for k in range(1, 4):
            small(which, buffer, k, lax.rem(group + k, 4), group).start()
    for turn in range(2):
        for u in every:
            array, side, piece, slot = units[u]
            there = bits[1 - side]
            stage_one(u, turn).wait_recv()
            mine = place(u, bits[side], there if turn else 1 - there)
            helds[array][slot, turn] = (
                nears[array][mine].astype(F32) + first_ins[array][slot, turn].astype(F32)
            ).astype(LOW)
            if turn == 0:
                stage_two(u).start()
    for u in every:
        array, side, piece, slot = units[u]
        stage_two(u).wait_recv()
        mine = place(u, bits[side], bits[1 - side])
        totals[array][mine] = (
            helds[array][slot, 1].astype(F32) + second_ins[array][slot].astype(F32)
        ).astype(LOW)
        stage_three(u).start()
        stage_four(u, 0).start()
    for u in every:
        stage_three(u, True).wait_recv()
        stage_four(u, 1).start()
    for which, buffer in smalls:
        for k in range(1, 4):
            origin = lax.rem(group + k, 4)
            small(which, buffer, k, origin, origin).wait_recv()
    added = lambda buffer: (buffer[0].astype(F32) + buffer[1].astype(F32)) + (
        buffer[2].astype(F32) + buffer[3].astype(F32)
    )
    vector_total[...] = added(flat)
    for array, buffer in smalls[1:]:
        rows, quarter, pieces = shapes[array]
        totals[array][4 * quarter : rows] = added(buffer)[0 : rows - 4 * quarter].astype(LOW)
    for u in every:
        for turn in range(2):
            stage_four(u, turn, True).wait_recv()
    for u in every:
        stage_two(u).wait_send()
        stage_three(u).wait_send()
        for turn in range(2):
            stage_one(u, turn).wait_send()
            stage_four(u, turn).wait_send()
    for which, buffer in smalls:
        for k in range(1, 4):
            small(which, buffer, k, lax.rem(group + k, 4), group).wait_send()


def sum_over_groups(values, vector):
    shapes = []
    for value in values:
        rows = value.shape[0]
        quarter = rows // 64 * 16
        shapes.append((rows, quarter, 2 if quarter % 32 == 0 and quarter > 256 else 1))
    units = sum(2 * pieces for rows, quarter, pieces in shapes)
    vmem = pl.BlockSpec(memory_space=pltpu.VMEM)
    scratch = []
    for lead in ((2,), (2,), ()):
        for rows, quarter, pieces in shapes:
            scratch.append(pltpu.VMEM((2 * pieces,) + lead + (quarter // pieces, D // 2), LOW))
    for rows, quarter, pieces in shapes:
        spare = -(-(rows - 4 * quarter) // 16) * 16
        scratch.append(pltpu.VMEM((4, max(spare, 16), D), LOW))
    dma = pltpu.SemaphoreType.DMA
    count = len(values)
    *totals, vector_total = pl.pallas_call(
        functools.partial(sum_kernel, tuple(shapes)),
        out_shape=[jax.ShapeDtypeStruct(value.shape, LOW) for value in values]
        + [jax.ShapeDtypeStruct(vector.shape, F32)],
        in_specs=[pl.BlockSpec(memory_space=pl.ANY)] * count + [vmem],
        out_specs=[vmem] * (count + 1),
        scratch_shapes=scratch
        + [pltpu.VMEM(value.shape, LOW) for value in values]
        + [
            pltpu.VMEM((4,) + vector.shape, F32),
            dma((count,)),
            dma((units, 2)), dma((units, 2)), dma((units,)), dma((units,)), dma((units,)),
            dma((units,)), dma((units, 2)), dma((units, 2)), dma((count + 1, 4)), dma((count + 1, 4)),
        ],
        compiler_params=pltpu.CompilerParams(
            collective_id=4, has_side_effects=True, vmem_limit_bytes=52 * 1024 * 1024
        ),
        cost_estimate=pl.CostEstimate(flops=0, bytes_accessed=300_000_000, transcendentals=0),
        name="sum_groups",
    )(*values, vector)
    return totals, vector_total


def prepare(n, slots, vocab, tokens, routes, segments, loss_pos):
    steps, count = tokens.shape
    start = lax.axis_index("fsdp") * vocab
    row_count = loss_pos.shape[1]
    owner = tokens // vocab
    places = jnp.arange(count)
    earlier = places[None, None, :] < places[None, :, None]
    same = tokens[:, :, None] == tokens[:, None, :]
    first = jnp.logical_not(jnp.any(same & earlier, axis=2))
    same_owner = owner[:, :, None] == owner[:, None, :]
    rank = jnp.sum((same_owner & earlier & first[:, None, :]).astype(jnp.int32), axis=2)
    own_slot = owner * slots + rank
    slot = jnp.sum(jnp.where(same & first[:, None, :], own_slot[:, None, :], 0), axis=2)
    at_slot = (own_slot[:, :, None] == jnp.arange(n * slots)[None, None, :]) & first[:, :, None]
    ids = jnp.sum(jnp.where(at_slot, tokens[:, :, None] + 1, 0), axis=1) - 1
    picked = loss_pos[:, :, None] == places[None, None, :]
    shifted = lambda by: jnp.sum(
        jnp.where(loss_pos[:, :, None] + by == places[None, None, :], tokens[:, None, :], 0), axis=2
    )
    row_routes = jnp.sum(jnp.where(picked, routes[:, None, :], 0), axis=2)
    row_segs = jnp.sum(jnp.where(picked, segments[:, None, :], 0), axis=2)
    most = jnp.broadcast_to(jnp.max(jnp.where(first, rank, 0)), (steps, 128))
    filler = jnp.zeros((steps, -(n * slots + 3 * row_count) % 128), jnp.int32)
    packed = jnp.concatenate([ids, row_routes, shifted(1), shifted(2), filler, most], axis=1)
    everyone, worst = share(n, packed)
    fits = worst[0, 127] < slots
    wanted = lax.dynamic_slice_in_dim(everyone, lax.axis_index("fsdp") * slots, slots, axis=2) - start
    after = n * slots
    rows = lambda part: jnp.swapaxes(part, 0, 1).reshape(steps, -1)
    lines = [
        rows(wanted),
        slot,
        loss_pos,
        row_segs,
        segments,
        row_routes,
        rows(everyone[:, :, after : after + row_count]),
        rows(everyone[:, :, after + row_count : after + 3 * row_count]) - start,
    ]
    longest = -(-max(line.shape[1] for line in lines) // 128) * 128
    fill = lambda line: jnp.pad(line, ((0, 0), (0, longest - line.shape[1])))
    result = jnp.stack([fill(line) for line in lines], axis=1)
    return result, fits


def general_step(tokens, routes, segments, loss_pos, all_ids, inner_step, weights):
    embed_w, attn_w, expert_w, vector_w = weights
    vocab_shard = embed_w.shape[0]
    vocab_start = lax.axis_index("fsdp") * vocab_shard
    row_total = lax.axis_size("fsdp") * loss_pos.shape[2]
    logit_scale = 2.0 * D ** (-0.5)
    vocab_places = jnp.arange(vocab_shard)
    head_weights = jnp.array([1.0, SECOND_WEIGHT], jnp.float32)
    embed_low = embed_w.astype(jnp.bfloat16)
    attn_low = lax.all_gather(attn_w.astype(jnp.bfloat16), "fsdp", axis=1, tiled=True)
    expert_low = expert_w.astype(jnp.bfloat16)
    ids_group = all_ids[inner_step]
    ids_local = tokens[inner_step, 0]
    seg_ids = segments[inner_step, 0]
    route_ids = routes[inner_step, 0, :, 0]
    pick_ids = loss_pos[inner_step, 0]
    chosen = ids_group - vocab_start
    inside = (chosen >= 0) & (chosen < vocab_shard)
    looked = jnp.take(embed_low, jnp.clip(chosen, 0, vocab_shard - 1), axis=0).astype(
        jnp.float32
    )
    x_embed = lax.psum_scatter(
        jnp.where(inside[:, None], looked, 0.0).astype(jnp.bfloat16),
        "fsdp",
        scatter_dimension=0,
        tiled=True,
    ).astype(jnp.float32)
    x_attn, kept = rows_forward(attn_low, vector_w, x_embed, seg_ids, pick_ids)
    b, b_factor = norm_apply(x_attn, vector_w[1])
    router_probs = jax.nn.softmax(jnp.dot(b, vector_w[4:].T, precision=HIGH), axis=-1)
    row_routes = route_ids[pick_ids]
    onehot = (row_routes[:, None] == jnp.arange(EXPERTS)[None, :]).astype(jnp.float32)
    gating = jnp.sum(router_probs * onehot, axis=1)
    b_all = gather_rows(b.astype(jnp.bfloat16))
    routes_all = gather_rows(row_routes)
    route_mask = routes_all[None, :, None] == jnp.arange(EXPERTS)[:, None, None]
    hidden_pre = jnp.einsum("cd,edf->ecf", b_all, expert_low[:, 0], preferred_element_type=jnp.float32)
    hidden_act = jnp.where(route_mask, smooth_act(hidden_pre), 0.0).astype(jnp.bfloat16)
    y_part = jnp.einsum("ecf,edf->cd", hidden_act, expert_low[:, 1], preferred_element_type=jnp.float32)
    returned = scatter_rows(y_part)
    z_rows = x_attn + gating[:, None] * returned
    first_float, first_factor = norm_apply(z_rows, vector_w[2])
    first_rows = first_float.astype(jnp.bfloat16)
    middle = jnp.dot(first_rows, attn_low[4], preferred_element_type=jnp.float32)
    second_float, second_factor = norm_apply(middle, vector_w[3])
    targets = jnp.stack([ids_local[pick_ids + 1], ids_local[pick_ids + 2]])
    rows_all, targets_all = (
        lax.all_gather(
            jnp.stack([first_rows, second_float.astype(jnp.bfloat16)]),
            "fsdp",
            axis=1,
            tiled=True,
        ),
        lax.all_gather(targets, "fsdp", axis=1, tiled=True),
    )
    logits = (
        jnp.einsum("jrd,vd->jrv", rows_all, embed_low, preferred_element_type=jnp.float32)
        * logit_scale
    )
    relative = targets_all - vocab_start
    onehot_target = (vocab_places[None, None, :] == relative[:, :, None]).astype(jnp.float32)
    target_part = jnp.sum(onehot_target * logits, axis=-1)
    local_top = jnp.max(logits, axis=-1)
    local_sum = jnp.sum(jnp.exp(logits - local_top[:, :, None]), axis=-1)
    parts = lax.all_gather(jnp.stack([local_top, local_sum, target_part]), "fsdp")
    row_top = jnp.max(parts[:, 0], axis=0)
    sum_exp = jnp.sum(parts[:, 1] * jnp.exp(parts[:, 0] - row_top), axis=0)
    target_logit = jnp.sum(parts[:, 2], axis=0)
    logsum = row_top + jnp.log(sum_exp)
    loss = (jnp.sum(head_weights[:, None] * (logsum - target_logit)) / row_total)
    dlogits = (
        (jnp.exp(logits - logsum[:, :, None]) - onehot_target)
        * (head_weights / row_total)[:, None, None]
    ).astype(jnp.bfloat16)
    dembed = (
        jnp.einsum("jrv,jrd->vd", dlogits, rows_all, preferred_element_type=jnp.float32)
        * logit_scale
    )
    drows = (
        jnp.einsum("jrv,vd->jrd", dlogits, embed_low, preferred_element_type=jnp.float32)
        * logit_scale
    )
    drows_own = lax.psum_scatter(
        drows.astype(jnp.bfloat16), "fsdp", scatter_dimension=1, tiled=True
    ).astype(jnp.float32)
    dmiddle, gain_mtp = norm_back(middle, second_factor, vector_w[3], drows_own[1])
    dmiddle_low = dmiddle.astype(jnp.bfloat16)
    dsecond_proj = jnp.dot(first_rows.T, dmiddle_low, preferred_element_type=jnp.float32)
    dfirst = drows_own[0] + jnp.dot(
        dmiddle_low, attn_low[4].T, preferred_element_type=jnp.float32
    )
    dz_rows, gain_final = norm_back(z_rows, first_factor, vector_w[2], dfirst)
    dgating = jnp.sum(dz_rows * returned, axis=1)
    dy_all = gather_rows((gating[:, None] * dz_rows).astype(jnp.bfloat16))
    dy_masked = jnp.where(route_mask, dy_all[None], 0)
    down_grad = jnp.einsum("ecf,ecd->edf", hidden_act, dy_masked, preferred_element_type=jnp.float32)
    dhidden = jnp.einsum("ecd,edf->ecf", dy_masked, expert_low[:, 1], preferred_element_type=jnp.float32)
    unused, act_back = jax.vjp(smooth_act, hidden_pre)
    dhidden_pre = act_back(dhidden)[0].astype(jnp.bfloat16)
    up_grad = jnp.einsum("cd,ecf->edf", b_all, dhidden_pre, preferred_element_type=jnp.float32)
    dexpert = jnp.stack([up_grad, down_grad], axis=1)
    db_part = jnp.einsum("ecf,edf->cd", dhidden_pre, expert_low[:, 0], preferred_element_type=jnp.float32)
    dnormed = scatter_rows(db_part)
    prob_grad = onehot * dgating[:, None]
    dlogit = router_probs * (prob_grad - jnp.sum(router_probs * prob_grad, axis=1, keepdims=True))
    drouter = jnp.dot(dlogit.T, b, precision=HIGH)
    dnormed = dnormed + jnp.dot(dlogit, vector_w[4:], precision=HIGH)
    dx_part, gain_ffn = norm_back(x_attn, b_factor, vector_w[1], dnormed)
    dx_embed, dlayer, gain_attn = rows_backward(
        attn_low, vector_w, x_embed, kept, dz_rows + dx_part, pick_ids
    )
    dattn = scatter_rows(jnp.concatenate([dlayer, dsecond_proj[None]], axis=0), axis=1)
    gather_chosen = ids_group - vocab_start
    gather_inside = (gather_chosen >= 0) & (gather_chosen < vocab_shard)
    seg_index = jnp.where(gather_inside, gather_chosen, vocab_shard)
    added = jax.ops.segment_sum(
        lax.all_gather(dx_embed.astype(jnp.bfloat16), "fsdp", axis=0, tiled=True).astype(
            jnp.float32
        ),
        seg_index,
        num_segments=vocab_shard + 1,
    )
    dembed = dembed + added[:vocab_shard]
    dvector_part = jnp.concatenate(
        [jnp.stack([gain_attn, gain_ffn, gain_final, gain_mtp]), drouter], axis=0
    )
    squares = jnp.sum(dembed * dembed) + jnp.sum(dattn * dattn) + jnp.sum(dexpert * dexpert)
    dvector, squares_all = lax.psum((dvector_part, squares), "fsdp")
    return dembed, dattn, dexpert, dvector, squares_all, loss


def adam_update(weight, first_moment, second, gradient, step_float, rate_here, decay_here):
    first_new = BETA_ONE * first_moment + (1.0 - BETA_ONE) * gradient
    second_new = BETA_TWO * second + (1.0 - BETA_TWO) * gradient * gradient
    first_hat = first_new / (1.0 - BETA_ONE**step_float)
    second_hat = second_new / (1.0 - BETA_TWO**step_float)
    weight_new = weight - rate_here * (
        first_hat / (jnp.sqrt(second_hat) + ADAM_EPS) + decay_here * weight
    )
    return (weight_new, first_new, second_new)


def window(
    step,
    embedding,
    embedding_first,
    embedding_second,
    embedding_outer,
    attention,
    attention_first,
    attention_second,
    attention_outer,
    experts,
    experts_first,
    experts_second,
    experts_outer,
    vectors,
    vectors_first,
    vectors_second,
    vectors_outer,
    inner_count,
    row_total,
):
    group_count = lax.axis_size("grp")
    threshold = 0.05 / math.sqrt(row_total)
    vector_rates = jnp.where(jnp.arange(vectors.shape[0])[:, None] < 4, LR_GAIN, LR_ROUTER)
    rate_list = (LR_EMBED, LR_MATRIX, LR_MATRIX, vector_rates)
    decay_list = (DECAY, DECAY, DECAY, 0.0)
    weights_now = (embedding, attention, experts, vectors)
    first_now = (embedding_first[0], attention_first[0], experts_first[0], vectors_first[0])
    second_now = (embedding_second[0], attention_second[0], experts_second[0], vectors_second[0])
    loss_list = []
    norm_list = []
    for inner_step in range(inner_count):
        dembed, dattn, dexpert, dvector, squares_all, loss = step(inner_step, weights_now)
        loss_list.append(loss)
        norm_value = jnp.sqrt(squares_all + jnp.sum(dvector * dvector))
        norm_list.append(norm_value)
        factor = jnp.minimum(1.0, threshold / norm_value)
        gradients = (dembed * factor, dattn * factor, dexpert * factor, dvector * factor)
        step_float = float(STEP0 + inner_step + 1)
        results = [
            adam_update(
                weights_now[k],
                first_now[k],
                second_now[k],
                gradients[k],
                step_float,
                rate_list[k],
                decay_list[k],
            )
            for k in range(4)
        ]
        weights_now = tuple((element[0] for element in results))
        first_now = tuple((element[1] for element in results))
        second_now = tuple((element[2] for element in results))
    masters = (embedding, attention, experts, vectors)
    outers = (embedding_outer, attention_outer, experts_outer, vectors_outer)
    deltas = tuple((master - current for master, current in zip(masters, weights_now)))
    summed = jax.tree.map(
        lambda part: part.astype(jnp.float32), lax.psum(for_sending(deltas), "grp")
    )
    new_outer = []
    new_master = []
    for k in range(4):
        delta_mean = summed[k] / group_count
        outer_new = OUTER_MOMENTUM * outers[k] + delta_mean
        new_outer.append(outer_new)
        new_master.append(masters[k] - OUTER_RATE * (delta_mean + OUTER_MOMENTUM * outer_new))
    return (
        jnp.stack(loss_list)[None],
        jnp.stack(norm_list)[None],
        first_now[0][None],
        second_now[0][None],
        new_master[0],
        new_outer[0],
        new_master[0].astype(jnp.bfloat16),
        first_now[1][None],
        second_now[1][None],
        new_master[1],
        new_outer[1],
        new_master[1].astype(jnp.bfloat16),
        first_now[2][None],
        second_now[2][None],
        new_master[2],
        new_outer[2],
        new_master[2].astype(jnp.bfloat16),
        gradients[3][None],
        first_now[3][None],
        second_now[3][None],
        new_master[3],
        new_outer[3],
    )


def adam_move(move, first_moment, second, gradient, step_float, rate_here, decay_here):
    first_new = BETA_ONE * first_moment + (1.0 - BETA_ONE) * gradient
    second_new = BETA_TWO * second + (1.0 - BETA_TWO) * gradient * gradient
    first_hat = first_new * (1.0 / (1.0 - BETA_ONE**step_float))
    second_hat = second_new * (1.0 / (1.0 - BETA_TWO**step_float))
    step = rate_here * (first_hat / (jnp.sqrt(second_hat) + ADAM_EPS))
    if move is not None:
        step = (1.0 - rate_here * decay_here) * move + step
    return (step, first_new, second_new)


def quick_window(n, slots, sizes, steps, x_start, lows, masters, firsts, seconds, outers):
    embedding, attention, experts, vectors = masters
    vocab = embedding.shape[0]
    vector_rates = jnp.where(jnp.arange(vectors.shape[0])[:, None] < 4, LR_GAIN, LR_ROUTER)
    rate_list = (LR_EMBED, LR_MATRIX, LR_MATRIX, vector_rates)
    decay_list = (DECAY, DECAY, DECAY, 0.0)
    taken = []

    def replay(k, factors):
        state = (None, firsts[k], seconds[k])
        for s, factor in enumerate(factors):
            gradient = taken[s][k].astype(jnp.float32) * factor
            state = adam_move(
                *state, gradient, float(STEP0 + s + 1), rate_list[k], decay_list[k]
            )
        return state

    def left(k, count):
        return (1.0 - rate_list[k] * decay_list[k]) ** count

    def moved(k, factors):
        return left(k, len(factors)) * masters[k] - replay(k, factors)[0]

    loss_list, norm_list, factor_list = [], [], []
    vector_state = (vectors, firsts[3], seconds[3])
    for s in range(steps.shape[0]):
        ints = steps[s]
        if s:
            again = lax.optimization_barrier(tuple(factor_list))
            attn_low = lax.all_gather(
                moved(1, again).astype(jnp.bfloat16), "fsdp", axis=1, tiled=True
            )
            expert_low = moved(2, again).astype(jnp.bfloat16)
            embed_low = padded(moved(0, again).astype(jnp.bfloat16))
            x_low = fetch(n, slots, sizes, ints, embed_low)
        else:
            (embed_low, attn_low, expert_low), x_low = lows, x_start
        *grads, dvector, loss, norm_value, factor = run_step(
            n, slots, vocab, sizes, ints, vector_state[0], x_low, embed_low, attn_low, expert_low
        )
        loss, norm_value, factor = loss[0, 0], norm_value[0, 0], factor[0, 0]
        taken.append(grads)
        loss_list.append(loss)
        norm_list.append(norm_value)
        factor_list.append(factor)
        vector_gradient = dvector * factor
        vector_state = adam_update(
            *vector_state, vector_gradient, float(STEP0 + s + 1), vector_rates, 0.0
        )
    again = lax.optimization_barrier(tuple(factor_list))
    low_delta = lambda k, state: state[0].astype(jnp.bfloat16)
    expert_state = replay(2, again)
    expert_delta = low_delta(2, expert_state)
    expert_sum = lax.psum(expert_delta, "grp")
    *again, expert_delta = lax.optimization_barrier((*again, expert_delta))
    states = [replay(0, again), replay(1, again), expert_state, vector_state]
    attn_delta = low_delta(1, states[1])
    (embed_sum, attn_sum), vector_sum = sum_over_groups(
        (low_delta(0, states[0]), attn_delta.reshape(-1, D)), vectors - vector_state[0]
    )
    sums = (embed_sum, attn_sum.reshape(attn_delta.shape), expert_sum, vector_sum)
    results = [jnp.stack(loss_list)[None], jnp.stack(norm_list)[None]]
    for k in range(4):
        delta_mean = sums[k].astype(jnp.float32) * (1.0 / lax.axis_size("grp"))
        if k < 3:
            delta_mean = delta_mean + (1.0 - left(k, len(factor_list))) * masters[k]
        outer_new = OUTER_MOMENTUM * outers[k] + delta_mean
        master_new = masters[k] - OUTER_RATE * (delta_mean + OUTER_MOMENTUM * outer_new)
        if k == 3:
            results.append(vector_gradient[None])
        results += [states[k][1][None], states[k][2][None], master_new, outer_new]
        if k < 3:
            results.append(master_new.astype(jnp.bfloat16))
    return tuple(results)


def padded(embed_low):
    extra = -embed_low.shape[0] % 16
    return jnp.pad(embed_low, ((0, extra), (0, 0))) if extra else embed_low


def shards(
    tokens,
    routes,
    segments,
    loss_pos,
    embedding,
    embedding_first,
    embedding_second,
    embedding_outer,
    attention,
    attention_first,
    attention_second,
    attention_outer,
    experts,
    experts_first,
    experts_second,
    experts_outer,
    vectors,
    vectors_first,
    vectors_second,
    vectors_outer,
):
    inner_count = tokens.shape[0]
    vocab_shard = embedding.shape[0]
    n = lax.axis_size("fsdp")
    row_total = n * loss_pos.shape[2]
    slots = 48
    steps, fits = prepare(
        n, slots, vocab_shard, tokens[:, 0], routes[:, 0, :, 0], segments[:, 0], loss_pos[:, 0]
    )
    lows = (
        padded(embedding.astype(jnp.bfloat16)),
        lax.all_gather(attention.astype(jnp.bfloat16), "fsdp", axis=1, tiled=True),
        experts.astype(jnp.bfloat16),
    )
    sizes = (tokens.shape[2], loss_pos.shape[2])
    x_start = fetch(n, slots, sizes, steps[0], lows[0])
    state = (
        embedding,
        embedding_first,
        embedding_second,
        embedding_outer,
        attention,
        attention_first,
        attention_second,
        attention_outer,
        experts,
        experts_first,
        experts_second,
        experts_outer,
        vectors,
        vectors_first,
        vectors_second,
        vectors_outer,
    )

    def quick(*state):
        masters, firsts, seconds, outers = (
            [state[4 * k + part] for k in range(4)] for part in range(4)
        )
        firsts, seconds = [value[0] for value in firsts], [value[0] for value in seconds]
        return quick_window(
            n, slots, sizes, steps, x_start, lows, masters, firsts, seconds, outers
        )

    def general(*state):
        all_ids = lax.all_gather(tokens[:, 0, :], "fsdp", axis=1, tiled=True)
        step = functools.partial(general_step, tokens, routes, segments, loss_pos, all_ids)
        return window(step, *state, inner_count, row_total)

    return lax.cond(fits, quick, general, *state)


def solution(mesh):
    return jax.shard_map(
        shards,
        mesh=mesh,
        in_specs=(
            P(None, "grp", "fsdp"),
            P(None, "grp", "fsdp", None),
            P(None, "grp", "fsdp"),
            P(None, "grp", "fsdp"),
            P("fsdp", None),
            P("grp", "fsdp", None),
            P("grp", "fsdp", None),
            P("fsdp", None),
            P(None, "fsdp", None),
            P("grp", None, "fsdp", None),
            P("grp", None, "fsdp", None),
            P(None, "fsdp", None),
            P(None, None, None, "fsdp"),
            P("grp", None, None, None, "fsdp"),
            P("grp", None, None, None, "fsdp"),
            P(None, None, None, "fsdp"),
            P(),
            P("grp", None, None),
            P("grp", None, None),
            P(),
        ),
        out_specs=(
            P("grp", None),
            P("grp", None),
            P("grp", "fsdp", None),
            P("grp", "fsdp", None),
            P("fsdp", None),
            P("fsdp", None),
            P("fsdp", None),
            P("grp", None, "fsdp", None),
            P("grp", None, "fsdp", None),
            P(None, "fsdp", None),
            P(None, "fsdp", None),
            P(None, "fsdp", None),
            P("grp", None, None, None, "fsdp"),
            P("grp", None, None, None, "fsdp"),
            P(None, None, None, "fsdp"),
            P(None, None, None, "fsdp"),
            P(None, None, None, "fsdp"),
            P("grp", None, None),
            P("grp", None, None),
            P("grp", None, None),
            P(),
            P(),
        ),
        check_vma=False,
    )
```

```python
import functools
import math

import jax
import jax.numpy as jnp
from jax import lax
from jax.experimental import pallas as pl
from jax.experimental.pallas import tpu as pltpu
from jax.sharding import PartitionSpec as P

D = 768
HEADS = 12
HEAD_DIM = 64
EXPERTS = 2
STEP0 = 5
CAP = 192


HIGH = lax.Precision.HIGHEST
EPSILON = 1e-06
ATTN_GAIN = 8.0
SECOND_WEIGHT = 0.3
BETA_ONE = 0.9
BETA_TWO = 0.95
ADAM_EPS = 1e-08
DECAY = 0.1
LR_EMBED = 0.5
LR_MATRIX = 0.012
LR_GAIN = 0.3
LR_ROUTER = 0.012
OUTER_RATE = 0.7
OUTER_MOMENTUM = 0.9


def for_sending(value):

    def short(part):
        return part.astype(jnp.bfloat16) if part.dtype == jnp.float32 else part

    return jax.tree.map(short, value)


def smooth_act(values):
    return jax.nn.gelu(values, approximate=True)


def norm_apply(x, gain_row):
    factor = lax.rsqrt(jnp.mean(x * x, axis=-1, keepdims=True) + EPSILON)
    return (x * factor * gain_row, factor)


def norm_back(x, factor, gain_row, upstream):
    normed = x * factor
    gain_grad = jnp.sum(upstream * normed, axis=0)
    scaled = upstream * gain_row
    return (
        factor * (scaled - normed * jnp.mean(scaled * normed, axis=-1, keepdims=True)),
        gain_grad,
    )


def rows_forward(attn_low, vector_w, x_embed, seg_ids, pick_ids):
    a_float, a_factor = norm_apply(x_embed, vector_w[0])
    a = a_float.astype(jnp.bfloat16)
    a_rows = a[pick_ids]
    q = jnp.dot(a_rows, attn_low[0], preferred_element_type=jnp.float32).astype(jnp.bfloat16)
    k = jnp.dot(a, attn_low[1], preferred_element_type=jnp.float32).astype(jnp.bfloat16)
    v = jnp.dot(a, attn_low[2], preferred_element_type=jnp.float32).astype(jnp.bfloat16)
    places = jnp.arange(x_embed.shape[0])
    allowed = (places[None, :] <= pick_ids[:, None]) & (
        seg_ids[pick_ids][:, None] == seg_ids[None, :]
    )
    count = pick_ids.shape[0]
    head_of = jnp.arange(D) // HEAD_DIM
    head_mask = (head_of[None, None, :] == jnp.arange(HEADS)[:, None, None])
    q_wide = jnp.where(head_mask, q[None], 0).reshape(HEADS * count, D)
    scores = jnp.einsum("rd,td->rt", q_wide, k, preferred_element_type=jnp.float32) * HEAD_DIM ** (-0.5)
    allowed = jnp.tile(allowed, (HEADS, 1))
    scores = jnp.where(allowed, scores, -1e30)
    exponent = jnp.exp(scores - jnp.max(scores, axis=-1, keepdims=True))
    probs = exponent / jnp.sum(exponent, axis=-1, keepdims=True)
    spread = jnp.dot(probs.astype(jnp.bfloat16), v, preferred_element_type=jnp.float32)
    o = jnp.sum(jnp.where(head_mask, spread.reshape(HEADS, count, D), 0.0), axis=0).astype(jnp.bfloat16)
    x_attn = x_embed[pick_ids] + ATTN_GAIN * jnp.dot(o, attn_low[3], preferred_element_type=jnp.float32)
    return x_attn, (a_factor, a, a_rows, q_wide, k, v, probs, o, head_mask)


def rows_backward(attn_low, vector_w, x_embed, kept, dx_attn, pick_ids):
    a_factor, a, a_rows, q_wide, k, v, probs, o, head_mask = kept
    count = pick_ids.shape[0]
    dbranch = dx_attn.astype(jnp.bfloat16)
    dwout = ATTN_GAIN * jnp.dot(o.T, dbranch, preferred_element_type=jnp.float32)
    do = (ATTN_GAIN * jnp.dot(dbranch, attn_low[3].T, preferred_element_type=jnp.float32)).astype(jnp.bfloat16)
    do_wide = jnp.where(head_mask, do[None], 0).reshape(HEADS * count, D)
    dprobs = jnp.einsum("rd,td->rt", do_wide, v, preferred_element_type=jnp.float32)
    dscores = (probs * (dprobs - jnp.sum(probs * dprobs, axis=-1, keepdims=True))).astype(jnp.bfloat16)
    factor_qk = HEAD_DIM ** (-0.5)
    dq = jnp.dot(dscores, k, preferred_element_type=jnp.float32).reshape(HEADS, count, D)
    dq = (jnp.sum(jnp.where(head_mask, dq, 0.0), axis=0) * factor_qk).astype(jnp.bfloat16)
    dk = (jnp.dot(dscores.T, q_wide, preferred_element_type=jnp.float32) * factor_qk).astype(jnp.bfloat16)
    dv = jnp.dot(probs.astype(jnp.bfloat16).T, do_wide, preferred_element_type=jnp.float32).astype(jnp.bfloat16)
    dlayer = jnp.stack(
        [
            jnp.dot(a_rows.T, dq, preferred_element_type=jnp.float32),
            jnp.dot(a.T, dk, preferred_element_type=jnp.float32),
            jnp.dot(a.T, dv, preferred_element_type=jnp.float32),
            dwout,
        ]
    )
    places = jnp.arange(x_embed.shape[0])
    pick_mask = (places[:, None] == pick_ids[None, :]).astype(jnp.float32)
    dinput = jnp.dot(dk, attn_low[1].T, preferred_element_type=jnp.float32)
    dinput = dinput + jnp.dot(dv, attn_low[2].T, preferred_element_type=jnp.float32)
    dq_in = jnp.dot(dq, attn_low[0].T, preferred_element_type=jnp.float32)
    dinput = dinput + jnp.dot(pick_mask, dq_in, precision=HIGH)
    dx, gain_attn = norm_back(x_embed, a_factor, vector_w[0], dinput)
    return dx + jnp.dot(pick_mask, dx_attn, precision=HIGH), dlayer, gain_attn


def gather_rows(value, axis=0):
    return lax.all_gather(value, "fsdp", axis=axis, tiled=True)


def scatter_rows(value, axis=0):
    return lax.psum_scatter(
        value.astype(jnp.bfloat16), "fsdp", scatter_dimension=axis, tiled=True
    ).astype(jnp.float32)


TILE = 512
MESH = pl.DeviceIdType.MESH
F32 = jnp.float32
LOW = jnp.bfloat16
B_ROWS, Y_PART, HEAD_ROWS, TOPS, D_ROWS, DY_ROWS, DB_PART = range(7)
Q_ROWS, P_A, MIDDLE_ROWS, BRANCH_ROWS, DQ_ROWS, DS_A, G_OUT, D_VEC, SQUARES, EXCHANGES = range(7, 17)


def dot_nn(left, right):
    return lax.dot_general(left, right, (((1,), (0,)), ((), ())), preferred_element_type=F32)


def dot_nt(left, right):
    return lax.dot_general(left, right, (((1,), (1,)), ((), ())), preferred_element_type=F32)


def dot_tn(left, right):
    return lax.dot_general(left, right, (((0,), (0,)), ((), ())), preferred_element_type=F32)


def lanes(shape):
    return lax.broadcasted_iota(jnp.int32, shape, len(shape) - 1)


def sublanes(shape):
    return lax.broadcasted_iota(jnp.int32, shape, len(shape) - 2)


def norm_factor(x):
    return lax.rsqrt(jnp.mean(x * x, axis=-1, keepdims=True) + EPSILON)


def norm_grad(x, factor, gain_row, upstream):
    normed = x * factor
    scaled = upstream * gain_row
    back = factor * (scaled - normed * jnp.mean(scaled * normed, axis=-1, keepdims=True))
    return back, jnp.sum(upstream * normed, axis=0, keepdims=True)


GELU_C = math.sqrt(2.0 / math.pi)


def gelu_of(u):
    return 0.5 * u * (1.0 + jnp.tanh(GELU_C * (u + 0.044715 * (u * u * u))))


def gelu_slope(u):
    t = jnp.tanh(GELU_C * (u + 0.044715 * (u * u * u)))
    return 0.5 * (1.0 + t) + 0.5 * u * (1.0 - t * t) * GELU_C * (1.0 + 3.0 * 0.044715 * u * u)


class Links:
    def __init__(self, n, send, recv):
        self.n, self.send, self.recv = n, send, recv
        self.me = lax.axis_index("fsdp")

    def others(self, body):
        def one_step(k, carry):
            body(k, lax.rem(self.me + k, self.n))
            return carry

        lax.fori_loop(1, self.n, one_step, 0)

    def link(self, which, k, source, target, peer, origin):
        return pltpu.make_async_remote_copy(
            src_ref=source,
            dst_ref=target,
            send_sem=self.send.at[which, k],
            recv_sem=self.recv.at[which, origin],
            device_id={"fsdp": peer},
            device_id_type=MESH,
        )

    def greet(self, extra=0):
        barrier = pltpu.get_barrier_semaphore()
        self.others(
            lambda k, peer: pl.semaphore_signal(
                barrier, inc=1, device_id={"fsdp": peer}, device_id_type=MESH
            )
        )
        return barrier

    def spread(self, which, buffer):
        me = self.me
        self.others(
            lambda k, peer: self.link(which, k, buffer.at[me], buffer.at[me], peer, me).start()
        )

    def deal(self, which, source, target):
        me = self.me
        self.others(
            lambda k, peer: self.link(which, k, source.at[peer], target.at[me], peer, me).start()
        )

    def arrive(self, which, target):
        self.others(
            lambda k, peer: self.link(
                which, k, target.at[peer], target.at[peer], peer, peer
            ).wait_recv()
        )

    def sent(self, which, source):
        me = self.me
        self.others(
            lambda k, peer: self.link(
                which, k, source.at[peer], source.at[peer], peer, me
            ).wait_send()
        )

    def partners(self, body):
        def one_step(k, carry):
            body(k, lax.rem(self.me + 2 * k, self.n))
            return carry

        lax.fori_loop(1, self.n // 2, one_step, 0)

    def relay(self, which, buffer):
        me, twin = self.me, self.me + 1 - 2 * lax.rem(self.me, 2)
        self.link(which, self.n // 2, buffer.at[me], buffer.at[me], twin, me).start()
        self.partners(
            lambda k, peer: self.link(which, k, buffer.at[me], buffer.at[me], peer, me).start()
        )

    def relayed(self, which, buffer):
        me, twin = self.me, self.me + 1 - 2 * lax.rem(self.me, 2)
        n = self.n

        def pass_on(k, peer):
            copy = self.link(which, k, buffer.at[peer], buffer.at[peer], peer, peer)
            copy.wait_recv()
            self.link(which, n // 2 + k, buffer.at[peer], buffer.at[peer], twin, peer).start()

        self.partners(pass_on)

        def got(k, carry):
            origin = lax.rem(twin + 2 * k, n)
            self.link(which, k, buffer.at[origin], buffer.at[origin], twin, origin).wait_recv()
            return carry

        lax.fori_loop(0, n // 2, got, 0)

    def relay_sent(self, which, buffer):
        def gone(k, carry):
            peer = lax.rem(self.me + 1, self.n)
            self.link(which, k, buffer.at[0], buffer.at[0], peer, 0).wait_send()
            return carry

        lax.fori_loop(1, self.n, gone, 0)


def tiles_of(vocab_rows, body, carry):
    whole = vocab_rows // TILE
    carry = lax.fori_loop(
        0, whole, lambda i, c: body(i, pl.multiple_of(i * TILE, TILE), TILE, c), carry
    )
    if vocab_rows % TILE:
        carry = body(whole, whole * TILE, vocab_rows % TILE, carry)
    return carry


def rows_at_once(n, slots):
    return max(g for g in range(1, n + 1) if n % g == 0 and g * slots <= 512)


def share_kernel(n, groups, packed, everyone, worst, marks, send, recv, mark_send, mark_recv):
    links = Links(n, send, recv)
    me = links.me
    group = lax.axis_index("grp")

    def other_groups(body):
        for k in range(1, groups):
            body(k, lax.rem(group + k, groups))

    barrier = links.greet()
    other_groups(
        lambda k, peer: pl.semaphore_signal(
            barrier, inc=1, device_id={"grp": peer}, device_id_type=MESH
        )
    )
    pl.semaphore_wait(barrier, n - 1 + groups - 1)
    everyone[me] = packed[...]
    links.spread(0, everyone)
    links.arrive(0, everyone)
    most = everyone[0]
    for j in range(1, n):
        most = jnp.maximum(most, everyone[j])
    marks[group] = jnp.broadcast_to(most[:1, -128:], (8, 128))

    def mark(k, peer, origin):
        return pltpu.make_async_remote_copy(
            src_ref=marks.at[origin],
            dst_ref=marks.at[origin],
            send_sem=mark_send.at[k],
            recv_sem=mark_recv.at[origin],
            device_id={"grp": peer},
            device_id_type=MESH,
        )

    other_groups(lambda k, peer: mark(k, peer, group).start())
    other_groups(lambda k, peer: mark(k, peer, peer).wait_recv())
    most = marks[0]
    for j in range(1, groups):
        most = jnp.maximum(most, marks[j])
    worst[...] = most
    links.sent(0, everyone)
    other_groups(lambda k, peer: mark(k, peer, group).wait_send())


def share(n, packed):
    groups = lax.axis_size("grp")
    vmem = pl.BlockSpec(memory_space=pltpu.VMEM)
    return pl.pallas_call(
        functools.partial(share_kernel, n, groups),
        out_shape=(
            jax.ShapeDtypeStruct((n,) + packed.shape, jnp.int32),
            jax.ShapeDtypeStruct((8, 128), jnp.int32),
        ),
        in_specs=[vmem],
        out_specs=(vmem, vmem),
        scratch_shapes=[
            pltpu.VMEM((groups, 8, 128), jnp.int32),
            pltpu.SemaphoreType.DMA((1, n)),
            pltpu.SemaphoreType.DMA((1, n)),
            pltpu.SemaphoreType.DMA((groups,)),
            pltpu.SemaphoreType.DMA((groups,)),
        ],
        compiler_params=pltpu.CompilerParams(collective_id=1, has_side_effects=True),
        name="share_ids",
    )(packed)


def fetch_kernel(dims, ints, eb, x_out, id_s, xs, xr, send, recv):
    n, slots, vocab_rows, tokens, row_count = dims
    turned = ints[...].astype(F32).T.astype(jnp.int32)
    id_s[...] = turned[: n * slots, 0:1]
    slot_col = turned[:tokens, 1:2]
    links = Links(n, send, recv)
    me = links.me
    group = rows_at_once(n, slots)
    chunk = group * slots
    pl.semaphore_wait(links.greet(), n - 1)

    def look(c, carry):
        ids = id_s[pl.ds(pl.multiple_of(c * chunk, chunk), chunk), :]

        def add(i, start, size, acc):
            hit = (lanes((chunk, size)) + start == ids).astype(F32).astype(LOW)
            return acc + dot_nn(hit, eb[pl.ds(start, size), :])

        found = tiles_of(vocab_rows, add, jnp.zeros((chunk, D), F32))
        xs[pl.ds(c * group, group)] = found.astype(LOW).reshape(group, slots, D)
        return carry

    lax.fori_loop(0, n // group, look, 0)
    links.deal(0, xs, xr)
    xr[me] = xs[me]
    links.arrive(0, xr)
    x = jnp.zeros((tokens, D), F32)
    for c in range(n // group):
        hit = (lanes((tokens, chunk)) + c * chunk == slot_col).astype(F32).astype(LOW)
        x = x + dot_nn(hit, xr[c * group : (c + 1) * group].reshape(chunk, D))
    x_out[...] = x.astype(LOW)
    links.sent(0, xs)


def fetch(n, slots, sizes, ints, embed_low):
    vmem = pl.BlockSpec(memory_space=pltpu.VMEM)
    vocab_rows = embed_low.shape[0]
    return pl.pallas_call(
        functools.partial(fetch_kernel, (n, slots, vocab_rows) + sizes),
        out_shape=jax.ShapeDtypeStruct((sizes[0], D), LOW),
        in_specs=[vmem] * 2,
        out_specs=vmem,
        scratch_shapes=[
            pltpu.VMEM((n * slots, 1), jnp.int32),
            pltpu.VMEM((n, slots, D), LOW),
            pltpu.VMEM((n, slots, D), LOW),
            pltpu.SemaphoreType.DMA((1, n)),
            pltpu.SemaphoreType.DMA((1, n)),
        ],
        compiler_params=pltpu.CompilerParams(
            collective_id=2, has_side_effects=True, vmem_limit_bytes=40 * 1024 * 1024
        ),
        name="fetch_rows",
    )(ints, embed_low)


def packs(shard, wide):
    return wide == 192 and shard % 32 == 0


def step_kernel(
    dims,
    ints, vec, x_low, eb_in, attn_in, expw_in,
    dembed_out, dattn_out, dexp_out, dvec_out, loss_out, norm_out, factor_out,
    eb, attn, expw, xs, gr, ball, ys, yr, rows, tops, drs, drr, dyall, dbs, dbr,
    q_all, pas, par, middle_all, branch_all, dq_all, dss, dsr, dvec, sums, logit_s, dlog_s, pre_s, hid_s, dpre_s, flip_s, tile_s, part_s, hit_s,
    send, recv, out_sem, load_sem,
):
    n, slots, vocab, vocab_rows, hidden, tokens, row_count = dims
    all_rows = n * row_count
    wide = HEADS * row_count
    shard = D // n
    packed = packs(shard, wide)
    row_total = float(all_rows)
    scale = 2.0 * D ** (-0.5)
    factor_qk = HEAD_DIM ** (-0.5)
    links = Links(n, send, recv)
    me = links.me
    spread, deal, arrive, sent = links.spread, links.deal, links.arrive, links.sent
    relay, relayed = links.relay, links.relayed
    tiled = functools.partial(tiles_of, vocab_rows)
    loads = [
        pltpu.make_async_copy(source, target, load_sem.at[i])
        for i, (source, target) in enumerate(((attn_in, attn), (expw_in, expw), (eb_in, eb)))
    ]
    for load in loads:
        load.start()

    def added(buffer):
        total = buffer[0].astype(F32)
        for j in range(1, n):
            total = total + buffer[j].astype(F32)
        return total

    pl.semaphore_wait(links.greet(), n - 1)
    group = rows_at_once(n, slots)
    chunk = group * slots
    x = x_low[...].astype(F32)
    id_lane, slot_lane, pick_lane = ints[0:1, : n * slots], ints[1:2, :tokens], ints[2:3, :row_count]
    seg_lane, target_lane = ints[4:5, :tokens], ints[7:8, : 2 * all_rows]
    turned = ints[...].astype(F32).T.astype(jnp.int32)
    pick_col, seg_rows = turned[:row_count, 2:3], turned[:row_count, 3:4]
    route_col, route_all = turned[:row_count, 5:6], turned[:all_rows, 6:7]

    gain_a, gain_b, gain_c, gain_d = (vec[i : i + 1, :] for i in range(4))
    x_factor = norm_factor(x)
    a = (x * x_factor * gain_a).astype(LOW)
    pick = (lanes((row_count, tokens)) == pick_col).astype(F32).astype(LOW)
    x_rows = dot_nn(pick, x_low[...])
    a_rows = dot_nn(pick, a).astype(LOW)
    loads[0].wait()
    q = dot_nn(a_rows, attn[0]).astype(LOW)
    k = dot_nn(a, attn[1]).astype(LOW)
    v = dot_nn(a, attn[2]).astype(LOW)
    head_mask = (
        lax.shift_right_logical(lanes((HEADS, row_count, D)), HEAD_DIM.bit_length() - 1)
        == lax.broadcasted_iota(jnp.int32, (HEADS, row_count, D), 0)
    )

    def widen(low_rows):
        return (
            jnp.where(head_mask, low_rows.astype(F32)[None], 0.0).reshape(wide, D).astype(LOW)
        )

    def narrow(values):
        return jnp.sum(jnp.where(head_mask, values.reshape(HEADS, row_count, D), 0.0), axis=0)

    q_wide = widen(q)
    scores = dot_nt(q_wide, k) * factor_qk
    allowed = (lanes((row_count, tokens)) <= pick_col) & (seg_lane == seg_rows)
    scores = jnp.where(
        allowed[None], scores.reshape(HEADS, row_count, tokens), -1e30
    ).reshape(wide, tokens)
    exponent = jnp.exp(scores - jnp.max(scores, axis=-1, keepdims=True))
    probs = exponent / jnp.sum(exponent, axis=-1, keepdims=True)
    probs_low = probs.astype(LOW)
    o = narrow(dot_nn(probs_low, v)).astype(LOW)
    x_attn = x_rows + ATTN_GAIN * dot_nn(o, attn[3])

    b_factor = norm_factor(x_attn)
    b = x_attn * b_factor * gain_b
    ball[me] = b.astype(LOW)
    spread(B_ROWS, ball)
    router_rows = [vec[4 + e : 5 + e, :] for e in range(EXPERTS)]
    router_logits = [jnp.sum(b * row, axis=-1, keepdims=True) for row in router_rows]
    highest = router_logits[0]
    for value in router_logits[1:]:
        highest = jnp.maximum(highest, value)
    router_exp = [jnp.exp(value - highest) for value in router_logits]
    router_sum = sum(router_exp[1:], router_exp[0])
    router_probs = [value / router_sum for value in router_exp]
    chosen = [(route_col == e).astype(F32) for e in range(EXPERTS)]
    gate = sum([p * c for p, c in zip(router_probs[1:], chosen[1:])], router_probs[0] * chosen[0])
    q_all[me] = q
    a_turned = a.astype(F32).T.astype(LOW)
    eye = (sublanes((row_count, row_count)) == lanes((row_count, row_count))).astype(F32).astype(LOW)
    flipped = lambda low_rows: dot_tn(low_rows, eye)
    pas[:, :, 0:wide] = dot_nt(a_turned, probs_low).reshape(n, shard, wide).astype(LOW)
    pas[:, :, wide : wide + row_count] = flipped(a_rows).reshape(n, shard, row_count).astype(LOW)
    pas[:, :, wide + row_count :] = flipped(o).reshape(n, shard, row_count).astype(LOW)
    arrive(B_ROWS, ball)
    loads[1].wait()
    b_all = ball[...].reshape(all_rows, D)
    y_part = jnp.zeros((all_rows, D), F32)
    for e in range(EXPERTS):
        pre = dot_nn(b_all, expw[e, 0])
        pre_s[e] = pre
        hid = jnp.where(route_all == e, gelu_of(pre), 0.0).astype(LOW)
        hid_s[e] = hid
        y_part = y_part + dot_nt(hid, expw[e, 1])
    ys[...] = y_part.astype(LOW).reshape(n, row_count, D)
    deal(Y_PART, ys, yr)
    yr[me] = ys[me]
    arrive(Y_PART, yr)
    y = added(yr)
    z = x_attn + gate * y

    z_factor = norm_factor(z)
    first = (z * z_factor * gain_c).astype(LOW)
    middle = dot_nn(first, attn[4])
    middle_factor = norm_factor(middle)
    rows[me, 0] = first
    rows[me, 1] = (middle * middle_factor * gain_d).astype(LOW)
    relay(HEAD_ROWS, rows)
    relayed(HEAD_ROWS, rows)
    deal(P_A, pas, par)
    par[me] = pas[me]
    loads[2].wait()
    loss_rows = 2 * all_rows
    head_rows = rows[...].reshape(loss_rows, D)

    def target_hit(start, size):
        return sublanes((size, loss_rows)) + start == target_lane

    def logits_tile(i, start, size, carry):
        top, total, at_target = carry
        value = dot_nt(eb[pl.ds(start, size), :], head_rows) * scale
        if vocab_rows != vocab:
            value = jnp.where(sublanes((size, loss_rows)) + start < vocab, value, -1e30)
        logit_s[pl.ds(start, size), :] = value
        hit = target_hit(start, size)
        at_target = at_target + jnp.sum(jnp.where(hit, value, 0.0), axis=0, keepdims=True)
        new_top = jnp.maximum(top, jnp.max(value, axis=0, keepdims=True))
        total = total * jnp.exp(top - new_top) + jnp.sum(
            jnp.exp(value - new_top), axis=0, keepdims=True
        )
        return new_top, total, at_target

    nothing = jnp.zeros((1, loss_rows), F32)
    top, total, at_target = tiled(logits_tile, (nothing - 1e30, nothing, nothing))
    place = sublanes((8, loss_rows))
    tops[me] = jnp.where(
        place == 0, top, jnp.where(place == 1, total, jnp.where(place == 2, at_target, 0.0))
    )
    spread(TOPS, tops)
    arrive(TOPS, tops)
    relay(Q_ROWS, q_all)
    top = tops[0, 0:1]
    for j in range(1, n):
        top = jnp.maximum(top, tops[j, 0:1])
    total, at_target = nothing, nothing
    for j in range(n):
        total = total + tops[j, 1:2] * jnp.exp(tops[j, 0:1] - top)
        at_target = at_target + tops[j, 2:3]
    logsum = top + jnp.log(total)
    is_first = lax.rem(lanes((1, loss_rows)), 2 * row_count) < row_count
    weight = jnp.where(is_first, 1.0, SECOND_WEIGHT) / row_total
    loss = jnp.sum(weight * (logsum - at_target), axis=-1, keepdims=True)
    loss_out[...] = loss

    def dlogits_tile(i, start, size, acc):
        soft = jnp.exp(logit_s[pl.ds(start, size), :] - logsum)
        low = ((soft - target_hit(start, size).astype(F32)) * weight).astype(LOW)
        dlog_s[pl.ds(start, size), :] = low
        return acc + dot_tn(low, eb[pl.ds(start, size), :])

    drows = tiled(dlogits_tile, jnp.zeros((loss_rows, D), F32)) * scale
    drs[...] = drows.astype(LOW).reshape(n, 2 * row_count, D)
    deal(D_ROWS, drs, drr)
    drr[me] = drs[me]
    arrive(D_ROWS, drr)
    drow = added(drr)
    dmiddle, gain_mtp = norm_grad(middle, middle_factor, gain_d, drow[row_count:])
    dmiddle_low = dmiddle.astype(LOW)
    dfirst = drow[:row_count] + dot_nt(dmiddle_low, attn[4])
    dz, gain_final = norm_grad(z, z_factor, gain_c, dfirst)

    dgate = jnp.sum(dz * y, axis=-1, keepdims=True)
    dyall[me] = (gate * dz).astype(LOW)
    spread(DY_ROWS, dyall)
    arrive(DY_ROWS, dyall)
    middle_all[me] = dmiddle_low
    relay(MIDDLE_ROWS, middle_all)
    dy_all = dyall[...].reshape(all_rows, D)
    db_part = jnp.zeros((all_rows, D), F32)
    for e in range(EXPERTS):
        dhid = dot_nn(dy_all, expw[e, 1])
        slope = jnp.where(route_all == e, gelu_slope(pre_s[e]), 0.0)
        dpre = (slope * dhid).astype(LOW)
        dpre_s[e] = dpre
        db_part = db_part + dot_nt(dpre, expw[e, 0])
    dbs[...] = db_part.astype(LOW).reshape(n, row_count, D)
    deal(DB_PART, dbs, dbr)
    dbr[me] = dbs[me]
    squares = jnp.zeros((1, D), F32)

    def squared(values):
        return jnp.sum(values * values, axis=0, keepdims=True)

    hidden_squares = jnp.zeros((1, hidden), F32)
    for e in range(EXPERTS):
        up = dot_tn(b_all, dpre_s[e])
        down = dot_tn(dy_all, hid_s[e])
        dexp_out[e, 0] = up.astype(LOW)
        dexp_out[e, 1] = down.astype(LOW)
        hidden_squares = hidden_squares + squared(up) + squared(down)
    arrive(DB_PART, dbr)
    prob_grads = [c * dgate for c in chosen]
    mixed = sum([p * g for p, g in zip(router_probs[1:], prob_grads[1:])], router_probs[0] * prob_grads[0])
    dlogits = [p * (g - mixed) for p, g in zip(router_probs, prob_grads)]
    drouter = [jnp.sum(g * b, axis=0, keepdims=True) for g in dlogits]
    dnormed = added(dbr)
    for g, row in zip(dlogits, router_rows):
        dnormed = dnormed + g * row
    dx_part, gain_ffn = norm_grad(x_attn, b_factor, gain_b, dnormed)
    dx_attn = dz + dx_part

    dbranch = dx_attn.astype(LOW)
    branch_all[me] = dbranch
    relay(BRANCH_ROWS, branch_all)
    do = (ATTN_GAIN * dot_nt(dbranch, attn[3])).astype(LOW)
    do_wide = widen(do)
    dprobs = dot_nt(do_wide, v)
    dscores = (probs * (dprobs - jnp.sum(probs * dprobs, axis=-1, keepdims=True))).astype(LOW)
    dq = (narrow(dot_nn(dscores, k)) * factor_qk).astype(LOW)
    dq_all[me] = dq
    relay(DQ_ROWS, dq_all)
    dk = (dot_tn(dscores, q_wide) * factor_qk).astype(LOW)
    dv = dot_tn(probs_low, do_wide).astype(LOW)
    dinput = dot_nt(dk, attn[1]) + dot_nt(dv, attn[2])
    dx, gain_attn = norm_grad(x, x_factor, gain_a, dinput)
    row_back, gain_more = norm_grad(x_rows, norm_factor(x_rows), gain_a, dot_nt(dq, attn[0]))
    spots = (sublanes((tokens, row_count)) == pick_lane).astype(F32)
    dx = dx + lax.dot_general(
        spots, row_back + dx_attn, (((1,), (0,)), ((), ())), precision=HIGH,
        preferred_element_type=F32,
    )
    dx_low = dx.astype(LOW)
    for c in range(n // group):
        hit = (sublanes((chunk, tokens)) + c * chunk == slot_lane).astype(F32).astype(LOW)
        xs[c * group : (c + 1) * group] = dot_nn(hit, dx_low).astype(LOW).reshape(group, slots, D)
    deal(G_OUT, xs, gr)
    gr[me] = xs[me]
    line = sublanes((8, D))
    shares = jnp.zeros((8, D), F32)
    for i, value in enumerate([gain_attn + gain_more, gain_ffn, gain_final, gain_mtp] + drouter):
        shares = jnp.where(line == i, value, shares)
    dvec[me] = shares
    relay(D_VEC, dvec)
    turned_scores = dot_nt(a_turned, dscores).reshape(n, shard, wide)
    if packed:
        dss[:, 0:shard] = turned_scores[:, :, 0:128].astype(LOW)
        dss[:, shard:, 0 : wide - 128] = turned_scores[:, : shard // 2, 128:].astype(LOW)
        dss[:, shard:, wide - 128 :] = turned_scores[:, shard // 2 :, 128:].astype(LOW)
    else:
        dss[...] = turned_scores.astype(LOW)
    deal(DS_A, dss, dsr)
    dsr[me] = dss[me]

    mine = pl.ds(pl.multiple_of(me * shard, 8), shard)

    def own_slices(start, right):
        total = jnp.zeros((shard, D), F32)
        for j in range(n):
            total = total + dot_nn(par[j, :, start : start + row_count], right[j])
        return total

    def own_rows(left, right):
        flip_s[...] = left.astype(F32).reshape(all_rows, D).T
        return dot_nn(flip_s[mine, :].astype(LOW), right.reshape(all_rows, D))

    def keep(i, part):
        dattn_out[i] = part.astype(LOW)
        return squared(part)

    arrive(P_A, par)
    relayed(MIDDLE_ROWS, middle_all)
    squares = squares + keep(4, own_rows(rows[:, 0], middle_all[...]))
    relayed(BRANCH_ROWS, branch_all)
    squares = squares + keep(3, ATTN_GAIN * own_slices(wide + row_count, branch_all))
    do_all = ATTN_GAIN * dot_nt(branch_all[...].reshape(all_rows, D), attn[3])
    dvalue = jnp.zeros((shard, D), F32)
    for j in range(n):
        do_one = do_all[j * row_count : (j + 1) * row_count].astype(LOW)
        dvalue = dvalue + dot_nn(par[j, :, 0:wide], widen(do_one))
    squares = squares + keep(2, dvalue)

    def ready_tile(i, start, size, carry):
        part_s[pl.ds(start, size), :] = scale * dot_nn(dlog_s[pl.ds(start, size), :], head_rows)
        hit = (sublanes((size, n * slots)) + start == id_lane).astype(F32)
        hit_s[pl.ds(start, size), :] = hit.astype(LOW)
        return carry

    tiled(ready_tile, 0)
    arrive(G_OUT, gr)
    whole = vocab_rows // TILE

    def leave(i, start, size):
        slot = lax.rem(i, 2)
        return pltpu.make_async_copy(
            tile_s.at[slot, pl.ds(0, size)], dembed_out.at[pl.ds(start, size)], out_sem.at[slot]
        )

    def dembed_tile(i, start, size, acc):
        value = part_s[pl.ds(start, size), :] + dot_nn(
            hit_s[pl.ds(start, size), :], gr[...].reshape(n * slots, D)
        )

        def free():
            leave(i - 2, start - 2 * TILE, TILE).wait()

        if isinstance(i, int):
            if i >= 2:
                free()
        else:
            pl.when(i >= 2)(free)
        tile_s[lax.rem(i, 2), pl.ds(0, size)] = value.astype(LOW)
        leave(i, start, size).start()
        return acc + squared(value)

    squares = tiled(dembed_tile, squares)
    relayed(Q_ROWS, q_all)
    relayed(DQ_ROWS, dq_all)
    squares = squares + keep(0, own_slices(wide, dq_all))
    arrive(DS_A, dsr)
    dkey = jnp.zeros((shard, D), F32)
    for j in range(n):
        q_one = widen(q_all[j])
        if packed:
            tail = q_one[128:wide]
            upper = dot_nn(dsr[j, shard:, 0 : wide - 128], tail)
            lower = dot_nn(dsr[j, shard:, wide - 128 :], tail)
            dkey = dkey + dot_nn(dsr[j, 0:shard], q_one[0:128])
            dkey = dkey + jnp.concatenate([upper, lower], axis=0)
        else:
            dkey = dkey + dot_nn(dsr[j], q_one)
    squares = squares + keep(1, dkey * factor_qk)
    tiles = [(i, i * TILE, TILE) for i in range(whole)]
    if vocab_rows % TILE:
        tiles.append((whole, whole * TILE, vocab_rows % TILE))
    total_squares = jnp.sum(squares, axis=-1, keepdims=True) + jnp.sum(
        hidden_squares, axis=-1, keepdims=True
    )
    sums[me] = jnp.broadcast_to(total_squares, (8, 128))
    spread(SQUARES, sums)
    relayed(D_VEC, dvec)
    arrive(SQUARES, sums)
    shared = added(dvec)
    dvector = shared[0 : 4 + EXPERTS]
    dvec_out[...] = dvector
    own = jnp.sum(squared(dvector), axis=-1, keepdims=True)
    norm = jnp.sqrt(added(sums)[0:1, 0:1] + own)
    norm_out[...] = norm
    factor_out[...] = jnp.minimum(1.0, 0.05 / math.sqrt(row_total) / norm)
    for i, start, size in tiles[-2:]:
        leave(i, start, size).wait()
    for which, source in (
        (B_ROWS, ball), (Y_PART, ys), (TOPS, tops), (D_ROWS, drs), (DY_ROWS, dyall),
        (DB_PART, dbs), (P_A, pas), (DS_A, dss), (G_OUT, xs), (SQUARES, sums),
    ):
        sent(which, source)
    for which, source in (
        (HEAD_ROWS, rows), (Q_ROWS, q_all), (MIDDLE_ROWS, middle_all),
        (BRANCH_ROWS, branch_all), (DQ_ROWS, dq_all), (D_VEC, dvec),
    ):
        links.relay_sent(which, source)


def run_step(n, slots, vocab, sizes, ints, vec, x_low, embed_low, attn_low, expert_low):
    vocab_rows = embed_low.shape[0]
    row_count = sizes[1]
    hidden = expert_low.shape[3]
    shard = D // n
    all_rows = n * row_count
    wide = HEADS * row_count
    score_shape = (n, shard + shard // 2, 128) if packs(shard, wide) else (n, shard, wide)
    vmem = pl.BlockSpec(memory_space=pltpu.VMEM)
    anywhere = pl.BlockSpec(memory_space=pl.ANY)
    low = lambda *shape: pltpu.VMEM(shape, LOW)
    wide_float = lambda *shape: pltpu.VMEM(shape, F32)
    outs = pl.pallas_call(
        functools.partial(step_kernel, (n, slots, vocab, vocab_rows, hidden) + sizes),
        out_shape=(
            jax.ShapeDtypeStruct((vocab_rows, D), LOW),
            jax.ShapeDtypeStruct((5, shard, D), LOW),
            jax.ShapeDtypeStruct((EXPERTS, 2, D, hidden), LOW),
            jax.ShapeDtypeStruct((4 + EXPERTS, D), F32),
            jax.ShapeDtypeStruct((1, 1), F32),
            jax.ShapeDtypeStruct((1, 1), F32),
            jax.ShapeDtypeStruct((1, 1), F32),
        ),
        in_specs=[vmem] * 3 + [anywhere] * 3,
        out_specs=(anywhere, vmem, vmem, vmem, vmem, vmem, vmem),
        scratch_shapes=[
            low(vocab_rows, D), low(5, D, D), low(EXPERTS, 2, D, hidden),
            low(n, slots, D), low(n, slots, D),
            low(n, row_count, D), low(n, row_count, D), low(n, row_count, D),
            low(n, 2, row_count, D), wide_float(n, 8, 2 * all_rows),
            low(n, 2 * row_count, D), low(n, 2 * row_count, D),
            low(n, row_count, D), low(n, row_count, D), low(n, row_count, D),
            low(n, row_count, D), low(n, shard, wide + 2 * row_count),
            low(n, shard, wide + 2 * row_count),
            low(n, row_count, D), low(n, row_count, D), low(n, row_count, D),
            low(*score_shape), low(*score_shape),
            wide_float(n, 8, D), wide_float(n, 8, 128),
            wide_float(vocab_rows, 2 * all_rows), low(vocab_rows, 2 * all_rows),
            wide_float(EXPERTS, all_rows, hidden), low(EXPERTS, all_rows, hidden),
            low(EXPERTS, all_rows, hidden), wide_float(D, all_rows), low(2, TILE, D),
            wide_float(vocab_rows, D), low(vocab_rows, n * slots),
            pltpu.SemaphoreType.DMA((EXCHANGES, n)),
            pltpu.SemaphoreType.DMA((EXCHANGES, n)),
            pltpu.SemaphoreType.DMA((2,)),
            pltpu.SemaphoreType.DMA((3,)),
        ],
        compiler_params=pltpu.CompilerParams(
            collective_id=3, has_side_effects=True, vmem_limit_bytes=60 * 1024 * 1024
        ),
        name="inner_step",
    )(ints, vec, x_low, embed_low, attn_low, expert_low)
    return (outs[0][:vocab],) + outs[1:]


def sum_kernel(shapes, *refs):
    count = len(shapes)
    values, vector, refs = refs[:count], refs[count], refs[count + 1 :]
    totals, vector_total, refs = refs[:count], refs[count], refs[count + 1 :]
    helds, first_ins, second_ins, rests, nears = (
        refs[i * count : (i + 1) * count] for i in range(5)
    )
    flat, load_sem, *sems = refs[5 * count :]
    loads = [
        pltpu.make_async_copy(value, near, load_sem.at[array])
        for array, (value, near) in enumerate(zip(values, nears))
    ]
    for load in loads:
        load.start()
    one_s, one_r, two_s, two_r, three_s, three_r, four_s, four_r, rest_s, rest_r = sems
    group = lax.axis_index("grp")
    width = D // 2
    bits = (lax.rem(group, 2), lax.div(group, 2))
    flip = lambda bit: group + (1 - 2 * bits[bit]) * (1 + bit)
    barrier = pltpu.get_barrier_semaphore()
    for k in range(1, 4):
        pl.semaphore_signal(
            barrier, inc=1, device_id={"grp": lax.rem(group + k, 4)}, device_id_type=MESH
        )
    pl.semaphore_wait(barrier, 3)
    units = [
        (array, side, piece, piece * 2 + side)
        for array, (rows, quarter, pieces) in enumerate(shapes)
        for piece in range(pieces)
        for side in range(2)
    ]

    def place(u, first_bit, second_bit):
        array, side, piece, slot = units[u]
        rows, quarter, pieces = shapes[array]
        size = quarter // pieces
        owner = first_bit + 2 * second_bit if side == 0 else second_bit + 2 * first_bit
        start = pl.multiple_of((owner * pieces + piece) * size, 16)
        return pl.ds(start, size), pl.ds(side * width, width)

    def copy(source, target, send, recv, peer):
        return pltpu.make_async_remote_copy(
            src_ref=source, dst_ref=target, send_sem=send, recv_sem=recv,
            device_id={"grp": peer}, device_id_type=MESH,
        )

    def stage_one(u, turn):
        array, side, piece, slot = units[u]
        here, there = bits[side], bits[1 - side]
        out = place(u, 1 - here, there if turn else 1 - there)
        return copy(
            values[array].at[out], first_ins[array].at[slot, turn],
            one_s.at[u, turn], one_r.at[u, turn], flip(side),
        )

    def stage_two(u):
        array, side, piece, slot = units[u]
        return copy(
            helds[array].at[slot, 0], second_ins[array].at[slot], two_s.at[u], two_r.at[u], flip(1 - side)
        )

    def stage_three(u, other=False):
        array, side, piece, slot = units[u]
        there = bits[1 - side]
        block = totals[array].at[place(u, bits[side], 1 - there if other else there)]
        return copy(block, block, three_s.at[u], three_r.at[u], flip(1 - side))

    def stage_four(u, turn, other=False):
        array, side, piece, slot = units[u]
        here, there = bits[side], bits[1 - side]
        block = totals[array].at[
            place(u, 1 - here if other else here, there if turn == 0 else 1 - there)
        ]
        return copy(block, block, four_s.at[u, turn], four_r.at[u, turn], flip(side))

    every = range(len(units))
    for turn in range(2):
        for u in every:
            stage_one(u, turn).start()
    for load in loads:
        load.wait()
    flat[group] = vector[...]
    smalls = [(count, flat)]
    for array, (rows, quarter, pieces) in enumerate(shapes):
        spare = rows - 4 * quarter
        if spare:
            rests[array][group, 0:spare] = nears[array][4 * quarter : rows]
            smalls.append((array, rests[array]))

    def small(which, buffer, k, peer, origin):
        return copy(
            buffer.at[origin], buffer.at[origin], rest_s.at[which, k], rest_r.at[which, origin], peer
        )

    for which, buffer in smalls:
        for k in range(1, 4):
            small(which, buffer, k, lax.rem(group + k, 4), group).start()
    for turn in range(2):
        for u in every:
            array, side, piece, slot = units[u]
            there = bits[1 - side]
            stage_one(u, turn).wait_recv()
            mine = place(u, bits[side], there if turn else 1 - there)
            helds[array][slot, turn] = (
                nears[array][mine].astype(F32) + first_ins[array][slot, turn].astype(F32)
            ).astype(LOW)
            if turn == 0:
                stage_two(u).start()
    for u in every:
        array, side, piece, slot = units[u]
        stage_two(u).wait_recv()
        mine = place(u, bits[side], bits[1 - side])
        totals[array][mine] = (
            helds[array][slot, 1].astype(F32) + second_ins[array][slot].astype(F32)
        ).astype(LOW)
        stage_three(u).start()
        stage_four(u, 0).start()
    for u in every:
        stage_three(u, True).wait_recv()
        stage_four(u, 1).start()
    for which, buffer in smalls:
        for k in range(1, 4):
            origin = lax.rem(group + k, 4)
            small(which, buffer, k, origin, origin).wait_recv()
    added = lambda buffer: (buffer[0].astype(F32) + buffer[1].astype(F32)) + (
        buffer[2].astype(F32) + buffer[3].astype(F32)
    )
    vector_total[...] = added(flat)
    for array, buffer in smalls[1:]:
        rows, quarter, pieces = shapes[array]
        totals[array][4 * quarter : rows] = added(buffer)[0 : rows - 4 * quarter].astype(LOW)
    for u in every:
        for turn in range(2):
            stage_four(u, turn, True).wait_recv()
    for u in every:
        stage_two(u).wait_send()
        stage_three(u).wait_send()
        for turn in range(2):
            stage_one(u, turn).wait_send()
            stage_four(u, turn).wait_send()
    for which, buffer in smalls:
        for k in range(1, 4):
            small(which, buffer, k, lax.rem(group + k, 4), group).wait_send()


def sum_over_groups(values, vector):
    shapes = []
    for value in values:
        rows = value.shape[0]
        quarter = rows // 64 * 16
        shapes.append((rows, quarter, 2 if quarter % 32 == 0 and quarter > 256 else 1))
    units = sum(2 * pieces for rows, quarter, pieces in shapes)
    vmem = pl.BlockSpec(memory_space=pltpu.VMEM)
    scratch = []
    for lead in ((2,), (2,), ()):
        for rows, quarter, pieces in shapes:
            scratch.append(pltpu.VMEM((2 * pieces,) + lead + (quarter // pieces, D // 2), LOW))
    for rows, quarter, pieces in shapes:
        spare = -(-(rows - 4 * quarter) // 16) * 16
        scratch.append(pltpu.VMEM((4, max(spare, 16), D), LOW))
    dma = pltpu.SemaphoreType.DMA
    count = len(values)
    *totals, vector_total = pl.pallas_call(
        functools.partial(sum_kernel, tuple(shapes)),
        out_shape=[jax.ShapeDtypeStruct(value.shape, LOW) for value in values]
        + [jax.ShapeDtypeStruct(vector.shape, F32)],
        in_specs=[pl.BlockSpec(memory_space=pl.ANY)] * count + [vmem],
        out_specs=[vmem] * (count + 1),
        scratch_shapes=scratch
        + [pltpu.VMEM(value.shape, LOW) for value in values]
        + [
            pltpu.VMEM((4,) + vector.shape, F32),
            dma((count,)),
            dma((units, 2)), dma((units, 2)), dma((units,)), dma((units,)), dma((units,)),
            dma((units,)), dma((units, 2)), dma((units, 2)), dma((count + 1, 4)), dma((count + 1, 4)),
        ],
        compiler_params=pltpu.CompilerParams(
            collective_id=4, has_side_effects=True, vmem_limit_bytes=52 * 1024 * 1024
        ),
        cost_estimate=pl.CostEstimate(flops=0, bytes_accessed=300_000_000, transcendentals=0),
        name="sum_groups",
    )(*values, vector)
    return totals, vector_total


def prepare(n, slots, vocab, tokens, routes, segments, loss_pos):
    steps, count = tokens.shape
    start = lax.axis_index("fsdp") * vocab
    row_count = loss_pos.shape[1]
    owner = tokens // vocab
    places = jnp.arange(count)
    earlier = places[None, None, :] < places[None, :, None]
    same = tokens[:, :, None] == tokens[:, None, :]
    first = jnp.logical_not(jnp.any(same & earlier, axis=2))
    same_owner = owner[:, :, None] == owner[:, None, :]
    rank = jnp.sum((same_owner & earlier & first[:, None, :]).astype(jnp.int32), axis=2)
    own_slot = owner * slots + rank
    slot = jnp.sum(jnp.where(same & first[:, None, :], own_slot[:, None, :], 0), axis=2)
    at_slot = (own_slot[:, :, None] == jnp.arange(n * slots)[None, None, :]) & first[:, :, None]
    ids = jnp.sum(jnp.where(at_slot, tokens[:, :, None] + 1, 0), axis=1) - 1
    picked = loss_pos[:, :, None] == places[None, None, :]
    shifted = lambda by: jnp.sum(
        jnp.where(loss_pos[:, :, None] + by == places[None, None, :], tokens[:, None, :], 0), axis=2
    )
    row_routes = jnp.sum(jnp.where(picked, routes[:, None, :], 0), axis=2)
    row_segs = jnp.sum(jnp.where(picked, segments[:, None, :], 0), axis=2)
    most = jnp.broadcast_to(jnp.max(jnp.where(first, rank, 0)), (steps, 128))
    filler = jnp.zeros((steps, -(n * slots + 3 * row_count) % 128), jnp.int32)
    packed = jnp.concatenate([ids, row_routes, shifted(1), shifted(2), filler, most], axis=1)
    everyone, worst = share(n, packed)
    fits = worst[0, 127] < slots
    wanted = lax.dynamic_slice_in_dim(everyone, lax.axis_index("fsdp") * slots, slots, axis=2) - start
    after = n * slots
    rows = lambda part: jnp.swapaxes(part, 0, 1).reshape(steps, -1)
    lines = [
        rows(wanted),
        slot,
        loss_pos,
        row_segs,
        segments,
        row_routes,
        rows(everyone[:, :, after : after + row_count]),
        rows(everyone[:, :, after + row_count : after + 3 * row_count]) - start,
    ]
    longest = -(-max(line.shape[1] for line in lines) // 128) * 128
    fill = lambda line: jnp.pad(line, ((0, 0), (0, longest - line.shape[1])))
    result = jnp.stack([fill(line) for line in lines], axis=1)
    return result, fits


def general_step(tokens, routes, segments, loss_pos, all_ids, inner_step, weights):
    embed_w, attn_w, expert_w, vector_w = weights
    vocab_shard = embed_w.shape[0]
    vocab_start = lax.axis_index("fsdp") * vocab_shard
    row_total = lax.axis_size("fsdp") * loss_pos.shape[2]
    logit_scale = 2.0 * D ** (-0.5)
    vocab_places = jnp.arange(vocab_shard)
    head_weights = jnp.array([1.0, SECOND_WEIGHT], jnp.float32)
    embed_low = embed_w.astype(jnp.bfloat16)
    attn_low = lax.all_gather(attn_w.astype(jnp.bfloat16), "fsdp", axis=1, tiled=True)
    expert_low = expert_w.astype(jnp.bfloat16)
    ids_group = all_ids[inner_step]
    ids_local = tokens[inner_step, 0]
    seg_ids = segments[inner_step, 0]
    route_ids = routes[inner_step, 0, :, 0]
    pick_ids = loss_pos[inner_step, 0]
    chosen = ids_group - vocab_start
    inside = (chosen >= 0) & (chosen < vocab_shard)
    looked = jnp.take(embed_low, jnp.clip(chosen, 0, vocab_shard - 1), axis=0).astype(
        jnp.float32
    )
    x_embed = lax.psum_scatter(
        jnp.where(inside[:, None], looked, 0.0).astype(jnp.bfloat16),
        "fsdp",
        scatter_dimension=0,
        tiled=True,
    ).astype(jnp.float32)
    x_attn, kept = rows_forward(attn_low, vector_w, x_embed, seg_ids, pick_ids)
    b, b_factor = norm_apply(x_attn, vector_w[1])
    router_probs = jax.nn.softmax(jnp.dot(b, vector_w[4:].T, precision=HIGH), axis=-1)
    row_routes = route_ids[pick_ids]
    onehot = (row_routes[:, None] == jnp.arange(EXPERTS)[None, :]).astype(jnp.float32)
    gating = jnp.sum(router_probs * onehot, axis=1)
    b_all = gather_rows(b.astype(jnp.bfloat16))
    routes_all = gather_rows(row_routes)
    route_mask = routes_all[None, :, None] == jnp.arange(EXPERTS)[:, None, None]
    hidden_pre = jnp.einsum("cd,edf->ecf", b_all, expert_low[:, 0], preferred_element_type=jnp.float32)
    hidden_act = jnp.where(route_mask, smooth_act(hidden_pre), 0.0).astype(jnp.bfloat16)
    y_part = jnp.einsum("ecf,edf->cd", hidden_act, expert_low[:, 1], preferred_element_type=jnp.float32)
    returned = scatter_rows(y_part)
    z_rows = x_attn + gating[:, None] * returned
    first_float, first_factor = norm_apply(z_rows, vector_w[2])
    first_rows = first_float.astype(jnp.bfloat16)
    middle = jnp.dot(first_rows, attn_low[4], preferred_element_type=jnp.float32)
    second_float, second_factor = norm_apply(middle, vector_w[3])
    targets = jnp.stack([ids_local[pick_ids + 1], ids_local[pick_ids + 2]])
    rows_all, targets_all = (
        lax.all_gather(
            jnp.stack([first_rows, second_float.astype(jnp.bfloat16)]),
            "fsdp",
            axis=1,
            tiled=True,
        ),
        lax.all_gather(targets, "fsdp", axis=1, tiled=True),
    )
    logits = (
        jnp.einsum("jrd,vd->jrv", rows_all, embed_low, preferred_element_type=jnp.float32)
        * logit_scale
    )
    relative = targets_all - vocab_start
    onehot_target = (vocab_places[None, None, :] == relative[:, :, None]).astype(jnp.float32)
    target_part = jnp.sum(onehot_target * logits, axis=-1)
    local_top = jnp.max(logits, axis=-1)
    local_sum = jnp.sum(jnp.exp(logits - local_top[:, :, None]), axis=-1)
    parts = lax.all_gather(jnp.stack([local_top, local_sum, target_part]), "fsdp")
    row_top = jnp.max(parts[:, 0], axis=0)
    sum_exp = jnp.sum(parts[:, 1] * jnp.exp(parts[:, 0] - row_top), axis=0)
    target_logit = jnp.sum(parts[:, 2], axis=0)
    logsum = row_top + jnp.log(sum_exp)
    loss = (jnp.sum(head_weights[:, None] * (logsum - target_logit)) / row_total)
    dlogits = (
        (jnp.exp(logits - logsum[:, :, None]) - onehot_target)
        * (head_weights / row_total)[:, None, None]
    ).astype(jnp.bfloat16)
    dembed = (
        jnp.einsum("jrv,jrd->vd", dlogits, rows_all, preferred_element_type=jnp.float32)
        * logit_scale
    )
    drows = (
        jnp.einsum("jrv,vd->jrd", dlogits, embed_low, preferred_element_type=jnp.float32)
        * logit_scale
    )
    drows_own = lax.psum_scatter(
        drows.astype(jnp.bfloat16), "fsdp", scatter_dimension=1, tiled=True
    ).astype(jnp.float32)
    dmiddle, gain_mtp = norm_back(middle, second_factor, vector_w[3], drows_own[1])
    dmiddle_low = dmiddle.astype(jnp.bfloat16)
    dsecond_proj = jnp.dot(first_rows.T, dmiddle_low, preferred_element_type=jnp.float32)
    dfirst = drows_own[0] + jnp.dot(
        dmiddle_low, attn_low[4].T, preferred_element_type=jnp.float32
    )
    dz_rows, gain_final = norm_back(z_rows, first_factor, vector_w[2], dfirst)
    dgating = jnp.sum(dz_rows * returned, axis=1)
    dy_all = gather_rows((gating[:, None] * dz_rows).astype(jnp.bfloat16))
    dy_masked = jnp.where(route_mask, dy_all[None], 0)
    down_grad = jnp.einsum("ecf,ecd->edf", hidden_act, dy_masked, preferred_element_type=jnp.float32)
    dhidden = jnp.einsum("ecd,edf->ecf", dy_masked, expert_low[:, 1], preferred_element_type=jnp.float32)
    unused, act_back = jax.vjp(smooth_act, hidden_pre)
    dhidden_pre = act_back(dhidden)[0].astype(jnp.bfloat16)
    up_grad = jnp.einsum("cd,ecf->edf", b_all, dhidden_pre, preferred_element_type=jnp.float32)
    dexpert = jnp.stack([up_grad, down_grad], axis=1)
    db_part = jnp.einsum("ecf,edf->cd", dhidden_pre, expert_low[:, 0], preferred_element_type=jnp.float32)
    dnormed = scatter_rows(db_part)
    prob_grad = onehot * dgating[:, None]
    dlogit = router_probs * (prob_grad - jnp.sum(router_probs * prob_grad, axis=1, keepdims=True))
    drouter = jnp.dot(dlogit.T, b, precision=HIGH)
    dnormed = dnormed + jnp.dot(dlogit, vector_w[4:], precision=HIGH)
    dx_part, gain_ffn = norm_back(x_attn, b_factor, vector_w[1], dnormed)
    dx_embed, dlayer, gain_attn = rows_backward(
        attn_low, vector_w, x_embed, kept, dz_rows + dx_part, pick_ids
    )
    dattn = scatter_rows(jnp.concatenate([dlayer, dsecond_proj[None]], axis=0), axis=1)
    gather_chosen = ids_group - vocab_start
    gather_inside = (gather_chosen >= 0) & (gather_chosen < vocab_shard)
    seg_index = jnp.where(gather_inside, gather_chosen, vocab_shard)
    added = jax.ops.segment_sum(
        lax.all_gather(dx_embed.astype(jnp.bfloat16), "fsdp", axis=0, tiled=True).astype(
            jnp.float32
        ),
        seg_index,
        num_segments=vocab_shard + 1,
    )
    dembed = dembed + added[:vocab_shard]
    dvector_part = jnp.concatenate(
        [jnp.stack([gain_attn, gain_ffn, gain_final, gain_mtp]), drouter], axis=0
    )
    squares = jnp.sum(dembed * dembed) + jnp.sum(dattn * dattn) + jnp.sum(dexpert * dexpert)
    dvector, squares_all = lax.psum((dvector_part, squares), "fsdp")
    return dembed, dattn, dexpert, dvector, squares_all, loss


def adam_update(weight, first_moment, second, gradient, step_float, rate_here, decay_here):
    first_new = BETA_ONE * first_moment + (1.0 - BETA_ONE) * gradient
    second_new = BETA_TWO * second + (1.0 - BETA_TWO) * gradient * gradient
    first_hat = first_new / (1.0 - BETA_ONE**step_float)
    second_hat = second_new / (1.0 - BETA_TWO**step_float)
    weight_new = weight - rate_here * (
        first_hat / (jnp.sqrt(second_hat) + ADAM_EPS) + decay_here * weight
    )
    return (weight_new, first_new, second_new)


def window(
    step,
    embedding,
    embedding_first,
    embedding_second,
    embedding_outer,
    attention,
    attention_first,
    attention_second,
    attention_outer,
    experts,
    experts_first,
    experts_second,
    experts_outer,
    vectors,
    vectors_first,
    vectors_second,
    vectors_outer,
    inner_count,
    row_total,
):
    group_count = lax.axis_size("grp")
    threshold = 0.05 / math.sqrt(row_total)
    vector_rates = jnp.where(jnp.arange(vectors.shape[0])[:, None] < 4, LR_GAIN, LR_ROUTER)
    rate_list = (LR_EMBED, LR_MATRIX, LR_MATRIX, vector_rates)
    decay_list = (DECAY, DECAY, DECAY, 0.0)
    weights_now = (embedding, attention, experts, vectors)
    first_now = (embedding_first[0], attention_first[0], experts_first[0], vectors_first[0])
    second_now = (embedding_second[0], attention_second[0], experts_second[0], vectors_second[0])
    loss_list = []
    norm_list = []
    for inner_step in range(inner_count):
        dembed, dattn, dexpert, dvector, squares_all, loss = step(inner_step, weights_now)
        loss_list.append(loss)
        norm_value = jnp.sqrt(squares_all + jnp.sum(dvector * dvector))
        norm_list.append(norm_value)
        factor = jnp.minimum(1.0, threshold / norm_value)
        gradients = (dembed * factor, dattn * factor, dexpert * factor, dvector * factor)
        step_float = float(STEP0 + inner_step + 1)
        results = [
            adam_update(
                weights_now[k],
                first_now[k],
                second_now[k],
                gradients[k],
                step_float,
                rate_list[k],
                decay_list[k],
            )
            for k in range(4)
        ]
        weights_now = tuple((element[0] for element in results))
        first_now = tuple((element[1] for element in results))
        second_now = tuple((element[2] for element in results))
    masters = (embedding, attention, experts, vectors)
    outers = (embedding_outer, attention_outer, experts_outer, vectors_outer)
    deltas = tuple((master - current for master, current in zip(masters, weights_now)))
    summed = jax.tree.map(
        lambda part: part.astype(jnp.float32), lax.psum(for_sending(deltas), "grp")
    )
    new_outer = []
    new_master = []
    for k in range(4):
        delta_mean = summed[k] / group_count
        outer_new = OUTER_MOMENTUM * outers[k] + delta_mean
        new_outer.append(outer_new)
        new_master.append(masters[k] - OUTER_RATE * (delta_mean + OUTER_MOMENTUM * outer_new))
    return (
        jnp.stack(loss_list)[None],
        jnp.stack(norm_list)[None],
        first_now[0][None],
        second_now[0][None],
        new_master[0],
        new_outer[0],
        new_master[0].astype(jnp.bfloat16),
        first_now[1][None],
        second_now[1][None],
        new_master[1],
        new_outer[1],
        new_master[1].astype(jnp.bfloat16),
        first_now[2][None],
        second_now[2][None],
        new_master[2],
        new_outer[2],
        new_master[2].astype(jnp.bfloat16),
        gradients[3][None],
        first_now[3][None],
        second_now[3][None],
        new_master[3],
        new_outer[3],
    )


def adam_move(move, first_moment, second, gradient, step_float, rate_here, decay_here):
    first_new = BETA_ONE * first_moment + (1.0 - BETA_ONE) * gradient
    second_new = BETA_TWO * second + (1.0 - BETA_TWO) * gradient * gradient
    first_hat = first_new * (1.0 / (1.0 - BETA_ONE**step_float))
    second_hat = second_new * (1.0 / (1.0 - BETA_TWO**step_float))
    step = rate_here * (first_hat / (jnp.sqrt(second_hat) + ADAM_EPS))
    if move is not None:
        step = (1.0 - rate_here * decay_here) * move + step
    return (step, first_new, second_new)


def quick_window(n, slots, sizes, steps, x_start, lows, masters, firsts, seconds, outers):
    embedding, attention, experts, vectors = masters
    vocab = embedding.shape[0]
    vector_rates = jnp.where(jnp.arange(vectors.shape[0])[:, None] < 4, LR_GAIN, LR_ROUTER)
    rate_list = (LR_EMBED, LR_MATRIX, LR_MATRIX, vector_rates)
    decay_list = (DECAY, DECAY, DECAY, 0.0)
    taken = []

    def replay(k, factors):
        state = (None, firsts[k], seconds[k])
        for s, factor in enumerate(factors):
            gradient = taken[s][k].astype(jnp.float32) * factor
            state = adam_move(
                *state, gradient, float(STEP0 + s + 1), rate_list[k], decay_list[k]
            )
        return state

    def left(k, count):
        return (1.0 - rate_list[k] * decay_list[k]) ** count

    def moved(k, factors):
        return left(k, len(factors)) * masters[k] - replay(k, factors)[0]

    loss_list, norm_list, factor_list = [], [], []
    vector_state = (vectors, firsts[3], seconds[3])
    for s in range(steps.shape[0]):
        ints = steps[s]
        if s:
            again = lax.optimization_barrier(tuple(factor_list))
            attn_low = lax.all_gather(
                moved(1, again).astype(jnp.bfloat16), "fsdp", axis=1, tiled=True
            )
            expert_low = moved(2, again).astype(jnp.bfloat16)
            embed_low = padded(moved(0, again).astype(jnp.bfloat16))
            x_low = fetch(n, slots, sizes, ints, embed_low)
        else:
            (embed_low, attn_low, expert_low), x_low = lows, x_start
        *grads, dvector, loss, norm_value, factor = run_step(
            n, slots, vocab, sizes, ints, vector_state[0], x_low, embed_low, attn_low, expert_low
        )
        factor = factor[0, 0]
        taken.append(grads)
        loss_list.append(loss)
        norm_list.append(norm_value)
        factor_list.append(factor)
        vector_gradient = dvector * factor
        vector_state = adam_update(
            *vector_state, vector_gradient, float(STEP0 + s + 1), vector_rates, 0.0
        )
    again = lax.optimization_barrier(tuple(factor_list))
    low_delta = lambda k, state: state[0].astype(jnp.bfloat16)
    expert_state = replay(2, again)
    expert_delta = low_delta(2, expert_state)
    expert_sum = lax.psum(expert_delta, "grp")
    *again, expert_delta = lax.optimization_barrier((*again, expert_delta))
    states = [replay(0, again), replay(1, again), expert_state, vector_state]
    attn_delta = low_delta(1, states[1])
    (embed_sum, attn_sum), vector_sum = sum_over_groups(
        (low_delta(0, states[0]), attn_delta.reshape(-1, D)), vectors - vector_state[0]
    )
    sums = (embed_sum, attn_sum.reshape(attn_delta.shape), expert_sum, vector_sum)
    results = [jnp.concatenate(loss_list, axis=1), jnp.concatenate(norm_list, axis=1)]
    for k in range(4):
        delta_mean = sums[k].astype(jnp.float32) * (1.0 / lax.axis_size("grp"))
        if k < 3:
            delta_mean = delta_mean + (1.0 - left(k, len(factor_list))) * masters[k]
        outer_new = OUTER_MOMENTUM * outers[k] + delta_mean
        master_new = masters[k] - OUTER_RATE * (delta_mean + OUTER_MOMENTUM * outer_new)
        if k == 3:
            results.append(vector_gradient[None])
        results += [states[k][1][None], states[k][2][None], master_new, outer_new]
        if k < 3:
            results.append(master_new.astype(jnp.bfloat16))
    return tuple(results)


def padded(embed_low):
    extra = -embed_low.shape[0] % 16
    return jnp.pad(embed_low, ((0, extra), (0, 0))) if extra else embed_low


def shards(
    tokens,
    routes,
    segments,
    loss_pos,
    embedding,
    embedding_first,
    embedding_second,
    embedding_outer,
    attention,
    attention_first,
    attention_second,
    attention_outer,
    experts,
    experts_first,
    experts_second,
    experts_outer,
    vectors,
    vectors_first,
    vectors_second,
    vectors_outer,
):
    inner_count = tokens.shape[0]
    vocab_shard = embedding.shape[0]
    n = lax.axis_size("fsdp")
    row_total = n * loss_pos.shape[2]
    slots = 48
    steps, fits = prepare(
        n, slots, vocab_shard, tokens[:, 0], routes[:, 0, :, 0], segments[:, 0], loss_pos[:, 0]
    )
    lows = (
        padded(embedding.astype(jnp.bfloat16)),
        lax.all_gather(attention.astype(jnp.bfloat16), "fsdp", axis=1, tiled=True),
        experts.astype(jnp.bfloat16),
    )
    sizes = (tokens.shape[2], loss_pos.shape[2])
    x_start = fetch(n, slots, sizes, steps[0], lows[0])
    state = (
        embedding,
        embedding_first,
        embedding_second,
        embedding_outer,
        attention,
        attention_first,
        attention_second,
        attention_outer,
        experts,
        experts_first,
        experts_second,
        experts_outer,
        vectors,
        vectors_first,
        vectors_second,
        vectors_outer,
    )

    def quick(*state):
        masters, firsts, seconds, outers = (
            [state[4 * k + part] for k in range(4)] for part in range(4)
        )
        firsts, seconds = [value[0] for value in firsts], [value[0] for value in seconds]
        return quick_window(
            n, slots, sizes, steps, x_start, lows, masters, firsts, seconds, outers
        )

    def general(*state):
        all_ids = lax.all_gather(tokens[:, 0, :], "fsdp", axis=1, tiled=True)
        step = functools.partial(general_step, tokens, routes, segments, loss_pos, all_ids)
        return window(step, *state, inner_count, row_total)

    return lax.cond(fits, quick, general, *state)


def solution(mesh):
    return jax.shard_map(
        shards,
        mesh=mesh,
        in_specs=(
            P(None, "grp", "fsdp"),
            P(None, "grp", "fsdp", None),
            P(None, "grp", "fsdp"),
            P(None, "grp", "fsdp"),
            P("fsdp", None),
            P("grp", "fsdp", None),
            P("grp", "fsdp", None),
            P("fsdp", None),
            P(None, "fsdp", None),
            P("grp", None, "fsdp", None),
            P("grp", None, "fsdp", None),
            P(None, "fsdp", None),
            P(None, None, None, "fsdp"),
            P("grp", None, None, None, "fsdp"),
            P("grp", None, None, None, "fsdp"),
            P(None, None, None, "fsdp"),
            P(),
            P("grp", None, None),
            P("grp", None, None),
            P(),
        ),
        out_specs=(
            P("grp", None),
            P("grp", None),
            P("grp", "fsdp", None),
            P("grp", "fsdp", None),
            P("fsdp", None),
            P("fsdp", None),
            P("fsdp", None),
            P("grp", None, "fsdp", None),
            P("grp", None, "fsdp", None),
            P(None, "fsdp", None),
            P(None, "fsdp", None),
            P(None, "fsdp", None),
            P("grp", None, None, None, "fsdp"),
            P("grp", None, None, None, "fsdp"),
            P(None, None, None, "fsdp"),
            P(None, None, None, "fsdp"),
            P(None, None, None, "fsdp"),
            P("grp", None, None),
            P("grp", None, None),
            P("grp", None, None),
            P(),
            P(),
        ),
        check_vma=False,
    )
```
